256 devices in a mesh: dp: 8 (over z_hi, core), seq: 32 (over y, z_lo, x).
Axes of the slice: x: 4, y: 4, z: 8 (z_hi: 4, z_lo: 2; z = z_hi * 2 + z_lo), core: 2. Of those that a mesh axis runs over, the one named last changes fastest.
Arguments:
- frames: bfloat16 [8, 4096, 1536], P('dp', 'seq'), may hold values from -6 to 6
- w_qkv: bfloat16 [1536, 2304], P('seq'), may hold values from -0.26791294 to 0.26791294
- w_out: bfloat16 [768, 1536], P('seq'), may hold values from -0.21875 to 0.21875
- norm_gains: float32 [2, 1536], replicated, may hold values from 0.1 to 1.9
- conv_kernel: float32 [31, 1536], replicated, may hold values from -1 to 1
- conv_bias: float32 [1536], replicated, may hold values from -3 to 3
- out_grad: bfloat16 [8, 4096, 1536], P('dp', 'seq'), may hold values from -6 to 6
Outputs:
- block_out: bfloat16 [8, 4096, 1536], P('dp', 'seq')
- grad_input: bfloat16 [8, 4096, 1536], P('dp', 'seq')
- grad_qkv: bfloat16 [1536, 2304], P('seq')
- grad_out: bfloat16 [768, 1536], P('seq')
- grad_norms: float32 [2, 1536], replicated
- grad_kernel: float32 [31, 1536], replicated
- grad_bias: float32 [1536], replicated
The draws below stay inside these ranges and needn't reach their ends.
All inputs are finite; a program needn't handle non-finite values.
Results may differ from the reference program's by a relative error of at most 0.035.
Values may be sent and summed in bfloat16 or wider, within the bound.
A program may use at most 64 MiB of HBM per device.

```python
import math
import jax
import jax.numpy as jnp
from jax import lax

D = 1536
H = 12
HD = 64
K = 31
FR_DEV = 128
STREAMS = 8
FRAMES = 4096
N_SEQ = 32


def draw_w_qkv(key, part):
    key = jax.random.fold_in(key, 11)
    width = H * HD
    whole = jax.random.truncated_normal(key, -4.0, 4.0, (D, 3 * width), jnp.float32) * D ** (-0.5)
    return whole.astype(jnp.bfloat16)


def level_of(rng, dims, split, low, largest):
    level = 1.0
    for position, blocks in split:
        heights = jax.random.uniform(jax.random.fold_in(jax.random.fold_in(rng, 6), position), (blocks,), jnp.float32, low / len(split), largest / len(split))
        level = level * jnp.repeat(jnp.exp(heights), dims[position] // blocks).reshape((-1,) + (1,) * (len(dims) - 1 - position))
    return level


def centred(own_key, extent, deviation, reach, cuts=(), held_as=jnp.bfloat16):
    values = deviation * jax.random.normal(own_key, extent, jnp.float32)
    if cuts:
        values = values * level_of(own_key, extent, cuts, -0.22, 0.18)
    return jnp.clip(values, -reach, reach).astype(held_as)


def setup_inputs(seed: int = 0) -> dict:
    splits = jax.random.split(jax.random.key(seed), 8)
    frames = centred(splits[0], (STREAMS, FRAMES, D), 1.0, 6.0, ((0, 8), (1, 32)))
    w_qkv = draw_w_qkv(jax.random.fold_in(splits[7], 71), 0)
    w_out = centred(splits[2], (H * HD, D), (H * HD) ** -0.5, 0.21875, ((0, 32),))
    norm_gains = jnp.clip(1.0 + 0.18 * jax.random.normal(splits[3], (2, D), jnp.float32), 0.1, 1.9)
    conv_kernel = centred(splits[4], (K, D), K ** -0.5, 1.0, (), jnp.float32)
    conv_bias = centred(splits[5], (D,), 0.5, 3.0, (), jnp.float32)
    out_grad = centred(splits[6], (STREAMS, FRAMES, D), 1.0, 6.0, ((0, 8), (1, 32)))
    return dict(frames=frames, w_qkv=w_qkv, w_out=w_out, norm_gains=norm_gains, conv_kernel=conv_kernel, conv_bias=conv_bias, out_grad=out_grad)


EPS = 1e-05

def layer_norm(values, gain):
    center = values - lax.optimization_barrier(jnp.mean(values, axis=-1, keepdims=True))
    spread = lax.optimization_barrier(jnp.mean(center * center, axis=-1, keepdims=True))
    inverse = lax.rsqrt(spread + EPS)
    normed = center * inverse
    return (normed * gain, normed, inverse)

def norm_back(grad, normed, inverse, gain):
    scaled = grad * gain
    inner = scaled - lax.optimization_barrier(jnp.mean(scaled, axis=-1, keepdims=True)) - normed * lax.optimization_barrier(jnp.mean(scaled * normed, axis=-1, keepdims=True))
    return (inverse * inner, lax.optimization_barrier(jnp.sum(grad * normed, axis=0)))

def head_forward(query, keys, values):
    factor = query.shape[-1] ** (-0.5)
    scores = lax.dot_general(query, keys, (((1,), (1,)), ((), ())), preferred_element_type=jnp.float32) * factor
    top = lax.optimization_barrier(jnp.max(scores, axis=-1, keepdims=True))
    expo = jnp.exp(scores - top)
    total = lax.optimization_barrier(jnp.sum(expo, axis=-1, keepdims=True))
    probs = (expo / total).astype(jnp.bfloat16)
    attended = jnp.dot(probs, values, preferred_element_type=jnp.float32).astype(jnp.bfloat16)
    return (attended, top[:, 0] + jnp.log(total[:, 0]))

def class_sums(left, right):
    classes = N_SEQ // math.gcd(H, N_SEQ)
    share = left.shape[0] // (N_SEQ * classes)
    left_parts = left.astype(jnp.float32).reshape(N_SEQ, classes, share, left.shape[1]).transpose(1, 0, 2, 3).reshape(classes, N_SEQ * share, left.shape[1])
    right_parts = right.astype(jnp.float32).reshape(N_SEQ, classes, share, right.shape[1]).transpose(1, 0, 2, 3).reshape(classes, N_SEQ * share, right.shape[1])
    parts = jnp.einsum('qta,qtb->qab', left_parts, right_parts)
    rounded = lax.optimization_barrier(parts.astype(jnp.bfloat16))
    return lax.optimization_barrier(jnp.sum(rounded.astype(jnp.float32), axis=0))

def head_backward(query, keys, values, attended, log_total, grad_attended):
    factor = query.shape[-1] ** (-0.5)
    scores = lax.dot_general(query, keys, (((1,), (1,)), ((), ())), preferred_element_type=jnp.float32) * factor
    probs = jnp.exp(scores - log_total[:, None])
    value_grads = class_sums(probs.astype(jnp.bfloat16), grad_attended)
    prob_grads = lax.dot_general(grad_attended, values, (((1,), (1,)), ((), ())), preferred_element_type=jnp.float32)
    delta = lax.optimization_barrier(jnp.sum(grad_attended.astype(jnp.float32) * attended.astype(jnp.float32), axis=-1, keepdims=True))
    score_grads = (probs * (prob_grads - delta) * factor).astype(jnp.bfloat16)
    query_grads = jnp.dot(score_grads, keys, preferred_element_type=jnp.float32)
    key_grads = class_sums(score_grads, query)
    return (query_grads, key_grads, value_grads)

def depthwise(wide, kernel, length):
    total = jnp.zeros((length, wide.shape[1]), jnp.float32)
    for tap in range(kernel.shape[0]):
        total = total + wide[tap:tap + length] * kernel[tap]
    return total

def split_heads(block):
    return block.reshape(block.shape[0], H, -1).transpose(1, 0, 2)

def join_heads(block):
    return block.transpose(1, 0, 2).reshape(block.shape[1], -1)

def block_sum(left, right):
    left_blocks = left.reshape(N_SEQ, FR_DEV, left.shape[1])
    right_blocks = right.reshape(N_SEQ, FR_DEV, right.shape[1])

    def advance(total, pair):
        term = lax.dot_general(pair[0], pair[1], (((0,), (0,)), ((), ())), preferred_element_type=jnp.float32)
        rounded = lax.optimization_barrier(term.astype(jnp.bfloat16))
        return (total + rounded.astype(jnp.float32), None)
    begin = jnp.zeros((left.shape[1], right.shape[1]), jnp.float32)
    total, _ = lax.scan(advance, begin, (left_blocks, right_blocks))
    return total

def reference(frames, w_qkv, w_out, norm_gains, conv_kernel, conv_bias, out_grad):
    width_all = w_out.shape[0]
    taps = conv_kernel.shape[0]
    half = (taps - 1) // 2

    def one_stream(carry, pair):
        stream, upstream_raw = pair
        length = stream.shape[0]
        inputs = stream.astype(jnp.float32)
        shifted, normed1, inverse1 = layer_norm(inputs, norm_gains[0])
        hidden = shifted.astype(jnp.bfloat16)
        projected = jnp.dot(hidden, w_qkv, preferred_element_type=jnp.float32).astype(jnp.bfloat16)
        query_heads = split_heads(projected[:, :width_all])
        key_heads = split_heads(projected[:, width_all:2 * width_all])
        value_heads = split_heads(projected[:, 2 * width_all:])
        attended_heads, log_total = lax.map(lambda item: head_forward(item[0], item[1], item[2]), (query_heads, key_heads, value_heads))
        attended = join_heads(attended_heads)
        mixed = (inputs + jnp.dot(attended, w_out, preferred_element_type=jnp.float32)).astype(jnp.bfloat16)
        mixed32 = mixed.astype(jnp.float32)
        shifted2, normed2, inverse2 = layer_norm(mixed32, norm_gains[1])
        conv_in = shifted2.astype(jnp.bfloat16)
        conv_wide = jnp.pad(conv_in.astype(jnp.float32), ((half, half), (0, 0)))
        preact = depthwise(conv_wide, conv_kernel, length) + conv_bias
        sigma = jax.nn.sigmoid(preact)
        output = (mixed32 + preact * sigma).astype(jnp.bfloat16)
        upstream = upstream_raw.astype(jnp.float32)
        grad_pre = (upstream * sigma * (1.0 + preact * (1.0 - sigma))).astype(jnp.bfloat16)
        grad_pre_float = grad_pre.astype(jnp.float32)
        grad_pre_wide = jnp.pad(grad_pre_float, ((half, half), (0, 0)))
        grad_conv = depthwise(grad_pre_wide, conv_kernel[::-1], length)
        kernel_grad = jnp.stack([lax.optimization_barrier(jnp.sum(grad_pre_float * conv_wide[tap:tap + length], axis=0)) for tap in range(taps)])
        bias_grad = lax.optimization_barrier(jnp.sum(grad_pre_float, axis=0))
        mixed_norm_grad, gain2_grad = norm_back(grad_conv, normed2, inverse2, norm_gains[1])
        grad_mixed = (upstream + mixed_norm_grad).astype(jnp.bfloat16)
        grad_attended = lax.dot_general(grad_mixed, w_out, (((1,), (1,)), ((), ())), preferred_element_type=jnp.float32).astype(jnp.bfloat16)
        grad_heads = split_heads(grad_attended)
        query_grads, key_grads, value_grads = lax.map(lambda item: head_backward(item[0], item[1], item[2], item[3], item[4], item[5]), (query_heads, key_heads, value_heads, attended_heads, log_total, grad_heads))
        grad_proj = jnp.concatenate([join_heads(query_grads), join_heads(key_grads), join_heads(value_grads)], axis=1).astype(jnp.bfloat16)
        grad_hidden = lax.dot_general(grad_proj, w_qkv, (((1,), (1,)), ((), ())), preferred_element_type=jnp.float32)
        input_norm_grad, gain1_grad = norm_back(grad_hidden, normed1, inverse1, norm_gains[0])
        grad_input = (grad_mixed.astype(jnp.float32) + input_norm_grad).astype(jnp.bfloat16)
        proj_total, out_total, norms_total, kernel_total, bias_total = carry
        proj_total = proj_total + block_sum(hidden, grad_proj)
        out_total = out_total + block_sum(attended, grad_mixed)
        norms_total = norms_total + jnp.stack([gain1_grad, gain2_grad])
        kernel_total = kernel_total + kernel_grad
        bias_total = bias_total + bias_grad
        return ((proj_total, out_total, norms_total, kernel_total, bias_total), (output, grad_input))
    begin = (jnp.zeros(w_qkv.shape, jnp.float32), jnp.zeros(w_out.shape, jnp.float32), jnp.zeros(norm_gains.shape, jnp.float32), jnp.zeros(conv_kernel.shape, jnp.float32), jnp.zeros(conv_bias.shape, jnp.float32))
    totals, outputs = lax.scan(one_stream, begin, (frames, out_grad))
    proj_total, out_total, norms_total, kernel_total, bias_total = totals
    return (outputs[0], outputs[1], proj_total.astype(jnp.bfloat16), out_total.astype(jnp.bfloat16), norms_total, kernel_total, bias_total)
```

```python
import functools

import jax
import jax.numpy as jnp
from jax import lax
from jax.experimental import pallas as pl
from jax.experimental.pallas import tpu as pltpu
from jax.sharding import PartitionSpec as P

EPS = 1e-05
GROUPS = 4
PLANE = 8
HEADS = 3
HD = 64
F32 = jnp.float32
BF16 = jnp.bfloat16


def group_of(kind):
    seq, dp = lax.axis_index("seq"), lax.axis_index("dp")
    if kind == "y":
        return 4, seq // 8, lambda i: {"seq": i * 8 + seq % 8}
    if kind == "plane":
        return 8, seq % 8, lambda i: {"seq": (seq // 8) * 8 + i}
    if kind == "seq":
        return 32, seq, lambda i: {"seq": i}
    return 8, dp, lambda i: {"dp": i}


SIZES = {"y": 4, "plane": 8, "seq": 32, "dp": 8}


def greet(kinds):
    if "seq" in kinds:
        kinds = [k for k in kinds if k not in ("y", "plane")]
    barrier = pltpu.get_barrier_semaphore()
    total = 0
    for kind in kinds:
        count, me, where = group_of(kind)
        for k in range(1, count):
            pl.semaphore_signal(barrier, inc=1, device_id=where((me + k) % count))
        total += count - 1
    pl.semaphore_wait(barrier, total)


def exchange_kernel(jobs, *refs):
    n = len(jobs)
    ins, outs, sems = refs[:n], refs[n : 2 * n], refs[2 * n :]
    greet(sorted({kind for kind, _ in jobs}))
    copies = []
    for j, (kind, mode) in enumerate(jobs):
        count, me, where = group_of(kind)
        send, recv, own = sems[3 * j : 3 * j + 3]
        for k in range(1, count):
            peer = (me + k) % count
            src = ins[j] if mode == "gather" else ins[j].at[peer]
            copy = pltpu.make_async_remote_copy(
                src_ref=src,
                dst_ref=outs[j].at[me],
                send_sem=send.at[k - 1],
                recv_sem=recv.at[k - 1],
                device_id=where(peer),
            )
            copy.start()
            copies.append(copy)
        src = ins[j] if mode == "gather" else ins[j].at[me]
        mine = pltpu.make_async_copy(src, outs[j].at[me], own.at[0])
        mine.start()
        copies.append(mine)
    for copy in copies:
        copy.wait()


def exchange(cid, *jobs):
    arrays = [job[0] for job in jobs]
    kinds = [(job[1], job[2]) for job in jobs]
    shapes, scratch = [], []
    for array, kind, mode in jobs:
        count = SIZES[kind]
        shape = (count, *array.shape) if mode == "gather" else array.shape
        shapes.append(jax.ShapeDtypeStruct(shape, array.dtype))
        scratch += [
            pltpu.SemaphoreType.DMA((count - 1,)),
            pltpu.SemaphoreType.DMA((count - 1,)),
            pltpu.SemaphoreType.DMA((1,)),
        ]
    return pl.pallas_call(
        functools.partial(exchange_kernel, kinds),
        out_shape=shapes,
        in_specs=[pl.BlockSpec(memory_space=pl.ANY)] * len(jobs),
        out_specs=[pl.BlockSpec(memory_space=pl.ANY)] * len(jobs),
        scratch_shapes=scratch,
        compiler_params=pltpu.CompilerParams(collective_id=cid, has_side_effects=True),
        name=f"exchange{cid}",
    )(*arrays)


def halo(array, width):
    devices, length = lax.axis_size("seq"), array.shape[0]
    up = [(i, i + 1) for i in range(devices - 1)]
    down = [(j, i) for i, j in up]
    before = lax.ppermute(array[length - width :], "seq", up)
    after = lax.ppermute(array[:width], "seq", down)
    return jnp.concatenate([before, array, after], axis=0)


def layer_norm(values, gain):
    center = values - jnp.mean(values, axis=-1, keepdims=True)
    spread = jnp.mean(center * center, axis=-1, keepdims=True)
    inverse = lax.rsqrt(spread + EPS)
    normed = center * inverse
    return (normed * gain, normed, inverse)


def norm_back(grad, normed, inverse, gain):
    scaled = grad * gain
    inner = (
        scaled
        - jnp.mean(scaled, axis=-1, keepdims=True)
        - normed * jnp.mean(scaled * normed, axis=-1, keepdims=True)
    )
    return (inverse * inner, jnp.sum(grad * normed, axis=0))


def head_forward(query, keys, values):
    factor = query.shape[-1] ** (-0.5)
    scores = (
        lax.dot_general(query, keys, (((1,), (1,)), ((), ())), preferred_element_type=F32) * factor
    )
    top = jnp.max(scores, axis=-1, keepdims=True)
    expo = jnp.exp(scores - top)
    total = jnp.sum(expo, axis=-1, keepdims=True)
    probs = (expo / total).astype(BF16)
    attended = jnp.dot(probs, values, preferred_element_type=F32).astype(BF16)
    return (attended, top[:, 0] + jnp.log(total[:, 0]))


def head_backward(query, keys, values, attended, log_total, grad_attended):
    factor = query.shape[-1] ** (-0.5)
    scores = (
        lax.dot_general(query, keys, (((1,), (1,)), ((), ())), preferred_element_type=F32) * factor
    )
    probs = jnp.exp(scores - log_total[:, None])
    value_grads = lax.dot_general(
        probs.astype(BF16), grad_attended, (((0,), (0,)), ((), ())), preferred_element_type=F32
    )
    prob_grads = lax.dot_general(
        grad_attended, values, (((1,), (1,)), ((), ())), preferred_element_type=F32
    )
    delta = jnp.sum(
        grad_attended.astype(F32) * attended.astype(F32), axis=-1, keepdims=True
    )
    score_grads = (probs * (prob_grads - delta) * factor).astype(BF16)
    query_grads = jnp.dot(score_grads, keys, preferred_element_type=F32)
    key_grads = lax.dot_general(
        score_grads, query, (((0,), (0,)), ((), ())), preferred_element_type=F32
    )
    return (query_grads, key_grads, value_grads)


def depthwise(wide, kernel, length):
    total = jnp.zeros((length, wide.shape[1]), F32)
    for tap in range(kernel.shape[0]):
        total = total + wide[tap : tap + length] * kernel[tap]
    return total


def split_heads(block):
    return block.reshape(block.shape[0], HEADS, -1).transpose(1, 0, 2)


def join_heads(block):
    return block.transpose(1, 0, 2).reshape(block.shape[1], -1)


def matmul(a, b, dims=((1,), (0,))):
    return lax.dot_general(a, b, (dims, ((), ())), preferred_element_type=F32)


def local(frames, w_qkv, w_out, norm_gains, conv_kernel, conv_bias, out_grad):
    inputs = frames[0].astype(F32)
    rows, model = inputs.shape
    shard, three = w_qkv.shape
    width = three // (3 * GROUPS)
    trio = 3 * width
    share_out = w_out.shape[0]
    many = GROUPS * rows

    shifted, normed1, inverse1 = layer_norm(inputs, norm_gains[0])
    hidden = shifted.astype(BF16)
    w_parts = (
        w_qkv.reshape(shard, 3, GROUPS, width).transpose(2, 0, 1, 3).reshape(GROUPS, shard, trio)
    )
    hidden_all, w_mine = exchange(0, (hidden, "y", "gather"), (w_parts, "y", "a2a"))
    w_all, out_all = exchange(1, (w_mine, "plane", "gather"), (w_out, "plane", "gather"))
    hidden_all = hidden_all.reshape(many, model)
    w_group = w_all.transpose(1, 0, 2, 3).reshape(model, trio)
    out_group = out_all.reshape(width, model)

    projected = matmul(hidden_all, w_group).astype(BF16)
    (pairs,) = exchange(2, (projected[:, width:], "plane", "gather"))
    pairs = pairs.reshape(PLANE * many, 2 * width)
    query_heads = split_heads(projected[:, :width])
    key_heads = split_heads(pairs[:, :width])
    value_heads = split_heads(pairs[:, width:])
    attended_heads, log_total = lax.map(
        lambda item: head_forward(*item), (query_heads, key_heads, value_heads)
    )
    attended = join_heads(attended_heads)
    out_parts = matmul(attended, out_group).astype(BF16).reshape(GROUPS, rows, model)
    (out_terms,) = exchange(3, (out_parts, "y", "a2a"))
    mixed = (inputs + jnp.sum(out_terms.astype(F32), axis=0)).astype(BF16)

    mixed32 = mixed.astype(F32)
    shifted2, normed2, inverse2 = layer_norm(mixed32, norm_gains[1])
    conv_in = shifted2.astype(BF16)
    taps = conv_kernel.shape[0]
    half = (taps - 1) // 2
    conv_wide = halo(conv_in, half).astype(F32)
    preact = depthwise(conv_wide, conv_kernel, rows) + conv_bias
    sigma = jax.nn.sigmoid(preact)
    output = (mixed32 + preact * sigma).astype(BF16)
    upstream = out_grad[0].astype(F32)
    grad_pre = (upstream * sigma * (1.0 + preact * (1.0 - sigma))).astype(BF16)
    grad_pre_wide = halo(grad_pre, half).astype(F32)
    grad_conv = depthwise(grad_pre_wide, conv_kernel[::-1], rows)
    grad_pre_float = grad_pre.astype(F32)
    kernel_grad = jnp.stack(
        [jnp.sum(grad_pre_float * conv_wide[tap : tap + rows], axis=0) for tap in range(taps)]
    )
    bias_grad = jnp.sum(grad_pre_float, axis=0)
    mixed_norm_grad, gain2_grad = norm_back(grad_conv, normed2, inverse2, norm_gains[1])
    grad_mixed = (upstream + mixed_norm_grad).astype(BF16)

    (mixed_all,) = exchange(4, (grad_mixed, "y", "gather"))
    mixed_all = mixed_all.reshape(many, model)
    grad_attended = matmul(mixed_all, out_group, ((1,), (1,))).astype(BF16)
    query_grads, key_grads, value_grads = lax.map(
        lambda item: head_backward(*item),
        (
            query_heads,
            key_heads,
            value_heads,
            attended_heads,
            log_total,
            split_heads(grad_attended),
        ),
    )
    pair_parts = (
        jnp.concatenate([join_heads(key_grads), join_heads(value_grads)], axis=1)
        .reshape(PLANE, many, 2 * width)
        .astype(BF16)
    )
    (pair_terms,) = exchange(5, (pair_parts, "plane", "a2a"))
    pair_grads = jnp.sum(pair_terms.astype(F32), axis=0).astype(BF16)
    grad_proj = jnp.concatenate([join_heads(query_grads).astype(BF16), pair_grads], axis=1)

    hid_parts = matmul(grad_proj, w_group, ((1,), (1,))).astype(BF16).reshape(GROUPS, rows, model)
    w_grad = (
        matmul(hidden_all, grad_proj, ((0,), (0,)))
        .astype(BF16)
        .reshape(GROUPS, PLANE, shard, trio)
        .transpose(1, 0, 2, 3)
    )
    out_grad_parts = (
        matmul(attended, mixed_all, ((0,), (0,))).astype(BF16).reshape(PLANE, share_out, model)
    )
    hid_terms, w_terms, out_grad_terms = exchange(
        6, (hid_parts, "y", "a2a"), (w_grad, "plane", "a2a"), (out_grad_parts, "plane", "a2a")
    )
    grad_hidden = jnp.sum(hid_terms.astype(F32), axis=0)
    input_norm_grad, gain1_grad = norm_back(grad_hidden, normed1, inverse1, norm_gains[0])
    grad_input = (grad_mixed.astype(F32) + input_norm_grad).astype(BF16)

    dp = lax.axis_size("dp")
    w_sum = jnp.sum(w_terms.astype(F32), axis=0).astype(BF16)
    out_sum = jnp.sum(out_grad_terms.astype(F32), axis=0).astype(BF16)
    lanes = 128
    w_split = w_sum.reshape(GROUPS, dp, -1, lanes).transpose(1, 0, 2, 3)
    out_split = out_sum.reshape(dp, -1, lanes)
    small = jnp.concatenate([gain1_grad[None], gain2_grad[None], kernel_grad, bias_grad[None]])
    count = small.shape[0]
    small_split = small.reshape(count, dp, -1).transpose(1, 0, 2)
    w_dp, out_dp, small_dp = exchange(
        7, (w_split, "dp", "a2a"), (out_split, "dp", "a2a"), (small_split, "dp", "a2a")
    )
    w_share = jnp.sum(w_dp.astype(F32), axis=0).astype(BF16)
    out_share = jnp.sum(out_dp.astype(F32), axis=0).astype(BF16)
    small_share = jnp.sum(small_dp, axis=0)
    w_home, small_seq = exchange(8, (w_share, "y", "a2a"), (small_share, "seq", "gather"))
    small_sum = jnp.sum(small_seq, axis=0)
    w_fin, out_fin, small_fin = exchange(
        9, (w_home, "dp", "gather"), (out_share, "dp", "gather"), (small_sum, "dp", "gather")
    )
    grad_qkv = (
        w_fin.transpose(1, 0, 2, 3)
        .reshape(GROUPS, shard, 3, width)
        .transpose(1, 2, 0, 3)
        .reshape(shard, three)
    )
    grad_out = out_fin.reshape(share_out, model)
    small_all = small_fin.transpose(1, 0, 2).reshape(count, model)
    return (
        output[None],
        grad_input[None],
        grad_qkv,
        grad_out,
        small_all[:2],
        small_all[2 : count - 1],
        small_all[count - 1],
    )


def solution(mesh):
    in_specs = (
        P("dp", "seq", None),
        P("seq", None),
        P("seq", None),
        P(),
        P(),
        P(),
        P("dp", "seq", None),
    )
    out_specs = (
        P("dp", "seq", None),
        P("dp", "seq", None),
        P("seq", None),
        P("seq", None),
        P(),
        P(),
        P(),
    )
    return jax.shard_map(local, mesh=mesh, in_specs=in_specs, out_specs=out_specs, check_vma=False)
```

```python
import functools

import jax
import jax.numpy as jnp
from jax import lax
from jax.experimental import pallas as pl
from jax.experimental.pallas import tpu as pltpu
from jax.sharding import PartitionSpec as P

EPS = 1e-05
GROUPS = 4
PLANE = 8
HEADS = 3
HD = 64
F32 = jnp.float32
BF16 = jnp.bfloat16


def group_of(kind):
    seq, dp = lax.axis_index("seq"), lax.axis_index("dp")
    if kind == "y":
        return 4, seq // 8, lambda i: {"seq": i * 8 + seq % 8}
    if kind == "plane":
        return 8, seq % 8, lambda i: {"seq": (seq // 8) * 8 + i}
    if kind == "seq":
        return 32, seq, lambda i: {"seq": i}
    return 8, dp, lambda i: {"dp": i}


SIZES = {"y": 4, "plane": 8, "seq": 32, "dp": 8}


def greet(kinds):
    if "seq" in kinds:
        kinds = [k for k in kinds if k not in ("y", "plane")]
    barrier = pltpu.get_barrier_semaphore()
    total = 0
    for kind in kinds:
        count, me, where = group_of(kind)
        for k in range(1, count):
            pl.semaphore_signal(barrier, inc=1, device_id=where((me + k) % count))
        total += count - 1
    pl.semaphore_wait(barrier, total)


def exchange_kernel(jobs, *refs):
    n = len(jobs)
    ins, outs, sems = refs[:n], refs[n : 2 * n], refs[2 * n :]
    greet(sorted({kind for kind, _ in jobs}))
    copies = []
    for j, (kind, mode) in enumerate(jobs):
        count, me, where = group_of(kind)
        send, recv, own = sems[3 * j : 3 * j + 3]
        for k in range(1, count):
            peer = (me + k) % count
            src = ins[j] if mode == "gather" else ins[j].at[peer]
            copy = pltpu.make_async_remote_copy(
                src_ref=src,
                dst_ref=outs[j].at[me],
                send_sem=send.at[k - 1],
                recv_sem=recv.at[k - 1],
                device_id=where(peer),
            )
            copy.start()
            copies.append(copy)
        src = ins[j] if mode == "gather" else ins[j].at[me]
        mine = pltpu.make_async_copy(src, outs[j].at[me], own.at[0])
        mine.start()
        copies.append(mine)
    for copy in copies:
        copy.wait()


def exchange(cid, *jobs):
    arrays = [job[0] for job in jobs]
    kinds = [(job[1], job[2]) for job in jobs]
    shapes, scratch = [], []
    for array, kind, mode in jobs:
        count = SIZES[kind]
        shape = (count, *array.shape) if mode == "gather" else array.shape
        shapes.append(jax.ShapeDtypeStruct(shape, array.dtype))
        scratch += [
            pltpu.SemaphoreType.DMA((count - 1,)),
            pltpu.SemaphoreType.DMA((count - 1,)),
            pltpu.SemaphoreType.DMA((1,)),
        ]
    return pl.pallas_call(
        functools.partial(exchange_kernel, kinds),
        out_shape=shapes,
        in_specs=[pl.BlockSpec(memory_space=pl.ANY)] * len(jobs),
        out_specs=[pl.BlockSpec(memory_space=pl.ANY)] * len(jobs),
        scratch_shapes=scratch,
        compiler_params=pltpu.CompilerParams(collective_id=cid, has_side_effects=True),
        name=f"exchange{cid}",
    )(*arrays)


def dot(a, b, ca, cb):
    return lax.dot_general(a, b, (((ca,), (cb,)), ((), ())), preferred_element_type=F32)


class Place:
    def __init__(self):
        seq = lax.axis_index("seq")
        y, z, x = seq // 8, (seq // 4) % 2, seq % 4
        right, left, far, other = (x + 1) % 4, (x + 3) % 4, (x + 2) % 4, 1 - z
        self.y, self.yp, self.ym, self.yf = y, (y + 1) % 4, (y + 3) % 4, (y + 2) % 4
        self.me = z * 4 + x
        self.xp, self.xm, self.xf = z * 4 + right, z * 4 + left, z * 4 + far
        self.zo = other * 4 + x
        self.zxp, self.zxm, self.zxf = other * 4 + right, other * 4 + left, other * 4 + far

    def plane(self, p):
        return {"seq": self.y * 8 + p}

    def column(self, y):
        return {"seq": y * 8 + self.me}

    def greet(self):
        barrier = pltpu.get_barrier_semaphore()
        near = [self.column(y) for y in (self.yp, self.ym, self.yf)]
        near += [self.plane(p) for p in (self.xp, self.xm, self.zo)]
        for device in near:
            pl.semaphore_signal(barrier, inc=1, device_id=device)
        pl.semaphore_wait(barrier, len(near))


class Wire:
    def __init__(self, sems):
        self.sems, self.sent = sems, {}

    def go(self, k, src, dst, device):
        copy = pltpu.make_async_remote_copy(
            src_ref=src,
            dst_ref=dst,
            send_sem=self.sems.at[0, k],
            recv_sem=self.sems.at[1, k],
            device_id=device,
        )
        copy.start()
        self.sent[k] = copy

    def got(self, *ks):
        for k in ks:
            self.sent[k].wait_recv()

    def done(self):
        for copy in self.sent.values():
            copy.wait_send()


def wire_sems(count):
    return pltpu.SemaphoreType.DMA((2, count))


class ColumnGather(Wire):
    def __init__(self, sems, place, buf):
        super().__init__(sems)
        self.at, self.buf = place, buf
        self.half = buf.shape[1] // 2

    def begin(self):
        t, own = self.at, self.buf.at[self.at.y]
        self.go(0, own, own, t.column(t.yp))
        self.go(1, own, own, t.column(t.ym))

    def relay(self):
        t, h = self.at, self.half
        self.got(0)
        first = self.buf.at[t.ym, pl.ds(0, h)]
        self.go(2, first, first, t.column(t.yp))
        self.got(1)
        second = self.buf.at[t.yp, pl.ds(h, h)]
        self.go(3, second, second, t.column(t.ym))

    def finish(self):
        self.got(2, 3)


class ColumnReduce(Wire):
    def __init__(self, sems, place, part, relays, lands):
        super().__init__(sems)
        self.at, self.part, self.relays, self.lands = place, part, relays, lands
        self.half = part.shape[1] // 2

    def far(self):
        t, h = self.at, self.half
        self.go(0, self.part.at[t.yf, pl.ds(0, h)], self.relays.at[0], t.column(t.ym))
        self.go(1, self.part.at[t.yf, pl.ds(h, h)], self.relays.at[1], t.column(t.yp))

    def near(self):
        t, h = self.at, self.half
        low, high = pl.ds(0, h), pl.ds(h, h)
        self.go(2, self.part.at[t.ym, high], self.lands.at[0, high], t.column(t.ym))
        self.go(3, self.part.at[t.yp, low], self.lands.at[1, low], t.column(t.yp))
        self.got(0)
        self.part[t.ym, low] = (
            self.part[t.ym, low].astype(F32) + self.relays[0].astype(F32)
        ).astype(BF16)
        self.go(4, self.part.at[t.ym, low], self.lands.at[0, low], t.column(t.ym))
        self.got(1)
        self.part[t.yp, high] = (
            self.part[t.yp, high].astype(F32) + self.relays[1].astype(F32)
        ).astype(BF16)
        self.go(5, self.part.at[t.yp, high], self.lands.at[1, high], t.column(t.yp))

    def finish(self):
        self.got(2, 3, 4, 5)
        return (
            self.part[self.at.y].astype(F32)
            + self.lands[0].astype(F32)
            + self.lands[1].astype(F32)
        )


class PlaneGather(Wire):
    def __init__(self, sems, place, full, half):
        super().__init__(sems)
        self.at, self.full, self.half = place, full, half

    def begin(self):
        t, own = self.at, self.full(self.at.me)
        self.go(0, own, own, t.plane(t.xp))
        self.go(1, own, own, t.plane(t.xm))
        self.go(2, own, own, t.plane(t.zo))

    def relay(self):
        t = self.at
        self.got(0)
        first = self.half(t.xm, 0)
        self.go(3, first, first, t.plane(t.xp))
        self.got(1)
        second = self.half(t.xp, 1)
        self.go(4, second, second, t.plane(t.xm))
        self.got(2)
        other = self.full(t.zo)
        self.go(5, other, other, t.plane(t.xp))
        self.go(6, other, other, t.plane(t.xm))

    def cross(self):
        t = self.at
        for k in (0, 1):
            self.got(3 + k)
            part = self.half(t.xf, k)
            self.go(7 + k, part, part, t.plane(t.zo))

    def finish(self):
        self.got(5, 6, 7, 8)


class PlaneReduce(Wire):
    def __init__(self, sems, place, full, half, land, half_land):
        super().__init__(sems)
        self.at, self.full, self.half = place, full, half
        self.land, self.half_land = land, half_land

    def add(self, ref, *more):
        total = ref[...].astype(F32)
        for other in more:
            total = total + other[...].astype(F32)
        ref[...] = total.astype(BF16)

    def far(self):
        t = self.at
        self.go(0, self.full(t.zxf), self.land(0), t.plane(t.zo))

    def sides(self):
        t = self.at
        self.go(1, self.full(t.zxm), self.land(1), t.plane(t.xm))
        self.go(2, self.full(t.zxp), self.land(2), t.plane(t.xp))

    def opposite(self):
        t = self.at
        self.got(0)
        self.add(self.full(t.xf), self.land(0))
        self.go(3, self.half(t.xf, 0), self.half_land(0), t.plane(t.xm))
        self.go(4, self.half(t.xf, 1), self.half_land(1), t.plane(t.xp))

    def across(self):
        t = self.at
        self.got(1, 2)
        self.add(self.full(t.zo), self.land(1), self.land(2))
        self.go(5, self.full(t.zo), self.land(3), t.plane(t.zo))

    def near(self):
        t = self.at
        self.got(3)
        self.add(self.half(t.xm, 0), self.half_land(0))
        self.go(6, self.full(t.xm), self.land(4), t.plane(t.xm))
        self.got(4)
        self.add(self.half(t.xp, 1), self.half_land(1))
        self.go(7, self.full(t.xp), self.land(5), t.plane(t.xp))

    def finish(self):
        self.got(5, 6, 7)
        total = self.full(self.at.me)[...].astype(F32)
        for k in (3, 4, 5):
            total = total + self.land(k)[...].astype(F32)
        return total


def pick(i, *values):
    out = values[-1]
    for k in range(len(values) - 2, -1, -1):
        out = jnp.where(i == k, values[k], out)
    return out


def local_copies(pairs, sems):
    copies = [
        pltpu.make_async_copy(src, dst, sems.at[i]) for i, (src, dst) in enumerate(pairs)
    ]
    for copy in copies:
        copy.start()
    return copies


QB = 128


def forward_chunk(kv, c, qpad, top, total, acc):
    many = qpad.shape[1]
    for h in range(HEADS):
        both = kv[c, :, h * 128 : (h + 1) * 128]
        for b in range(many // QB):
            cols = slice(b * QB, (b + 1) * QB)
            scores = dot(both, qpad[h, cols, :], 1, 1)
            old = top[h, :, cols]
            new = jnp.maximum(old, jnp.max(scores, axis=0, keepdims=True))
            shrink = jnp.exp(old - new)
            expo = jnp.exp(scores - new)
            top[h, :, cols] = new
            total[h, :, cols] = total[h, :, cols] * shrink + jnp.sum(expo, axis=0, keepdims=True)
            acc[h, :, cols] = acc[h, :, cols] * shrink + dot(both, expo.astype(BF16), 0, 0)


def front_kernel(
    frames,
    gain,
    w_parts,
    w_out,
    mixed_out,
    hid_out,
    wq_out,
    wo_out,
    kv_out,
    qpad_out,
    att_out,
    lse_out,
    hid,
    wq,
    wo,
    wo32,
    wo16,
    kv,
    qpad,
    top,
    total,
    acc,
    att,
    part,
    relays,
    lands,
    w_sems,
    own_sem,
    hid_sems,
    wq_sems,
    wo_sems,
    kv_sems,
    red_sems,
    out_sems,
):
    t = Place()
    t.greet()
    rows = frames.shape[0]
    many = GROUPS * rows
    spread = Wire(w_sems)
    for k, y in enumerate((t.yp, t.ym, t.yf)):
        spread.go(k, w_parts.at[y], wq.at[t.y, t.me], t.column(y))
    own = pltpu.make_async_copy(w_parts.at[t.y], wq.at[t.y, t.me], own_sem.at[0])
    own.start()
    wo[t.me] = w_out[...]

    inputs = frames[...].astype(F32)
    shifted, _, _ = layer_norm(inputs, gain[...])
    hid[t.y] = shifted.astype(BF16)
    hid_net = ColumnGather(hid_sems, t, hid)
    hid_net.begin()
    own.wait()
    spread.got(0, 1, 2)
    wq_net = PlaneGather(
        wq_sems, t, lambda p: wq.at[:, p], lambda p, i: wq.at[pl.ds(2 * i, 2), p]
    )
    wo_net = PlaneGather(
        wo_sems, t, lambda p: wo.at[p], lambda p, i: wo.at[p, pl.ds(16 * i, 16)]
    )
    wq_net.begin()
    hid_net.relay()
    wq_net.relay()
    wq_net.cross()
    wo_net.begin()
    hid_net.finish()
    wq_net.finish()
    saves = local_copies([(hid, hid_out), (wq, wq_out)], out_sems.at[pl.ds(0, 2)])

    model = frames.shape[1]
    width = HEADS * HD
    hidden = hid[...].reshape(many, model)
    weights = wq[...].reshape(model, 3 * width)
    projected = dot(hidden, weights, 1, 0).astype(BF16)
    kv[t.me] = projected[:, width:]
    kv_net = PlaneGather(
        kv_sems,
        t,
        lambda p: kv.at[p],
        lambda p, i: kv.at[p, pl.ds(i * (many // 2), many // 2)],
    )
    kv_net.begin()
    zeros = jnp.zeros((many, HD), BF16)
    for h in range(HEADS):
        qpad[h] = jnp.concatenate(
            [projected[:, h * HD : (h + 1) * HD] * BF16(HD**-0.5), zeros], axis=1
        )
    top[...] = jnp.full_like(top, -jnp.inf)
    total[...] = jnp.zeros_like(total)
    acc[...] = jnp.zeros_like(acc)

    def attend(*chunks):
        if len(chunks) == 1:
            forward_chunk(kv, chunks[0], qpad, top, total, acc)
            return

        def step(i, carry):
            forward_chunk(kv, pick(i, *chunks), qpad, top, total, acc)
            return carry

        lax.fori_loop(0, len(chunks), step, 0)

    attend(t.me)
    kv_net.relay()
    wo_net.relay()
    attend(t.xm, t.xp, t.zo)
    kv_net.cross()
    wo_net.cross()
    attend(t.xf)
    kv_net.got(5, 6)
    attend(t.zxm, t.zxp)
    kv_net.got(7, 8)
    saves += local_copies([(kv, kv_out), (qpad, qpad_out)], out_sems.at[pl.ds(2, 2)])
    attend(t.zxf)
    wo_net.finish()
    share = width // PLANE
    for p in range(PLANE):
        wo32[p * share : (p + 1) * share, :] = wo[p, 0:share, :].astype(F32)
    wo16[...] = wo32[...].astype(BF16)
    blocks = []
    for h in range(HEADS):
        blocks.append((acc[h, HD : 2 * HD, :] / total[h]).T.astype(BF16))
        top[h] = top[h] + jnp.log(total[h])
    att[...] = jnp.concatenate(blocks, axis=1)
    saves += local_copies([(wo16, wo_out), (att, att_out), (top, lse_out)], out_sems.at[pl.ds(4, 3)])

    def product(y):
        here = att[pl.ds(pl.multiple_of(y * rows, rows), rows), :]
        part[y] = dot(here, wo16[...], 1, 0).astype(BF16)

    red = ColumnReduce(red_sems, t, part, relays, lands)
    product(t.yf)
    red.far()
    product(t.ym)
    product(t.yp)
    product(t.y)
    red.near()
    mixed_out[...] = (frames[...].astype(F32) + red.finish()).astype(BF16)
    for net in (spread, hid_net, wq_net, wo_net, kv_net, red):
        net.done()
    for copy in saves:
        copy.wait()


def front(frames, gain, w_parts, w_out):
    rows, model = frames.shape
    _, shard, trio = w_parts.shape
    width = trio // 3
    many = GROUPS * rows
    vmem, anywhere = pl.BlockSpec(memory_space=pltpu.VMEM), pl.BlockSpec(memory_space=pl.ANY)
    like = jax.ShapeDtypeStruct
    return pl.pallas_call(
        front_kernel,
        out_shape=[
            like((rows, model), BF16),
            like((GROUPS, rows, model), BF16),
            like((GROUPS, PLANE, shard, trio), BF16),
            like((width, model), BF16),
            like((PLANE, many, 2 * width), BF16),
            like((HEADS, many, 2 * HD), BF16),
            like((many, width), BF16),
            like((HEADS, 1, many), F32),
        ],
        in_specs=[vmem] * 4,
        out_specs=[vmem] + [anywhere] * 7,
        scratch_shapes=[
            pltpu.VMEM((GROUPS, rows, model), BF16),
            pltpu.VMEM((GROUPS, PLANE, shard, trio), BF16),
            pltpu.VMEM((PLANE, *w_out.shape), BF16),
            pltpu.VMEM((width, model), F32),
            pltpu.VMEM((width, model), BF16),
            pltpu.VMEM((PLANE, many, 2 * width), BF16),
            pltpu.VMEM((HEADS, many, 2 * HD), BF16),
            pltpu.VMEM((HEADS, 1, many), F32),
            pltpu.VMEM((HEADS, 1, many), F32),
            pltpu.VMEM((HEADS, 2 * HD, many), F32),
            pltpu.VMEM((many, width), BF16),
            pltpu.VMEM((GROUPS, rows, model), BF16),
            pltpu.VMEM((2, rows // 2, model), BF16),
            pltpu.VMEM((2, rows, model), BF16),
            wire_sems(3),
            pltpu.SemaphoreType.DMA((1,)),
            wire_sems(4),
            wire_sems(9),
            wire_sems(9),
            wire_sems(9),
            wire_sems(6),
            pltpu.SemaphoreType.DMA((7,)),
        ],
        compiler_params=pltpu.CompilerParams(
            collective_id=0, has_side_effects=True, vmem_limit_bytes=48 * 2**20
        ),
        name="front",
    )(frames, gain, w_parts, w_out)


def backward_chunk(kv, c, qpad, dopad, lse, delta, dqt, out):
    for h in range(HEADS):
        lanes = slice(h * 128, (h + 1) * 128)
        both, query, grad = kv[c, :, lanes], qpad[h], dopad[h]
        scores = dot(both, query, 1, 1)
        slopes = dot(both, grad, 1, 1)
        probs = jnp.exp(scores - lse[h])
        score_grads = (probs * (slopes - delta[h])).astype(BF16)
        out[c, :, lanes] = (
            dot(probs.astype(BF16), grad, 1, 0) + dot(score_grads, query, 1, 0)
        ).astype(BF16)
        dqt[h] += dot(both, score_grads, 0, 0)


def back_kernel(
    frames,
    gain,
    grad_mixed,
    hid_in,
    wq_in,
    wo_in,
    kv_in,
    qpad_in,
    att_in,
    lse_in,
    grad_input,
    gain_grad,
    w_sum,
    out_sum,
    mix,
    hid,
    wq,
    wo,
    kv,
    qpad,
    att,
    lse,
    dopad,
    delta,
    dqt,
    dkv,
    kv_land,
    kv_half,
    proj,
    part,
    relays,
    lands,
    w_part,
    w_land,
    w_half,
    o_part,
    o_land,
    o_half,
    in_sems,
    mix_sems,
    kv_sems,
    red_sems,
    w_sems,
    o_sems,
):
    t = Place()
    t.greet()
    rows, model = frames.shape
    many = GROUPS * rows
    width = HEADS * HD
    mix[t.y] = grad_mixed[...]
    mix_net = ColumnGather(mix_sems, t, mix)
    mix_net.begin()
    loads = local_copies(
        [
            (wo_in, wo),
            (att_in, att),
            (qpad_in, qpad),
            (lse_in, lse),
            (kv_in, kv),
            (hid_in, hid),
            (wq_in, wq),
        ],
        in_sems,
    )
    for copy in loads:
        copy.wait()
    mix_net.relay()
    mix_net.finish()

    mixed = mix[...].reshape(many, model)
    grads = dot(mixed, wo[...], 1, 1).astype(BF16)
    zeros = jnp.zeros((many, HD), BF16)
    for h in range(HEADS):
        lanes = slice(h * HD, (h + 1) * HD)
        mine = grads[:, lanes]
        dopad[h] = jnp.concatenate([zeros, mine], axis=1)
        delta[h] = jnp.sum(
            (att[:, lanes].astype(F32) * mine.astype(F32)).T, axis=0, keepdims=True
        )
    dqt[...] = jnp.zeros_like(dqt)

    def attend(*chunks):
        def step(i, carry):
            backward_chunk(kv, pick(i, *chunks), qpad, dopad, lse, delta, dqt, dkv)
            return carry

        if len(chunks) == 1:
            step(0, 0)
        else:
            lax.fori_loop(0, len(chunks), step, 0)

    half = many // 2
    net = PlaneReduce(
        kv_sems,
        t,
        lambda p: dkv.at[p],
        lambda p, i: dkv.at[p, pl.ds(i * half, half)],
        lambda k: kv_land.at[k],
        lambda k: kv_half.at[k],
    )
    attend(t.zxf)
    net.far()
    attend(t.zxm, t.zxp)
    net.sides()
    attend(t.xf)
    net.opposite()
    attend(t.zo)
    net.across()
    attend(t.xm, t.xp)
    net.near()
    attend(t.me)
    for h in range(HEADS):
        proj[:, h * HD : (h + 1) * HD] = (dqt[h, 0:HD, :] * HD**-0.5).T.astype(BF16)

    out_terms = dot(att[...], mixed, 0, 0).astype(BF16)
    share = width // PLANE
    for p in range(PLANE):
        o_part[p, 0:share, :] = out_terms[p * share : (p + 1) * share, :]
        o_part[p, share:, :] = jnp.zeros((o_part.shape[1] - share, model), BF16)
    o_net = PlaneReduce(
        o_sems,
        t,
        lambda p: o_part.at[p],
        lambda p, i: o_part.at[p, pl.ds(16 * i, 16)],
        lambda k: o_land.at[k],
        lambda k: o_half.at[k],
    )
    o_net.far()
    o_net.sides()
    proj[:, width:] = net.finish().astype(BF16)

    weights = wq[...].reshape(model, 3 * width)

    def product(y):
        here = proj[pl.ds(pl.multiple_of(y * rows, rows), rows), :]
        part[y] = dot(here, weights, 1, 1).astype(BF16)

    red = ColumnReduce(red_sems, t, part, relays, lands)
    product(t.yf)
    red.far()
    hidden = hid[...].reshape(many, model)
    w_terms = dot(hidden, proj[...], 0, 0).astype(BF16)
    w_part[...] = w_terms.reshape(w_part.shape)
    w_net = PlaneReduce(
        w_sems,
        t,
        lambda p: w_part.at[:, p],
        lambda p, i: w_part.at[pl.ds(2 * i, 2), p],
        lambda k: w_land.at[k],
        lambda k: w_half.at[k],
    )
    w_net.far()
    w_net.sides()
    product(t.ym)
    product(t.yp)
    product(t.y)
    o_net.opposite()
    o_net.across()
    red.near()
    w_net.opposite()
    w_net.across()
    o_net.near()
    w_net.near()
    grad_hidden = red.finish()
    _, normed, inverse = layer_norm(frames[...].astype(F32), gain[...])
    norm_grad, gain_sum = norm_back(grad_hidden, normed, inverse, gain[...])
    grad_input[...] = (grad_mixed[...].astype(F32) + norm_grad).astype(BF16)
    gain_grad[...] = gain_sum[None]
    out_sum[...] = o_net.finish().astype(BF16)
    w_sum[...] = w_net.finish().astype(BF16)
    for wire in (mix_net, net, o_net, red, w_net):
        wire.done()


def back(frames, gain, grad_mixed, hid, wq, wo, kv, qpad, att, lse):
    rows, model = frames.shape
    many = GROUPS * rows
    width = HEADS * HD
    shard = wq.shape[2]
    padded = 32
    vmem, anywhere = pl.BlockSpec(memory_space=pltpu.VMEM), pl.BlockSpec(memory_space=pl.ANY)
    like = jax.ShapeDtypeStruct

    def hold(array):
        return pltpu.VMEM(array.shape, array.dtype)

    return pl.pallas_call(
        back_kernel,
        out_shape=[
            like((rows, model), BF16),
            like((1, model), F32),
            like((GROUPS, shard, 3 * width), BF16),
            like((padded, model), BF16),
        ],
        in_specs=[vmem] * 3 + [anywhere] * 7,
        out_specs=[vmem] * 4,
        scratch_shapes=[
            pltpu.VMEM((GROUPS, rows, model), BF16),
            *[hold(a) for a in (hid, wq, wo, kv, qpad, att, lse)],
            hold(qpad),
            hold(lse),
            pltpu.VMEM((HEADS, 2 * HD, many), F32),
            hold(kv),
            pltpu.VMEM((6, *kv.shape[1:]), BF16),
            pltpu.VMEM((2, many // 2, 2 * width), BF16),
            pltpu.VMEM((many, 3 * width), BF16),
            pltpu.VMEM((GROUPS, rows, model), BF16),
            pltpu.VMEM((2, rows // 2, model), BF16),
            pltpu.VMEM((2, rows, model), BF16),
            hold(wq),
            pltpu.VMEM((6, GROUPS, shard, 3 * width), BF16),
            pltpu.VMEM((2, GROUPS // 2, shard, 3 * width), BF16),
            pltpu.VMEM((PLANE, padded, model), BF16),
            pltpu.VMEM((6, padded, model), BF16),
            pltpu.VMEM((2, padded // 2, model), BF16),
            pltpu.SemaphoreType.DMA((7,)),
            wire_sems(4),
            wire_sems(8),
            wire_sems(6),
            wire_sems(8),
            wire_sems(8),
        ],
        compiler_params=pltpu.CompilerParams(
            collective_id=1, has_side_effects=True, vmem_limit_bytes=56 * 2**20
        ),
        name="back",
    )(frames, gain, grad_mixed, hid, wq, wo, kv, qpad, att, lse)


def halo(array, width):
    devices, length = lax.axis_size("seq"), array.shape[0]
    up = [(i, i + 1) for i in range(devices - 1)]
    down = [(j, i) for i, j in up]
    before = lax.ppermute(array[length - width :], "seq", up)
    after = lax.ppermute(array[:width], "seq", down)
    return jnp.concatenate([before, array, after], axis=0)


def layer_norm(values, gain):
    center = values - jnp.mean(values, axis=-1, keepdims=True)
    spread = jnp.mean(center * center, axis=-1, keepdims=True)
    inverse = lax.rsqrt(spread + EPS)
    normed = center * inverse
    return (normed * gain, normed, inverse)


def norm_back(grad, normed, inverse, gain):
    scaled = grad * gain
    inner = (
        scaled
        - jnp.mean(scaled, axis=-1, keepdims=True)
        - normed * jnp.mean(scaled * normed, axis=-1, keepdims=True)
    )
    return (inverse * inner, jnp.sum(grad * normed, axis=0))


def depthwise(wide, kernel, length):
    total = jnp.zeros((length, wide.shape[1]), F32)
    for tap in range(kernel.shape[0]):
        total = total + wide[tap : tap + length] * kernel[tap]
    return total


def local(frames, w_qkv, w_out, norm_gains, conv_kernel, conv_bias, out_grad):
    frames = frames[0]
    rows, model = frames.shape
    shard, three = w_qkv.shape
    width = three // (3 * GROUPS)
    share_out = w_out.shape[0]

    split = w_qkv.reshape(shard, 3, GROUPS, HEADS, HD)
    w_parts = jnp.concatenate(
        [
            split[:, 0].reshape(shard, GROUPS, width),
            split[:, 1:].transpose(0, 2, 3, 1, 4).reshape(shard, GROUPS, 2 * width),
        ],
        axis=2,
    ).transpose(1, 0, 2)
    out_rows = jnp.pad(w_out, ((0, 32 - share_out), (0, 0)))
    mixed, *kept = front(frames, norm_gains[:1], w_parts, out_rows)

    mixed32 = mixed.astype(F32)
    shifted2, normed2, inverse2 = layer_norm(mixed32, norm_gains[1])
    conv_in = shifted2.astype(BF16)
    taps = conv_kernel.shape[0]
    half = (taps - 1) // 2
    conv_wide = halo(conv_in, half).astype(F32)
    preact = depthwise(conv_wide, conv_kernel, rows) + conv_bias
    sigma = jax.nn.sigmoid(preact)
    output = (mixed32 + preact * sigma).astype(BF16)
    upstream = out_grad[0].astype(F32)
    grad_pre = (upstream * sigma * (1.0 + preact * (1.0 - sigma))).astype(BF16)
    grad_pre_wide = halo(grad_pre, half).astype(F32)
    grad_conv = depthwise(grad_pre_wide, conv_kernel[::-1], rows)
    grad_pre_float = grad_pre.astype(F32)
    kernel_grad = lax.optimization_barrier(
        [jnp.sum(grad_pre_float * conv_wide[tap : tap + rows], axis=0) for tap in range(taps)]
    )
    bias_grad = jnp.sum(grad_pre_float, axis=0)
    mixed_norm_grad, gain2_grad = norm_back(grad_conv, normed2, inverse2, norm_gains[1])
    grad_mixed = (upstream + mixed_norm_grad).astype(BF16)

    grad_input, gain1_grad, w_sum, out_sum = back(frames, norm_gains[:1], grad_mixed, *kept)
    out_sum = out_sum[:share_out]

    dp = lax.axis_size("dp")
    lanes = 128
    w_split = w_sum.reshape(GROUPS, dp, -1, lanes).transpose(1, 0, 2, 3)
    out_split = out_sum.reshape(dp, -1, lanes)
    small = jnp.stack([gain1_grad[0], gain2_grad, bias_grad, *kernel_grad])
    count = small.shape[0]
    small_split = small.reshape(count, dp, -1).transpose(1, 0, 2)
    w_dp, out_dp, small_dp = exchange(
        7, (w_split, "dp", "a2a"), (out_split, "dp", "a2a"), (small_split, "dp", "a2a")
    )
    w_share = jnp.sum(w_dp.astype(F32), axis=0).astype(BF16)
    out_share = jnp.sum(out_dp.astype(F32), axis=0).astype(BF16)
    small_share = jnp.sum(small_dp, axis=0)
    w_home, small_seq = exchange(8, (w_share, "y", "a2a"), (small_share, "seq", "gather"))
    small_sum = jnp.sum(small_seq, axis=0)
    w_fin, out_fin, small_fin = exchange(
        9, (w_home, "dp", "gather"), (out_share, "dp", "gather"), (small_sum, "dp", "gather")
    )
    groups = w_fin.transpose(1, 0, 2, 3).reshape(GROUPS, shard, 3 * width)
    pairs = groups[:, :, width:].reshape(GROUPS, shard, HEADS, 2, HD)
    grad_qkv = jnp.concatenate(
        [
            groups[:, :, :width].transpose(1, 0, 2).reshape(shard, three // 3),
            pairs.transpose(1, 3, 0, 2, 4).reshape(shard, 2 * three // 3),
        ],
        axis=1,
    )
    grad_out = out_fin.reshape(share_out, model)
    small_all = small_fin.transpose(1, 0, 2).reshape(count, model)
    return (
        output[None],
        grad_input[None],
        grad_qkv,
        grad_out,
        small_all[:2],
        small_all[3:],
        small_all[2],
    )


def solution(mesh):
    in_specs = (
        P("dp", "seq", None),
        P("seq", None),
        P("seq", None),
        P(),
        P(),
        P(),
        P("dp", "seq", None),
    )
    out_specs = (
        P("dp", "seq", None),
        P("dp", "seq", None),
        P("seq", None),
        P("seq", None),
        P(),
        P(),
        P(),
    )
    return jax.shard_map(local, mesh=mesh, in_specs=in_specs, out_specs=out_specs, check_vma=False)
```

```python
import functools

import jax
import jax.numpy as jnp
from jax import lax
from jax.experimental import pallas as pl
from jax.experimental.pallas import tpu as pltpu
from jax.sharding import PartitionSpec as P

EPS = 1e-05
GROUPS = 4
PLANE = 8
HEADS = 3
HD = 64
F32 = jnp.float32
BF16 = jnp.bfloat16


def dot(a, b, ca, cb):
    return lax.dot_general(a, b, (((ca,), (cb,)), ((), ())), preferred_element_type=F32)


class Place:
    def __init__(self):
        seq = lax.axis_index("seq")
        y, z, x = seq // 8, (seq // 4) % 2, seq % 4
        right, left, far, other = (x + 1) % 4, (x + 3) % 4, (x + 2) % 4, 1 - z
        self.y, self.yp, self.ym, self.yf = y, (y + 1) % 4, (y + 3) % 4, (y + 2) % 4
        self.me = z * 4 + x
        self.xp, self.xm, self.xf = z * 4 + right, z * 4 + left, z * 4 + far
        self.zo = other * 4 + x
        self.zxp, self.zxm, self.zxf = other * 4 + right, other * 4 + left, other * 4 + far

        self.seq, self.dp = seq, lax.axis_index("dp")
        self.core, self.hi = self.dp % 2, self.dp // 2

    def plane(self, p):
        return {"seq": self.y * 8 + p}

    def holder(self, y, dp):
        return {"seq": y * 8 + self.me, "dp": dp}

    def greet_all(self):
        barrier = pltpu.get_barrier_semaphore()
        near = [{"seq": (self.seq + i) % 32} for i in range(1, 32)]
        near += [
            self.holder((self.y + i) % 4, (self.dp + j) % 8) for i in range(4) for j in range(1, 8)
        ]
        for device in near:
            pl.semaphore_signal(barrier, inc=1, device_id=device)
        pl.semaphore_wait(barrier, len(near))

    def column(self, y):
        return {"seq": y * 8 + self.me}

    def greet(self):
        barrier = pltpu.get_barrier_semaphore()
        near = [self.column(y) for y in (self.yp, self.ym, self.yf)]
        near += [self.plane(p) for p in (self.xp, self.xm, self.zo)]
        for device in near:
            pl.semaphore_signal(barrier, inc=1, device_id=device)
        pl.semaphore_wait(barrier, len(near))


class Wire:
    def __init__(self, sems):
        self.sems, self.sent = sems, {}

    def go(self, k, src, dst, device):
        copy = pltpu.make_async_remote_copy(
            src_ref=src,
            dst_ref=dst,
            send_sem=self.sems.at[0, k],
            recv_sem=self.sems.at[1, k],
            device_id=device,
        )
        copy.start()
        self.sent[k] = copy

    def got(self, *ks):
        for k in ks:
            self.sent[k].wait_recv()

    def done(self):
        for copy in self.sent.values():
            copy.wait_send()


def wire_sems(count):
    return pltpu.SemaphoreType.DMA((2, count))


class ColumnGather(Wire):
    def __init__(self, sems, place, buf):
        super().__init__(sems)
        self.at, self.buf = place, buf
        self.half = buf.shape[1] // 2

    def begin(self):
        t, own = self.at, self.buf.at[self.at.y]
        self.go(0, own, own, t.column(t.yp))
        self.go(1, own, own, t.column(t.ym))

    def relay(self):
        t, h = self.at, self.half
        self.got(0)
        first = self.buf.at[t.ym, pl.ds(0, h)]
        self.go(2, first, first, t.column(t.yp))
        self.got(1)
        second = self.buf.at[t.yp, pl.ds(h, h)]
        self.go(3, second, second, t.column(t.ym))

    def finish(self):
        self.got(2, 3)


class ColumnReduce(Wire):
    def __init__(self, sems, place, part, relays, lands):
        super().__init__(sems)
        self.at, self.part, self.relays, self.lands = place, part, relays, lands
        self.half = part.shape[1] // 2

    def far(self):
        t, h = self.at, self.half
        self.go(0, self.part.at[t.yf, pl.ds(0, h)], self.relays.at[0], t.column(t.ym))
        self.go(1, self.part.at[t.yf, pl.ds(h, h)], self.relays.at[1], t.column(t.yp))

    def near(self):
        t, h = self.at, self.half
        low, high = pl.ds(0, h), pl.ds(h, h)
        self.go(2, self.part.at[t.ym, high], self.lands.at[0, high], t.column(t.ym))
        self.go(3, self.part.at[t.yp, low], self.lands.at[1, low], t.column(t.yp))
        self.got(0)
        self.part[t.ym, low] = (
            self.part[t.ym, low].astype(F32) + self.relays[0].astype(F32)
        ).astype(BF16)
        self.go(4, self.part.at[t.ym, low], self.lands.at[0, low], t.column(t.ym))
        self.got(1)
        self.part[t.yp, high] = (
            self.part[t.yp, high].astype(F32) + self.relays[1].astype(F32)
        ).astype(BF16)
        self.go(5, self.part.at[t.yp, high], self.lands.at[1, high], t.column(t.yp))

    def finish(self):
        self.got(2, 3, 4, 5)
        return (
            self.part[self.at.y].astype(F32)
            + self.lands[0].astype(F32)
            + self.lands[1].astype(F32)
        )


class PlaneGather(Wire):
    def __init__(self, sems, place, full, half):
        super().__init__(sems)
        self.at, self.full, self.half = place, full, half

    def begin(self):
        t, own = self.at, self.full(self.at.me)
        self.go(0, own, own, t.plane(t.xp))
        self.go(1, own, own, t.plane(t.xm))
        self.go(2, own, own, t.plane(t.zo))

    def relay(self):
        t = self.at
        self.got(0)
        first = self.half(t.xm, 0)
        self.go(3, first, first, t.plane(t.xp))
        self.got(1)
        second = self.half(t.xp, 1)
        self.go(4, second, second, t.plane(t.xm))
        self.got(2)
        other = self.full(t.zo)
        self.go(5, other, other, t.plane(t.xp))
        self.go(6, other, other, t.plane(t.xm))

    def cross(self):
        t = self.at
        for k in (0, 1):
            self.got(3 + k)
            part = self.half(t.xf, k)
            self.go(7 + k, part, part, t.plane(t.zo))

    def finish(self):
        self.got(5, 6, 7, 8)


class PlaneReduce(Wire):
    def __init__(self, sems, place, full, half, land, half_land):
        super().__init__(sems)
        self.at, self.full, self.half = place, full, half
        self.land, self.half_land = land, half_land

    def add(self, ref, *more):
        total = ref[...].astype(F32)
        for other in more:
            total = total + other[...].astype(F32)
        ref[...] = total.astype(BF16)

    def far(self):
        t = self.at
        self.go(0, self.full(t.zxf), self.land(0), t.plane(t.zo))

    def sides(self):
        t = self.at
        self.go(1, self.full(t.zxm), self.land(1), t.plane(t.xm))
        self.go(2, self.full(t.zxp), self.land(2), t.plane(t.xp))

    def opposite(self):
        t = self.at
        self.got(0)
        self.add(self.full(t.xf), self.land(0))
        self.go(3, self.half(t.xf, 0), self.half_land(0), t.plane(t.xm))
        self.go(4, self.half(t.xf, 1), self.half_land(1), t.plane(t.xp))

    def across(self):
        t = self.at
        self.got(1, 2)
        self.add(self.full(t.zo), self.land(1), self.land(2))
        self.go(5, self.full(t.zo), self.land(3), t.plane(t.zo))

    def near(self):
        t = self.at
        self.got(3)
        self.add(self.half(t.xm, 0), self.half_land(0))
        self.go(6, self.full(t.xm), self.land(4), t.plane(t.xm))
        self.got(4)
        self.add(self.half(t.xp, 1), self.half_land(1))
        self.go(7, self.full(t.xp), self.land(5), t.plane(t.xp))

    def finish(self):
        self.got(5, 6, 7)
        total = self.full(self.at.me)[...].astype(F32)
        for k in (3, 4, 5):
            total = total + self.land(k)[...].astype(F32)
        return total


def pick(i, *values):
    out = values[-1]
    for k in range(len(values) - 2, -1, -1):
        out = jnp.where(i == k, values[k], out)
    return out


def local_copies(pairs, sems):
    copies = [
        pltpu.make_async_copy(src, dst, sems.at[i]) for i, (src, dst) in enumerate(pairs)
    ]
    for copy in copies:
        copy.start()
    return copies


QB = 128


def forward_chunk(kv, c, qpad, top, total, acc):
    many = qpad.shape[1]
    for h in range(HEADS):
        both = kv[c, :, h * 128 : (h + 1) * 128]
        for b in range(many // QB):
            cols = slice(b * QB, (b + 1) * QB)
            scores = dot(both, qpad[h, cols, :], 1, 1)
            old = top[h, :, cols]
            new = jnp.maximum(old, jnp.max(scores, axis=0, keepdims=True))
            shrink = jnp.exp(old - new)
            expo = jnp.exp(scores - new)
            top[h, :, cols] = new
            total[h, :, cols] = total[h, :, cols] * shrink + jnp.sum(expo, axis=0, keepdims=True)
            acc[h, :, cols] = acc[h, :, cols] * shrink + dot(both, expo.astype(BF16), 0, 0)


def front_kernel(
    frames,
    gain,
    w_parts,
    w_out,
    mixed_out,
    hid_out,
    wq_out,
    wo_out,
    kv_out,
    qpad_out,
    att_out,
    lse_out,
    hid,
    wq,
    wo,
    wo32,
    wo16,
    kv,
    qpad,
    top,
    total,
    acc,
    att,
    part,
    relays,
    lands,
    w_sems,
    own_sem,
    hid_sems,
    wq_sems,
    wo_sems,
    kv_sems,
    red_sems,
    out_sems,
):
    t = Place()
    t.greet()
    rows = frames.shape[0]
    many = GROUPS * rows
    spread = Wire(w_sems)
    for k, y in enumerate((t.yp, t.ym, t.yf)):
        spread.go(k, w_parts.at[y], wq.at[t.y, t.me], t.column(y))
    own = pltpu.make_async_copy(w_parts.at[t.y], wq.at[t.y, t.me], own_sem.at[0])
    own.start()
    wo[t.me] = w_out[...]

    inputs = frames[...].astype(F32)
    shifted, _, _ = layer_norm(inputs, gain[...])
    hid[t.y] = shifted.astype(BF16)
    hid_net = ColumnGather(hid_sems, t, hid)
    hid_net.begin()
    own.wait()
    spread.got(0, 1, 2)
    wq_net = PlaneGather(
        wq_sems, t, lambda p: wq.at[:, p], lambda p, i: wq.at[pl.ds(2 * i, 2), p]
    )
    wo_net = PlaneGather(
        wo_sems, t, lambda p: wo.at[p], lambda p, i: wo.at[p, pl.ds(16 * i, 16)]
    )
    wq_net.begin()
    hid_net.relay()
    wq_net.relay()
    wq_net.cross()
    wo_net.begin()
    hid_net.finish()
    wq_net.finish()
    saves = local_copies([(hid, hid_out), (wq, wq_out)], out_sems.at[pl.ds(0, 2)])

    model = frames.shape[1]
    width = HEADS * HD
    hidden = hid[...].reshape(many, model)
    weights = wq[...].reshape(model, 3 * width)
    projected = dot(hidden, weights, 1, 0).astype(BF16)
    kv[t.me] = projected[:, width:]
    kv_net = PlaneGather(
        kv_sems,
        t,
        lambda p: kv.at[p],
        lambda p, i: kv.at[p, pl.ds(i * (many // 2), many // 2)],
    )
    kv_net.begin()
    zeros = jnp.zeros((many, HD), BF16)
    for h in range(HEADS):
        qpad[h] = jnp.concatenate(
            [projected[:, h * HD : (h + 1) * HD] * BF16(HD**-0.5), zeros], axis=1
        )
    top[...] = jnp.full_like(top, -jnp.inf)
    total[...] = jnp.zeros_like(total)
    acc[...] = jnp.zeros_like(acc)

    def attend(*chunks):
        if len(chunks) == 1:
            forward_chunk(kv, chunks[0], qpad, top, total, acc)
            return

        def step(i, carry):
            forward_chunk(kv, pick(i, *chunks), qpad, top, total, acc)
            return carry

        lax.fori_loop(0, len(chunks), step, 0)

    attend(t.me)
    kv_net.relay()
    wo_net.relay()
    attend(t.xm, t.xp, t.zo)
    kv_net.cross()
    wo_net.cross()
    attend(t.xf)
    kv_net.got(5, 6)
    attend(t.zxm, t.zxp)
    kv_net.got(7, 8)
    saves += local_copies([(kv, kv_out), (qpad, qpad_out)], out_sems.at[pl.ds(2, 2)])
    attend(t.zxf)
    wo_net.finish()
    share = width // PLANE
    for p in range(PLANE):
        wo32[p * share : (p + 1) * share, :] = wo[p, 0:share, :].astype(F32)
    wo16[...] = wo32[...].astype(BF16)
    blocks = []
    for h in range(HEADS):
        blocks.append((acc[h, HD : 2 * HD, :] / total[h]).T.astype(BF16))
        top[h] = top[h] + jnp.log(total[h])
    att[...] = jnp.concatenate(blocks, axis=1)
    saves += local_copies([(wo16, wo_out), (att, att_out), (top, lse_out)], out_sems.at[pl.ds(4, 3)])

    def product(y):
        here = att[pl.ds(pl.multiple_of(y * rows, rows), rows), :]
        part[y] = dot(here, wo16[...], 1, 0).astype(BF16)

    red = ColumnReduce(red_sems, t, part, relays, lands)
    product(t.yf)
    red.far()
    product(t.ym)
    product(t.yp)
    product(t.y)
    red.near()
    mixed_out[...] = (frames[...].astype(F32) + red.finish()).astype(BF16)
    for net in (spread, hid_net, wq_net, wo_net, kv_net, red):
        net.done()
    for copy in saves:
        copy.wait()


def front(frames, gain, w_parts, w_out):
    rows, model = frames.shape
    _, shard, trio = w_parts.shape
    width = trio // 3
    many = GROUPS * rows
    vmem, anywhere = pl.BlockSpec(memory_space=pltpu.VMEM), pl.BlockSpec(memory_space=pl.ANY)
    like = jax.ShapeDtypeStruct
    return pl.pallas_call(
        front_kernel,
        out_shape=[
            like((rows, model), BF16),
            like((GROUPS, rows, model), BF16),
            like((GROUPS, PLANE, shard, trio), BF16),
            like((width, model), BF16),
            like((PLANE, many, 2 * width), BF16),
            like((HEADS, many, 2 * HD), BF16),
            like((many, width), BF16),
            like((HEADS, 1, many), F32),
        ],
        in_specs=[vmem] * 4,
        out_specs=[vmem] + [anywhere] * 7,
        scratch_shapes=[
            pltpu.VMEM((GROUPS, rows, model), BF16),
            pltpu.VMEM((GROUPS, PLANE, shard, trio), BF16),
            pltpu.VMEM((PLANE, *w_out.shape), BF16),
            pltpu.VMEM((width, model), F32),
            pltpu.VMEM((width, model), BF16),
            pltpu.VMEM((PLANE, many, 2 * width), BF16),
            pltpu.VMEM((HEADS, many, 2 * HD), BF16),
            pltpu.VMEM((HEADS, 1, many), F32),
            pltpu.VMEM((HEADS, 1, many), F32),
            pltpu.VMEM((HEADS, 2 * HD, many), F32),
            pltpu.VMEM((many, width), BF16),
            pltpu.VMEM((GROUPS, rows, model), BF16),
            pltpu.VMEM((2, rows // 2, model), BF16),
            pltpu.VMEM((2, rows, model), BF16),
            wire_sems(3),
            pltpu.SemaphoreType.DMA((1,)),
            wire_sems(4),
            wire_sems(9),
            wire_sems(9),
            wire_sems(9),
            wire_sems(6),
            pltpu.SemaphoreType.DMA((7,)),
        ],
        compiler_params=pltpu.CompilerParams(
            collective_id=0, has_side_effects=True, vmem_limit_bytes=48 * 2**20
        ),
        name="front",
    )(frames, gain, w_parts, w_out)


def backward_chunk(kv, c, qpad, dopad, lse, delta, dqt, out):
    for h in range(HEADS):
        lanes = slice(h * 128, (h + 1) * 128)
        both, query, grad = kv[c, :, lanes], qpad[h], dopad[h]
        scores = dot(both, query, 1, 1)
        slopes = dot(both, grad, 1, 1)
        probs = jnp.exp(scores - lse[h])
        score_grads = (probs * (slopes - delta[h])).astype(BF16)
        out[c, :, lanes] = (
            dot(probs.astype(BF16), grad, 1, 0) + dot(score_grads, query, 1, 0)
        ).astype(BF16)
        dqt[h] += dot(both, score_grads, 0, 0)


def back_kernel(
    frames,
    gain,
    grad_mixed,
    hid_in,
    wq_in,
    wo_in,
    kv_in,
    qpad_in,
    att_in,
    lse_in,
    small,
    gain2_grad,
    grad_input,
    grad_qkv,
    grad_out,
    kernel_sum,
    bias_sum,
    norms_sum,
    mix,
    hid,
    wq,
    wo,
    kv,
    qpad,
    att,
    lse,
    dopad,
    delta,
    dqt,
    dkv,
    kv_land,
    kv_half,
    proj,
    part,
    relays,
    lands,
    w_part,
    w_core,
    w_land,
    w_half,
    w_hi,
    w_done,
    w_fin,
    o_part,
    o_core,
    o_land,
    o_half,
    o_hi,
    o_done,
    o_fin,
    s_send,
    s_seq,
    s_mine,
    s_dp,
    s_done,
    s_fin,
    in_sems,
    mix_sems,
    kv_sems,
    red_sems,
    core_sems,
    w_sems,
    o_sems,
    hi_sems,
    w_fin_send,
    w_fin_recv,
    o_fin_send,
    o_fin_recv,
    s_sems,
    s_dp_sems,
    s_fin_sems,
):
    t = Place()
    t.greet_all()
    rows, model = frames.shape
    many = GROUPS * rows
    width = HEADS * HD
    taps = kernel_sum.shape[0]
    mix[t.y] = grad_mixed[...]
    mix_net = ColumnGather(mix_sems, t, mix)
    mix_net.begin()
    loads = local_copies(
        [
            (wo_in, wo),
            (att_in, att),
            (qpad_in, qpad),
            (lse_in, lse),
            (kv_in, kv),
            (hid_in, hid),
            (wq_in, wq),
        ],
        in_sems,
    )
    for copy in loads:
        copy.wait()
    mix_net.relay()
    mix_net.finish()

    mixed = mix[...].reshape(many, model)
    grads = dot(mixed, wo[...], 1, 1).astype(BF16)
    zeros = jnp.zeros((many, HD), BF16)
    for h in range(HEADS):
        lanes = slice(h * HD, (h + 1) * HD)
        mine = grads[:, lanes]
        dopad[h] = jnp.concatenate([zeros, mine], axis=1)
        delta[h] = jnp.sum(
            (att[:, lanes].astype(F32) * mine.astype(F32)).T, axis=0, keepdims=True
        )
    dqt[...] = jnp.zeros_like(dqt)

    def attend(*chunks):
        def step(i, carry):
            backward_chunk(kv, pick(i, *chunks), qpad, dopad, lse, delta, dqt, dkv)
            return carry

        if len(chunks) == 1:
            step(0, 0)
        else:
            lax.fori_loop(0, len(chunks), step, 0)

    half = many // 2
    net = PlaneReduce(
        kv_sems,
        t,
        lambda p: dkv.at[p],
        lambda p, i: dkv.at[p, pl.ds(i * half, half)],
        lambda k: kv_land.at[k],
        lambda k: kv_half.at[k],
    )
    attend(t.zxf)
    net.far()
    attend(t.zxm, t.zxp)
    net.sides()
    attend(t.xf)
    net.opposite()
    attend(t.zo)
    net.across()
    attend(t.xm, t.xp)
    net.near()
    attend(t.me)
    for h in range(HEADS):
        proj[:, h * HD : (h + 1) * HD] = (dqt[h, 0:HD, :] * HD**-0.5).T.astype(BF16)

    out_terms = dot(att[...], mixed, 0, 0)
    share = width // PLANE
    blocks = o_part.shape[2]
    wide = model // 2
    for c in range(2):
        for p in range(PLANE):
            for i in range(blocks):
                piece = o_part.at[c, p, i]
                if i * 8 < share:
                    start = p * share + i * 8
                    piece[...] = out_terms[
                        start : start + 8, c * wide : (c + 1) * wide
                    ].astype(BF16)
                else:
                    piece[...] = jnp.zeros(piece.shape, BF16)
    order = (t.zxf, t.zxm, t.zxp, t.xf, t.zo, t.xm, t.xp, t.me)
    buddy = {"dp": t.hi * 2 + 1 - t.core}
    pair = Wire(core_sems)
    for k, p in enumerate(order):
        pair.go(k, o_part.at[1 - t.core, p], o_core.at[p], buddy)
    proj[:, width:] = net.finish().astype(BF16)

    weights = wq[...].reshape(model, 3 * width)

    def product(y):
        here = proj[pl.ds(pl.multiple_of(y * rows, rows), rows), :]
        part[y] = dot(here, weights, 1, 1).astype(BF16)

    red = ColumnReduce(red_sems, t, part, relays, lands)
    product(t.yf)
    red.far()
    hidden = hid[...].reshape(many, model)
    half_rows = w_part.shape[3]
    w_terms = dot(hidden, proj[...], 0, 0).reshape(
        GROUPS, PLANE, 2, half_rows, 3 * width
    )
    for c in range(2):
        w_part[c] = w_terms[:, :, c].astype(BF16)
    for k, p in enumerate(order):
        pair.go(8 + k, w_part.at[1 - t.core, :, p], w_core.at[:, p], buddy)
    w_mine, o_mine = w_part.at[t.core], o_part.at[t.core]
    o_net = PlaneReduce(
        o_sems,
        t,
        lambda p: o_mine.at[p],
        lambda p, i: o_mine.at[p, pl.ds(2 * i, 2)],
        lambda k: o_land.at[k],
        lambda k: o_half.at[k],
    )
    w_net = PlaneReduce(
        w_sems,
        t,
        lambda p: w_mine.at[:, p],
        lambda p, i: w_mine.at[pl.ds(2 * i, 2), p],
        lambda k: w_land.at[k],
        lambda k: w_half.at[k],
    )

    def join(first, last):
        for k in range(first, last):
            p = order[k]
            pair.got(k, 8 + k)
            o_net.add(o_mine.at[p], o_core.at[p])
            w_net.add(w_mine.at[:, p], w_core.at[:, p])

    product(t.ym)
    product(t.yp)
    product(t.y)
    red.near()
    join(0, 1)
    w_net.far()
    o_net.far()
    join(1, 3)
    w_net.sides()
    o_net.sides()
    join(3, 8)
    w_net.opposite()
    o_net.opposite()
    w_net.across()
    o_net.across()
    w_net.near()
    o_net.near()

    grad_hidden = red.finish()
    _, normed, inverse = layer_norm(frames[...].astype(F32), gain[...])
    norm_grad, gain_sum = norm_back(grad_hidden, normed, inverse, gain[...])
    grad_input[...] = (grad_mixed[...].astype(F32) + norm_grad).astype(BF16)
    gains = (gain_sum[None], gain2_grad[...])
    count = s_send.shape[0]
    for r in range(count):
        s_send[r, :, 0:model] = small[r]
        if r < 2 * (model // 128):
            row, col = divmod(r, model // 128)
            s_send[r, :, model:] = gains[row][:, col * 128 : (col + 1) * 128]
        else:
            s_send[r, :, model:] = jnp.zeros((1, 128), F32)
    s_net = Wire(s_sems)
    s_seq[t.seq] = s_send[t.seq]
    for k in range(1, count):
        r = (t.seq + k) % count
        s_net.go(k - 1, s_send.at[r], s_seq.at[t.seq], {"seq": r})

    o_total, w_total = o_net.finish(), w_net.finish()
    o_mine[t.me] = o_total.astype(BF16)
    w_mine[:, t.me] = w_total.astype(BF16)
    hi_net = Wire(hi_sems)
    for k in range(1, 4):
        j = (t.hi + k) % 4
        there = {"dp": j * 2 + t.core}
        hi_net.go(k - 1, w_mine.at[j, t.me], w_hi.at[k - 1], there)
        hi_net.go(2 + k, o_mine.at[t.me, j], o_hi.at[k - 1], there)

    s_net.got(*range(count - 1))
    s_mine[...] = jnp.sum(s_seq[...], axis=0)
    s_dp[t.dp] = s_mine[...]
    s_dp_net = Wire(s_dp_sems)
    for k in range(1, 8):
        s_dp_net.go(k - 1, s_mine, s_dp.at[t.dp], {"dp": (t.dp + k) % 8})

    hi_net.got(*range(6))
    w_out_block = w_mine[t.hi, t.me].astype(F32)
    o_out_block = o_mine[t.me, t.hi].astype(F32)
    for k in range(3):
        w_out_block = w_out_block + w_hi[k].astype(F32)
        o_out_block = o_out_block + o_hi[k].astype(F32)
    w_done[...] = w_out_block.astype(BF16)
    o_done[...] = o_out_block.astype(BF16)
    finals = []
    for k in range(1, 8):
        d = (t.dp + k) % 8
        for src, dst, send, recv, y in (
            (w_done, w_fin.at[t.y, t.core], w_fin_send.at[k], w_fin_recv.at[t.y, t.core], t.hi),
            (o_done, o_fin.at[t.hi, t.core], o_fin_send.at[k], o_fin_recv.at[t.hi, t.core], t.y),
        ):
            copy = pltpu.make_async_remote_copy(
                src_ref=src, dst_ref=dst, send_sem=send, recv_sem=recv, device_id=t.holder(y, d)
            )
            copy.start()
            finals.append(copy)
    o_own = pltpu.make_async_copy(
        o_done, o_fin.at[t.hi, t.core], o_fin_recv.at[t.hi, t.core]
    )
    o_own.start()
    w_own = pltpu.make_async_copy(w_done, w_fin.at[t.y, t.core], w_fin_recv.at[t.y, t.core])
    w_away = pltpu.make_async_remote_copy(
        src_ref=w_done,
        dst_ref=w_fin.at[t.y, t.core],
        send_sem=w_fin_send.at[0],
        recv_sem=w_fin_recv.at[t.y, t.core],
        device_id=t.holder(t.hi, t.dp),
    )

    @pl.when(t.hi == t.y)
    def _():
        w_own.start()

    @pl.when(t.hi != t.y)
    def _():
        w_away.start()

    s_dp_net.got(*range(7))
    summed = s_dp[0]
    for d in range(1, 8):
        summed = summed + s_dp[d]
    s_done[...] = summed
    s_fin[t.seq] = summed
    s_fin_net = Wire(s_fin_sems)
    for k in range(1, count):
        s_fin_net.go(k - 1, s_done, s_fin.at[t.seq], {"seq": (t.seq + k) % count})

    for i in range(4):
        for c in range(2):
            pltpu.make_async_copy(w_done, w_fin.at[i, c], w_fin_recv.at[i, c]).wait()
            pltpu.make_async_copy(o_done, o_fin.at[i, c], o_fin_recv.at[i, c]).wait()
    pieces = [w_fin[y].astype(F32).reshape(2 * half_rows, 3 * width) for y in range(GROUPS)]
    columns = [piece[:, :width] for piece in pieces]
    for kind in range(2):
        for piece in pieces:
            for h in range(HEADS):
                start = width + (2 * h + kind) * HD
                columns.append(piece[:, start : start + HD])
    grad_qkv[...] = jnp.concatenate(columns, axis=1).astype(BF16)
    sides = [
        o_fin[0 : share // 8, c].astype(F32).reshape(share, wide) for c in range(2)
    ]
    grad_out[...] = jnp.concatenate(sides, axis=1).astype(BF16)
    s_fin_net.got(*range(count - 1))
    for r in range(count):
        row = s_fin[r]
        if r < taps:
            kernel_sum[r : r + 1, :] = row[:, :model]
        else:
            bias_sum[...] = row[:, :model]
        if r < 2 * (model // 128):
            i, col = divmod(r, model // 128)
            norms_sum[i : i + 1, col * 128 : (col + 1) * 128] = row[:, model:]
    for copy in finals:
        copy.wait_send()

    @pl.when(t.hi != t.y)
    def _():
        w_away.wait_send()

    for wire in (mix_net, net, pair, o_net, red, w_net, hi_net, s_net, s_dp_net, s_fin_net):
        wire.done()


def back(frames, gain, grad_mixed, hid, wq, wo, kv, qpad, att, lse, small, gain2_grad):
    rows, model = frames.shape
    many = GROUPS * rows
    width = HEADS * HD
    shard = wq.shape[2]
    half = shard // 2
    count = small.shape[0]
    vmem, anywhere = pl.BlockSpec(memory_space=pltpu.VMEM), pl.BlockSpec(memory_space=pl.ANY)
    like = jax.ShapeDtypeStruct

    def hold(array):
        return pltpu.VMEM(array.shape, array.dtype)

    def bf16(*shape):
        return pltpu.VMEM(shape, BF16)

    def f32(*shape):
        return pltpu.VMEM(shape, F32)

    return pl.pallas_call(
        back_kernel,
        out_shape=[
            like((rows, model), BF16),
            like((shard, 12 * width), BF16),
            like((width // PLANE, model), BF16),
            like((count - 1, model), F32),
            like((1, model), F32),
            like((2, model), F32),
        ],
        in_specs=[vmem] * 3 + [anywhere] * 7 + [vmem] * 2,
        out_specs=[vmem] * 6,
        scratch_shapes=[
            bf16(GROUPS, rows, model),
            *[hold(a) for a in (hid, wq, wo, kv, qpad, att, lse)],
            hold(qpad),
            hold(lse),
            f32(HEADS, 2 * HD, many),
            hold(kv),
            bf16(6, *kv.shape[1:]),
            bf16(2, many // 2, 2 * width),
            bf16(many, 3 * width),
            bf16(GROUPS, rows, model),
            bf16(2, rows // 2, model),
            bf16(2, rows, model),
            bf16(2, GROUPS, PLANE, half, 3 * width),
            bf16(GROUPS, PLANE, half, 3 * width),
            bf16(6, GROUPS, half, 3 * width),
            bf16(2, GROUPS // 2, half, 3 * width),
            bf16(3, half, 3 * width),
            bf16(half, 3 * width),
            bf16(GROUPS, 2, half, 3 * width),
            bf16(2, PLANE, 4, 8, model // 2),
            bf16(PLANE, 4, 8, model // 2),
            bf16(6, 4, 8, model // 2),
            bf16(2, 2, 8, model // 2),
            bf16(3, 8, model // 2),
            bf16(8, model // 2),
            bf16(4, 2, 8, model // 2),
            f32(count, 1, model + 128),
            f32(count, 1, model + 128),
            f32(1, model + 128),
            f32(8, 1, model + 128),
            f32(1, model + 128),
            f32(count, 1, model + 128),
            pltpu.SemaphoreType.DMA((7,)),
            wire_sems(4),
            wire_sems(8),
            wire_sems(6),
            wire_sems(16),
            wire_sems(8),
            wire_sems(8),
            wire_sems(6),
            pltpu.SemaphoreType.DMA((8,)),
            pltpu.SemaphoreType.DMA((4, 2)),
            pltpu.SemaphoreType.DMA((8,)),
            pltpu.SemaphoreType.DMA((4, 2)),
            wire_sems(count - 1),
            wire_sems(7),
            wire_sems(count - 1),
        ],
        compiler_params=pltpu.CompilerParams(
            collective_id=1, has_side_effects=True, vmem_limit_bytes=58 * 2**20
        ),
        name="back",
    )(frames, gain, grad_mixed, hid, wq, wo, kv, qpad, att, lse, small, gain2_grad)


def halo(array, width):
    devices, length = lax.axis_size("seq"), array.shape[0]
    up = [(i, i + 1) for i in range(devices - 1)]
    down = [(j, i) for i, j in up]
    before = lax.ppermute(array[length - width :], "seq", up)
    after = lax.ppermute(array[:width], "seq", down)
    return jnp.concatenate([before, array, after], axis=0)


def layer_norm(values, gain):
    center = values - jnp.mean(values, axis=-1, keepdims=True)
    spread = jnp.mean(center * center, axis=-1, keepdims=True)
    inverse = lax.rsqrt(spread + EPS)
    normed = center * inverse
    return (normed * gain, normed, inverse)


def norm_back(grad, normed, inverse, gain):
    scaled = grad * gain
    inner = (
        scaled
        - jnp.mean(scaled, axis=-1, keepdims=True)
        - normed * jnp.mean(scaled * normed, axis=-1, keepdims=True)
    )
    return (inverse * inner, jnp.sum(grad * normed, axis=0))


def depthwise(wide, kernel, length):
    total = jnp.zeros((length, wide.shape[1]), F32)
    for tap in range(kernel.shape[0]):
        total = total + wide[tap : tap + length] * kernel[tap]
    return total


def local(frames, w_qkv, w_out, norm_gains, conv_kernel, conv_bias, out_grad):
    frames = frames[0]
    rows, model = frames.shape
    shard, three = w_qkv.shape
    width = three // (3 * GROUPS)
    share_out = w_out.shape[0]

    split = w_qkv.reshape(shard, 3, GROUPS, HEADS, HD)
    w_parts = jnp.concatenate(
        [
            split[:, 0].reshape(shard, GROUPS, width),
            split[:, 1:].transpose(0, 2, 3, 1, 4).reshape(shard, GROUPS, 2 * width),
        ],
        axis=2,
    ).transpose(1, 0, 2)
    out_rows = jnp.pad(w_out, ((0, 32 - share_out), (0, 0)))
    mixed, *kept = front(frames, norm_gains[:1], w_parts, out_rows)

    mixed32 = mixed.astype(F32)
    shifted2, normed2, inverse2 = layer_norm(mixed32, norm_gains[1])
    conv_in = shifted2.astype(BF16)
    taps = conv_kernel.shape[0]
    half = (taps - 1) // 2
    conv_wide = halo(conv_in, half).astype(F32)
    preact = depthwise(conv_wide, conv_kernel, rows) + conv_bias
    sigma = jax.nn.sigmoid(preact)
    output = (mixed32 + preact * sigma).astype(BF16)
    upstream = out_grad[0].astype(F32)
    grad_pre = (upstream * sigma * (1.0 + preact * (1.0 - sigma))).astype(BF16)
    grad_pre_wide = halo(grad_pre, half).astype(F32)
    grad_conv = depthwise(grad_pre_wide, conv_kernel[::-1], rows)
    grad_pre_float = grad_pre.astype(F32)
    kernel_grad = lax.optimization_barrier(
        [jnp.sum(grad_pre_float * conv_wide[tap : tap + rows], axis=0) for tap in range(taps)]
    )
    bias_grad = jnp.sum(grad_pre_float, axis=0)
    mixed_norm_grad, gain2_grad = norm_back(grad_conv, normed2, inverse2, norm_gains[1])
    grad_mixed = (upstream + mixed_norm_grad).astype(BF16)

    small = jnp.stack([*kernel_grad, bias_grad])[:, None]
    grad_input, grad_qkv, grad_out, kernel_sum, bias_sum, norms_sum = back(
        frames, norm_gains[:1], grad_mixed, *kept, small, gain2_grad[None]
    )
    return (
        output[None],
        grad_input[None],
        grad_qkv,
        grad_out,
        norms_sum,
        kernel_sum,
        bias_sum[0],
    )


def solution(mesh):
    in_specs = (
        P("dp", "seq", None),
        P("seq", None),
        P("seq", None),
        P(),
        P(),
        P(),
        P("dp", "seq", None),
    )
    out_specs = (
        P("dp", "seq", None),
        P("dp", "seq", None),
        P("seq", None),
        P("seq", None),
        P(),
        P(),
        P(),
    )
    return jax.shard_map(local, mesh=mesh, in_specs=in_specs, out_specs=out_specs, check_vma=False)
```

```python
import functools

import jax
import jax.numpy as jnp
from jax import lax
from jax.experimental import pallas as pl
from jax.experimental.pallas import tpu as pltpu
from jax.sharding import PartitionSpec as P

EPS = 1e-05
GROUPS = 4
PLANE = 8
HEADS = 3
HD = 64
F32 = jnp.float32
BF16 = jnp.bfloat16


def layer_norm(values, gain):
    center = values - jnp.mean(values, axis=-1, keepdims=True)
    spread = jnp.mean(center * center, axis=-1, keepdims=True)
    inverse = lax.rsqrt(spread + EPS)
    normed = center * inverse
    return (normed * gain, normed, inverse)


def norm_back(grad, normed, inverse, gain):
    scaled = grad * gain
    inner = (
        scaled
        - jnp.mean(scaled, axis=-1, keepdims=True)
        - normed * jnp.mean(scaled * normed, axis=-1, keepdims=True)
    )
    return (inverse * inner, jnp.sum(grad * normed, axis=0))


def dot(a, b, ca, cb):
    return lax.dot_general(a, b, (((ca,), (cb,)), ((), ())), preferred_element_type=F32)


class Place:
    def __init__(self):
        seq = lax.axis_index("seq")
        y, z, x = seq // 8, (seq // 4) % 2, seq % 4
        right, left, far, other = (x + 1) % 4, (x + 3) % 4, (x + 2) % 4, 1 - z
        self.y, self.yp, self.ym, self.yf = y, (y + 1) % 4, (y + 3) % 4, (y + 2) % 4
        self.me = z * 4 + x
        self.xp, self.xm, self.xf = z * 4 + right, z * 4 + left, z * 4 + far
        self.zo = other * 4 + x
        self.zxp, self.zxm, self.zxf = other * 4 + right, other * 4 + left, other * 4 + far

        self.seq, self.dp = seq, lax.axis_index("dp")
        self.core, self.hi = self.dp % 2, self.dp // 2

    def plane(self, p):
        return {"seq": self.y * 8 + p}

    def holder(self, y, dp):
        return {"seq": y * 8 + self.me, "dp": dp}

    def greet(self):
        barrier = pltpu.get_barrier_semaphore()
        near = [{"seq": (self.seq + i) % 32} for i in range(1, 32)]
        near += [
            self.holder((self.y + i) % 4, (self.dp + j) % 8) for i in range(4) for j in range(1, 8)
        ]
        for device in near:
            pl.semaphore_signal(barrier, inc=1, device_id=device)
        pl.semaphore_wait(barrier, len(near))

    def column(self, y):
        return {"seq": y * 8 + self.me}


class Wire:
    def __init__(self, sems):
        self.sems, self.sent = sems, {}

    def go(self, k, src, dst, device):
        copy = pltpu.make_async_remote_copy(
            src_ref=src,
            dst_ref=dst,
            send_sem=self.sems.at[0, k],
            recv_sem=self.sems.at[1, k],
            device_id=device,
        )
        copy.start()
        self.sent[k] = copy

    def got(self, *ks):
        for k in ks:
            self.sent[k].wait_recv()

    def done(self):
        for copy in self.sent.values():
            copy.wait_send()


def wire_sems(count):
    return pltpu.SemaphoreType.DMA((2, count))


class ColumnGather(Wire):
    def __init__(self, sems, place, buf):
        super().__init__(sems)
        self.at, self.buf = place, buf
        self.half = buf.shape[1] // 2

    def begin(self):
        t, own = self.at, self.buf.at[self.at.y]
        self.go(0, own, own, t.column(t.yp))
        self.go(1, own, own, t.column(t.ym))

    def relay(self):
        t, h = self.at, self.half
        self.got(0)
        first = self.buf.at[t.ym, pl.ds(0, h)]
        self.go(2, first, first, t.column(t.yp))
        self.got(1)
        second = self.buf.at[t.yp, pl.ds(h, h)]
        self.go(3, second, second, t.column(t.ym))

    def finish(self):
        self.got(2, 3)


class ColumnReduce(Wire):
    def __init__(self, sems, place, part, relays, lands):
        super().__init__(sems)
        self.at, self.part, self.relays, self.lands = place, part, relays, lands
        self.half = part.shape[1] // 2

    def far(self):
        t, h = self.at, self.half
        self.go(0, self.part.at[t.yf, pl.ds(0, h)], self.relays.at[0], t.column(t.ym))
        self.go(1, self.part.at[t.yf, pl.ds(h, h)], self.relays.at[1], t.column(t.yp))

    def near(self):
        t, h = self.at, self.half
        low, high = pl.ds(0, h), pl.ds(h, h)
        self.go(2, self.part.at[t.ym, high], self.lands.at[0, high], t.column(t.ym))
        self.go(3, self.part.at[t.yp, low], self.lands.at[1, low], t.column(t.yp))

    def relay(self):
        t, h = self.at, self.half
        low, high = pl.ds(0, h), pl.ds(h, h)
        self.got(0)
        self.part[t.ym, low] = (
            self.part[t.ym, low].astype(F32) + self.relays[0].astype(F32)
        ).astype(BF16)
        self.go(4, self.part.at[t.ym, low], self.lands.at[0, low], t.column(t.ym))
        self.got(1)
        self.part[t.yp, high] = (
            self.part[t.yp, high].astype(F32) + self.relays[1].astype(F32)
        ).astype(BF16)
        self.go(5, self.part.at[t.yp, high], self.lands.at[1, high], t.column(t.yp))

    def finish(self):
        self.got(2, 3, 4, 5)
        return (
            self.part[self.at.y].astype(F32)
            + self.lands[0].astype(F32)
            + self.lands[1].astype(F32)
        )


class PlaneGather(Wire):
    def __init__(self, sems, place, full, half):
        super().__init__(sems)
        self.at, self.full, self.half = place, full, half

    def begin(self):
        t, own = self.at, self.full(self.at.me)
        self.go(0, own, own, t.plane(t.xp))
        self.go(1, own, own, t.plane(t.xm))
        self.go(2, own, own, t.plane(t.zo))

    def relay(self):
        t = self.at
        self.got(0)
        first = self.half(t.xm, 0)
        self.go(3, first, first, t.plane(t.xp))
        self.got(1)
        second = self.half(t.xp, 1)
        self.go(4, second, second, t.plane(t.xm))
        self.got(2)
        other = self.full(t.zo)
        self.go(5, other, other, t.plane(t.xp))
        self.go(6, other, other, t.plane(t.xm))

    def cross(self):
        t = self.at
        for k in (0, 1):
            self.got(3 + k)
            part = self.half(t.xf, k)
            self.go(7 + k, part, part, t.plane(t.zo))

    def finish(self):
        self.got(5, 6, 7, 8)


class PlaneReduce(Wire):
    def __init__(self, sems, place, full, half, land, half_land):
        super().__init__(sems)
        self.at, self.full, self.half = place, full, half
        self.land, self.half_land = land, half_land

    def add(self, ref, *more):
        total = ref[...].astype(F32)
        for other in more:
            total = total + other[...].astype(F32)
        ref[...] = total.astype(BF16)

    def far(self):
        t = self.at
        self.go(0, self.full(t.zxf), self.land(0), t.plane(t.zo))

    def sides(self):
        t = self.at
        self.go(1, self.full(t.zxm), self.land(1), t.plane(t.xm))
        self.go(2, self.full(t.zxp), self.land(2), t.plane(t.xp))

    def opposite(self):
        t = self.at
        self.got(0)
        self.add(self.full(t.xf), self.land(0))
        self.go(3, self.half(t.xf, 0), self.half_land(0), t.plane(t.xm))
        self.go(4, self.half(t.xf, 1), self.half_land(1), t.plane(t.xp))

    def across(self):
        t = self.at
        self.got(1, 2)
        self.add(self.full(t.zo), self.land(1), self.land(2))
        self.go(5, self.full(t.zo), self.land(3), t.plane(t.zo))

    def near(self):
        t = self.at
        self.got(3)
        self.add(self.half(t.xm, 0), self.half_land(0))
        self.go(6, self.full(t.xm), self.land(4), t.plane(t.xm))
        self.got(4)
        self.add(self.half(t.xp, 1), self.half_land(1))
        self.go(7, self.full(t.xp), self.land(5), t.plane(t.xp))

    def finish(self):
        self.got(5, 6, 7)
        total = self.full(self.at.me)[...].astype(F32)
        for k in (3, 4, 5):
            total = total + self.land(k)[...].astype(F32)
        return total


def pick(i, *values):
    out = values[-1]
    for k in range(len(values) - 2, -1, -1):
        out = jnp.where(i == k, values[k], out)
    return out


def local_copies(pairs, sems):
    copies = [
        pltpu.make_async_copy(src, dst, sems.at[i]) for i, (src, dst) in enumerate(pairs)
    ]
    for copy in copies:
        copy.start()
    return copies


QB = 128


def forward_block(kv, c, h, cols, qpad, top, total, acc):
    both = kv[c, :, h * 128 : (h + 1) * 128]
    scores = dot(both, qpad[h, cols, :], 1, 1)
    old = top[h, :, cols]
    new = jnp.maximum(old, jnp.max(scores, axis=0, keepdims=True))
    shrink = jnp.exp(old - new)
    expo = jnp.exp(scores - new)
    top[h, :, cols] = new
    total[h, :, cols] = total[h, :, cols] * shrink + jnp.sum(expo, axis=0, keepdims=True)
    acc[h, :, cols] = acc[h, :, cols] * shrink + dot(both, expo.astype(BF16), 0, 0)


def forward_chunk(kv, c, qpad, top, total, acc):
    for h in range(HEADS):
        for b in range(qpad.shape[1] // QB):
            forward_block(kv, c, h, slice(b * QB, (b + 1) * QB), qpad, top, total, acc)


def backward_chunk(kv, c, qpad, dopad, lse, delta, dqt, out):
    for h in range(HEADS):
        lanes = slice(h * 128, (h + 1) * 128)
        both, query, grad = kv[c, :, lanes], qpad[h], dopad[h]
        scores = dot(both, query, 1, 1)
        slopes = dot(both, grad, 1, 1)
        probs = jnp.exp(scores - lse[h])
        score_grads = (probs * (slopes - delta[h])).astype(BF16)
        out[c, :, lanes] = (
            dot(probs.astype(BF16), grad, 1, 0) + dot(score_grads, query, 1, 0)
        ).astype(BF16)
        dqt[h] += dot(both, score_grads, 0, 0)


HALO = 16
LANES = 128


def shifts(wide, length, taps):
    for low in range(8):
        moved = wide if low == 0 else pltpu.roll(wide, wide.shape[0] - low, 0)
        for offset in range(low, taps + 1, 8):
            if offset > 0:
                yield offset, moved[offset - low : offset - low + length]


class Edge(Wire):
    def __init__(self, sems, place, wide):
        super().__init__(sems)
        t, rows = place, wide.shape[0]
        self.first, self.last = t.seq == 0, t.seq == 31
        nothing = jnp.zeros((HALO, wide.shape[1]), BF16)

        @pl.when(self.first)
        def _():
            wide[0:HALO] = nothing

        @pl.when(self.last)
        def _():
            wide[rows - HALO :] = nothing

        self.up = pltpu.make_async_remote_copy(
            src_ref=wide.at[pl.ds(rows - 2 * HALO, HALO)],
            dst_ref=wide.at[pl.ds(0, HALO)],
            send_sem=sems.at[0, 0],
            recv_sem=sems.at[1, 0],
            device_id={"seq": jnp.minimum(t.seq + 1, 31)},
        )
        self.down = pltpu.make_async_remote_copy(
            src_ref=wide.at[pl.ds(HALO, HALO)],
            dst_ref=wide.at[pl.ds(rows - HALO, HALO)],
            send_sem=sems.at[0, 1],
            recv_sem=sems.at[1, 1],
            device_id={"seq": jnp.maximum(t.seq - 1, 0)},
        )

    def begin(self):
        @pl.when(jnp.logical_not(self.last))
        def _():
            self.up.start()

        @pl.when(jnp.logical_not(self.first))
        def _():
            self.down.start()

    def finish(self):
        @pl.when(jnp.logical_not(self.last))
        def _():
            self.up.wait_send()
            self.down.wait_recv()

        @pl.when(jnp.logical_not(self.first))
        def _():
            self.down.wait_send()
            self.up.wait_recv()


def whole_kernel(names, *refs):
    r = dict(zip(names, refs))
    (
        frames,
        w_qkv,
        w_out,
        gains_in,
        conv_kernel,
        conv_bias,
        out_grad,
        block_out,
        grad_input,
        grad_qkv,
        grad_out,
        kernel_sum,
        bias_sum,
        norms_sum,
        w_parts,
        hid,
        wq,
        wo,
        wo32,
        wo16,
        kv,
        qpad,
        lse,
        total,
        acc,
        att,
        part,
        relays,
        lands,
        mixed_keep,
        normed_keep,
        conv_wide,
        grad_wide,
        conv_back,
        mix,
        dopad,
        delta,
        dqt,
        dkv,
        kv_land,
        kv_half,
        proj,
        part2,
        relays2,
        lands2,
        w_part,
        w_core,
        w_land,
        w_half,
        w_hi,
        w_done,
        w_fin,
        o_part,
        o_core,
        o_land,
        o_half,
        o_hi,
        o_done,
        o_fin,
        s_send,
        s_seq,
        s_mine,
        s_dp,
        s_done,
        s_fin,
        spread_sems,
        hid_sems,
        wq_sems,
        wo_sems,
        gather_sems,
        sum_sems,
        conv_sems,
        grad_sems,
        mix_sems,
        kv_sems,
        red_sems,
        core_sems,
        w_sems,
        o_sems,
        hi_sems,
        w_fin_send,
        w_fin_recv,
        o_fin_send,
        o_fin_recv,
        s_sems,
        s_dp_sems,
        s_fin_sems,
    ) = (r[n] for n in names)
    t = Place()
    t.greet()
    rows, model = frames.shape
    many = GROUPS * rows
    width = HEADS * HD
    shard = w_qkv.shape[0]
    gain1, gain2 = gains_in[0:1, :], gains_in[1:2, :]

    for g in range(GROUPS):
        columns = [w_qkv[:, g * width : (g + 1) * width]]
        for h in range(HEADS):
            for kind in (1, 2):
                start = (kind * GROUPS + g) * width + h * HD
                columns.append(w_qkv[:, start : start + HD])
        w_parts[g] = jnp.concatenate(columns, axis=1)
    spread = Wire(spread_sems)
    for k, y in enumerate((t.yp, t.ym, t.yf)):
        spread.go(k, w_parts.at[y], wq.at[t.y, t.me], t.column(y))
    wq[t.y, t.me] = w_parts[t.y]
    share = width // PLANE
    wo[t.me] = jnp.concatenate(
        [w_out[...].astype(F32), jnp.zeros((wo.shape[1] - share, model), F32)], axis=0
    ).astype(BF16)

    inputs = frames[...].astype(F32)
    shifted, _, _ = layer_norm(inputs, gain1)
    hid[t.y] = shifted.astype(BF16)
    hid_net = ColumnGather(hid_sems, t, hid)
    hid_net.begin()
    spread.got(0, 1, 2)
    wq_net = PlaneGather(
        wq_sems, t, lambda p: wq.at[:, p], lambda p, i: wq.at[pl.ds(2 * i, 2), p]
    )
    wo_net = PlaneGather(
        wo_sems, t, lambda p: wo.at[p], lambda p, i: wo.at[p, pl.ds(16 * i, 16)]
    )
    wq_net.begin()
    hid_net.relay()
    wq_net.relay()
    wq_net.cross()
    wo_net.begin()
    hid_net.finish()
    wq_net.finish()

    hidden = hid[...].reshape(many, model)
    weights = wq[...].reshape(model, 3 * width)
    projected = dot(hidden, weights, 1, 0).astype(BF16)
    kv[t.me] = projected[:, width:]
    kv_net = PlaneGather(
        gather_sems,
        t,
        lambda p: kv.at[p],
        lambda p, i: kv.at[p, pl.ds(i * (many // 2), many // 2)],
    )
    kv_net.begin()
    zeros = jnp.zeros((many, HD), BF16)
    for h in range(HEADS):
        qpad[h] = jnp.concatenate(
            [projected[:, h * HD : (h + 1) * HD] * BF16(HD**-0.5), zeros], axis=1
        )
    lse[...] = jnp.full_like(lse, -jnp.inf)
    total[...] = jnp.zeros_like(total)
    acc[...] = jnp.zeros_like(acc)

    def attend(*chunks):
        if len(chunks) == 1:
            forward_chunk(kv, chunks[0], qpad, lse, total, acc)
            return

        def step(i, carry):
            forward_chunk(kv, pick(i, *chunks), qpad, lse, total, acc)
            return carry

        lax.fori_loop(0, len(chunks), step, 0)

    attend(t.me)
    kv_net.relay()
    wo_net.relay()
    attend(t.xm, t.xp, t.zo)
    kv_net.cross()
    wo_net.cross()
    attend(t.xf)
    wo_net.finish()
    for p in range(PLANE):
        wo32[p * share : (p + 1) * share, :] = wo[p, 0:share, :].astype(F32)
    wo16[...] = wo32[...].astype(BF16)
    kv_net.got(5, 6)
    kv_net.got(7, 8)

    def last(y):
        cols = pl.ds(pl.multiple_of(y * rows, rows), rows)

        def step(i, carry):
            c = pick(i, t.zxm, t.zxp, t.zxf)
            for h in range(HEADS):
                forward_block(kv, c, h, cols, qpad, lse, total, acc)
            return carry

        lax.fori_loop(0, 3, step, 0)
        blocks = []
        for h in range(HEADS):
            blocks.append((acc[h, HD : 2 * HD, cols] / total[h, :, cols]).T.astype(BF16))
            lse[h, :, cols] = lse[h, :, cols] + jnp.log(total[h, :, cols])
        here = jnp.concatenate(blocks, axis=1)
        att[cols, :] = here
        part[y] = dot(here, wo16[...], 1, 0).astype(BF16)

    sum_net = ColumnReduce(sum_sems, t, part, relays, lands)
    last(t.yf)
    sum_net.far()
    last(t.ym)
    last(t.yp)
    sum_net.near()
    last(t.y)
    sum_net.relay()
    mixed = (frames[...].astype(F32) + sum_net.finish()).astype(BF16)

    mixed32 = mixed.astype(F32)
    mixed_keep[...] = mixed32
    shifted, normed, inverse = layer_norm(mixed32, gain2)
    inside = slice(HALO, HALO + rows)
    conv_wide[inside] = shifted.astype(BF16)
    conv_edge = Edge(conv_sems, t, conv_wide)
    conv_edge.begin()
    normed_keep[...] = normed
    conv_edge.finish()
    taps = conv_kernel.shape[0]

    def lanes_of(b):
        return pl.ds(pl.multiple_of(b * LANES, LANES), LANES)

    def convolve(b, carry):
        lanes = lanes_of(b)
        pre = jnp.zeros((rows, LANES), F32) + conv_bias[:, lanes]
        for offset, moved in shifts(conv_wide[:, lanes].astype(F32), rows, taps):
            pre = pre + moved * conv_kernel[offset - 1 : offset, lanes]
        sigma = 1.0 / (1.0 + jnp.exp(-pre))
        block_out[:, lanes] = (mixed_keep[:, lanes] + pre * sigma).astype(BF16)
        grad_wide[inside, lanes] = (
            out_grad[:, lanes].astype(F32) * sigma * (1.0 + pre * (1.0 - sigma))
        ).astype(BF16)
        return carry

    blocks = model // LANES
    lax.fori_loop(0, blocks, convolve, 0)
    grad_edge = Edge(grad_sems, t, grad_wide)
    grad_edge.begin()
    grad_edge.finish()

    def convolve_back(b, carry):
        lanes = lanes_of(b)
        grad = jnp.zeros((rows, LANES), F32)
        for offset, moved in shifts(grad_wide[:, lanes].astype(F32), rows, taps):
            grad = grad + moved * conv_kernel[taps - offset : taps - offset + 1, lanes]
        conv_back[:, lanes] = grad
        return carry

    lax.fori_loop(0, blocks, convolve_back, 0)
    norm_grad, gain2_grad = norm_back(conv_back[...], normed_keep[...], inverse, gain2)
    gain2_grad = gain2_grad[None]
    mix[t.y] = (out_grad[...].astype(F32) + norm_grad).astype(BF16)
    mix_net = ColumnGather(mix_sems, t, mix)
    mix_net.begin()

    def kernel_grads(b, carry):
        lanes = lanes_of(b)
        grad = grad_wide[inside, lanes].astype(F32)
        for offset, moved in shifts(conv_wide[:, lanes].astype(F32), rows, taps):
            s_send[offset - 1, :, lanes] = jnp.sum(grad * moved, axis=0, keepdims=True)
        s_send[taps, :, lanes] = jnp.sum(grad, axis=0, keepdims=True)
        return carry

    lax.fori_loop(0, blocks, kernel_grads, 0)
    mix_net.relay()
    mix_net.finish()

    mixed = mix[...].reshape(many, model)
    grads = dot(mixed, wo16[...], 1, 1).astype(BF16)
    for h in range(HEADS):
        lanes = slice(h * HD, (h + 1) * HD)
        mine = grads[:, lanes]
        dopad[h] = jnp.concatenate([zeros, mine], axis=1)
        delta[h] = jnp.sum(
            (att[:, lanes].astype(F32) * mine.astype(F32)).T, axis=0, keepdims=True
        )
    dqt[...] = jnp.zeros_like(dqt)

    def backward(*chunks):
        def step(i, carry):
            backward_chunk(kv, pick(i, *chunks), qpad, dopad, lse, delta, dqt, dkv)
            return carry

        if len(chunks) == 1:
            step(0, 0)
        else:
            lax.fori_loop(0, len(chunks), step, 0)

    half = many // 2
    net = PlaneReduce(
        kv_sems,
        t,
        lambda p: dkv.at[p],
        lambda p, i: dkv.at[p, pl.ds(i * half, half)],
        lambda k: kv_land.at[k],
        lambda k: kv_half.at[k],
    )
    backward(t.zxf)
    net.far()
    backward(t.zxm, t.zxp)
    net.sides()
    backward(t.xf)
    net.opposite()
    backward(t.zo)
    net.across()
    backward(t.xm, t.xp)
    net.near()
    backward(t.me)
    for h in range(HEADS):
        proj[:, h * HD : (h + 1) * HD] = (dqt[h, 0:HD, :] * HD**-0.5).T.astype(BF16)

    out_terms = dot(att[...], mixed, 0, 0)
    quarter = o_part.shape[2]
    wide = model // 2
    for c in range(2):
        for p in range(PLANE):
            for i in range(quarter):
                piece = o_part.at[c, p, i]
                if i * 8 < share:
                    start = p * share + i * 8
                    piece[...] = out_terms[
                        start : start + 8, c * wide : (c + 1) * wide
                    ].astype(BF16)
                else:
                    piece[...] = jnp.zeros(piece.shape, BF16)
    order = (t.zxf, t.zxm, t.zxp, t.xf, t.zo, t.xm, t.xp, t.me)
    buddy = {"dp": t.hi * 2 + 1 - t.core}
    pair = Wire(core_sems)
    for k, p in enumerate(order):
        pair.go(k, o_part.at[1 - t.core, p], o_core.at[p], buddy)
    proj[:, width:] = net.finish().astype(BF16)

    weights = wq[...].reshape(model, 3 * width)

    def product(y):
        here = proj[pl.ds(pl.multiple_of(y * rows, rows), rows), :]
        part2[y] = dot(here, weights, 1, 1).astype(BF16)

    red = ColumnReduce(red_sems, t, part2, relays2, lands2)
    product(t.yf)
    red.far()
    hidden = hid[...].reshape(many, model)
    half_rows = w_part.shape[3]
    w_terms = dot(hidden, proj[...], 0, 0).reshape(
        GROUPS, PLANE, 2, half_rows, 3 * width
    )
    for c in range(2):
        w_part[c] = w_terms[:, :, c].astype(BF16)
    for k, p in enumerate(order):
        pair.go(8 + k, w_part.at[1 - t.core, :, p], w_core.at[:, p], buddy)
    w_mine, o_mine = w_part.at[t.core], o_part.at[t.core]
    o_net = PlaneReduce(
        o_sems,
        t,
        lambda p: o_mine.at[p],
        lambda p, i: o_mine.at[p, pl.ds(2 * i, 2)],
        lambda k: o_land.at[k],
        lambda k: o_half.at[k],
    )
    w_net = PlaneReduce(
        w_sems,
        t,
        lambda p: w_mine.at[:, p],
        lambda p, i: w_mine.at[pl.ds(2 * i, 2), p],
        lambda k: w_land.at[k],
        lambda k: w_half.at[k],
    )

    def join(first, last):
        for k in range(first, last):
            p = order[k]
            pair.got(k, 8 + k)
            o_net.add(o_mine.at[p], o_core.at[p])
            w_net.add(w_mine.at[:, p], w_core.at[:, p])

    product(t.ym)
    product(t.yp)
    product(t.y)
    red.near()
    red.relay()
    join(0, 1)
    w_net.far()
    o_net.far()
    join(1, 3)
    w_net.sides()
    o_net.sides()
    join(3, 8)
    w_net.opposite()
    o_net.opposite()
    w_net.across()
    o_net.across()
    w_net.near()
    o_net.near()

    grad_hidden = red.finish()
    _, normed, inverse = layer_norm(frames[...].astype(F32), gain1)
    norm_grad, gain_sum = norm_back(grad_hidden, normed, inverse, gain1)
    grad_input[...] = (mix[t.y].astype(F32) + norm_grad).astype(BF16)
    gains = (gain_sum[None], gain2_grad)
    count = s_send.shape[0]
    for r in range(count):
        if r < 2 * (model // 128):
            row, col = divmod(r, model // 128)
            s_send[r, :, model:] = gains[row][:, col * 128 : (col + 1) * 128]
        else:
            s_send[r, :, model:] = jnp.zeros((1, 128), F32)
    s_net = Wire(s_sems)
    s_seq[t.seq] = s_send[t.seq]
    for k in range(1, count):
        r = (t.seq + k) % count
        s_net.go(k - 1, s_send.at[r], s_seq.at[t.seq], {"seq": r})

    o_total, w_total = o_net.finish(), w_net.finish()
    o_mine[t.me] = o_total.astype(BF16)
    w_mine[:, t.me] = w_total.astype(BF16)
    hi_net = Wire(hi_sems)
    for k in range(1, 4):
        j = (t.hi + k) % 4
        there = {"dp": j * 2 + t.core}
        hi_net.go(k - 1, w_mine.at[j, t.me], w_hi.at[k - 1], there)
        hi_net.go(2 + k, o_mine.at[t.me, j], o_hi.at[k - 1], there)

    s_net.got(*range(count - 1))
    s_mine[...] = jnp.sum(s_seq[...], axis=0)
    s_dp[t.dp] = s_mine[...]
    s_dp_net = Wire(s_dp_sems)
    for k in range(1, 8):
        s_dp_net.go(k - 1, s_mine, s_dp.at[t.dp], {"dp": (t.dp + k) % 8})

    hi_net.got(*range(6))
    w_out_block = w_mine[t.hi, t.me].astype(F32)
    o_out_block = o_mine[t.me, t.hi].astype(F32)
    for k in range(3):
        w_out_block = w_out_block + w_hi[k].astype(F32)
        o_out_block = o_out_block + o_hi[k].astype(F32)
    w_done[...] = w_out_block.astype(BF16)
    o_done[...] = o_out_block.astype(BF16)
    finals = []
    for k in range(1, 8):
        d = (t.dp + k) % 8
        for src, dst, send, recv, y in (
            (w_done, w_fin.at[t.y, t.core], w_fin_send.at[k], w_fin_recv.at[t.y, t.core], t.hi),
            (o_done, o_fin.at[t.hi, t.core], o_fin_send.at[k], o_fin_recv.at[t.hi, t.core], t.y),
        ):
            copy = pltpu.make_async_remote_copy(
                src_ref=src, dst_ref=dst, send_sem=send, recv_sem=recv, device_id=t.holder(y, d)
            )
            copy.start()
            finals.append(copy)
    o_own = pltpu.make_async_copy(
        o_done, o_fin.at[t.hi, t.core], o_fin_recv.at[t.hi, t.core]
    )
    o_own.start()
    w_own = pltpu.make_async_copy(w_done, w_fin.at[t.y, t.core], w_fin_recv.at[t.y, t.core])
    w_away = pltpu.make_async_remote_copy(
        src_ref=w_done,
        dst_ref=w_fin.at[t.y, t.core],
        send_sem=w_fin_send.at[0],
        recv_sem=w_fin_recv.at[t.y, t.core],
        device_id=t.holder(t.hi, t.dp),
    )

    @pl.when(t.hi == t.y)
    def _():
        w_own.start()

    @pl.when(t.hi != t.y)
    def _():
        w_away.start()

    s_dp_net.got(*range(7))
    summed = s_dp[0]
    for d in range(1, 8):
        summed = summed + s_dp[d]
    s_done[...] = summed
    s_fin[t.seq] = summed
    s_fin_net = Wire(s_fin_sems)
    for k in range(1, count):
        s_fin_net.go(k - 1, s_done, s_fin.at[t.seq], {"seq": (t.seq + k) % count})

    for i in range(4):
        for c in range(2):
            pltpu.make_async_copy(w_done, w_fin.at[i, c], w_fin_recv.at[i, c]).wait()
            pltpu.make_async_copy(o_done, o_fin.at[i, c], o_fin_recv.at[i, c]).wait()
    pieces = [w_fin[y].astype(F32).reshape(2 * half_rows, 3 * width) for y in range(GROUPS)]
    columns = [piece[:, :width] for piece in pieces]
    for kind in range(2):
        for piece in pieces:
            for h in range(HEADS):
                start = width + (2 * h + kind) * HD
                columns.append(piece[:, start : start + HD])
    grad_qkv[...] = jnp.concatenate(columns, axis=1).astype(BF16)
    sides = [
        o_fin[0 : share // 8, c].astype(F32).reshape(share, wide) for c in range(2)
    ]
    grad_out[...] = jnp.concatenate(sides, axis=1).astype(BF16)
    s_fin_net.got(*range(count - 1))
    for r in range(count):
        row = s_fin[r]
        if r < taps:
            kernel_sum[r : r + 1, :] = row[:, :model]
        else:
            bias_sum[...] = row[:, :model]
        if r < 2 * (model // 128):
            i, col = divmod(r, model // 128)
            norms_sum[i : i + 1, col * 128 : (col + 1) * 128] = row[:, model:]
    for copy in finals:
        copy.wait_send()

    @pl.when(t.hi != t.y)
    def _():
        w_away.wait_send()

    for wire in (spread, hid_net, wq_net, wo_net, kv_net, sum_net, mix_net, net, pair, o_net, red, w_net, hi_net, s_net, s_dp_net, s_fin_net):
        wire.done()


def bf16(*shape):
    return pltpu.VMEM(shape, BF16)


def f32(*shape):
    return pltpu.VMEM(shape, F32)


def dma(*shape):
    return pltpu.SemaphoreType.DMA(shape)


def whole(frames, w_qkv, w_out, gains, conv_kernel, conv_bias, out_grad):
    rows, model = frames.shape
    shard = w_qkv.shape[0]
    many = GROUPS * rows
    width = HEADS * HD
    half = shard // 2
    padded = 32
    count = conv_kernel.shape[0] + 1
    like = jax.ShapeDtypeStruct
    ins = dict(
        frames=frames,
        w_qkv=w_qkv,
        w_out=w_out,
        gains_in=gains,
        conv_kernel=conv_kernel,
        conv_bias=conv_bias,
        out_grad=out_grad,
    )
    outs = dict(
        block_out=like((rows, model), BF16),
        grad_input=like((rows, model), BF16),
        grad_qkv=like(w_qkv.shape, BF16),
        grad_out=like(w_out.shape, BF16),
        kernel_sum=like((count - 1, model), F32),
        bias_sum=like((1, model), F32),
        norms_sum=like((2, model), F32),
    )
    scratch = dict(
        w_parts=bf16(GROUPS, shard, 3 * width),
        hid=bf16(GROUPS, rows, model),
        wq=bf16(GROUPS, PLANE, shard, 3 * width),
        wo=bf16(PLANE, padded, model),
        wo32=f32(width, model),
        wo16=bf16(width, model),
        kv=bf16(PLANE, many, 2 * width),
        qpad=bf16(HEADS, many, 2 * HD),
        lse=f32(HEADS, 1, many),
        total=f32(HEADS, 1, many),
        acc=f32(HEADS, 2 * HD, many),
        att=bf16(many, width),
        part=bf16(GROUPS, rows, model),
        relays=bf16(2, rows // 2, model),
        lands=bf16(2, rows, model),
        mixed_keep=f32(rows, model),
        normed_keep=f32(rows, model),
        conv_wide=bf16(rows + 2 * HALO, model),
        grad_wide=bf16(rows + 2 * HALO, model),
        conv_back=f32(rows, model),
        mix=bf16(GROUPS, rows, model),
        dopad=bf16(HEADS, many, 2 * HD),
        delta=f32(HEADS, 1, many),
        dqt=f32(HEADS, 2 * HD, many),
        dkv=bf16(PLANE, many, 2 * width),
        kv_land=bf16(6, many, 2 * width),
        kv_half=bf16(2, many // 2, 2 * width),
        proj=bf16(many, 3 * width),
        part2=bf16(GROUPS, rows, model),
        relays2=bf16(2, rows // 2, model),
        lands2=bf16(2, rows, model),
        w_part=bf16(2, GROUPS, PLANE, half, 3 * width),
        w_core=bf16(GROUPS, PLANE, half, 3 * width),
        w_land=bf16(6, GROUPS, half, 3 * width),
        w_half=bf16(2, GROUPS // 2, half, 3 * width),
        w_hi=bf16(3, half, 3 * width),
        w_done=bf16(half, 3 * width),
        w_fin=bf16(GROUPS, 2, half, 3 * width),
        o_part=bf16(2, PLANE, 4, 8, model // 2),
        o_core=bf16(PLANE, 4, 8, model // 2),
        o_land=bf16(6, 4, 8, model // 2),
        o_half=bf16(2, 2, 8, model // 2),
        o_hi=bf16(3, 8, model // 2),
        o_done=bf16(8, model // 2),
        o_fin=bf16(4, 2, 8, model // 2),
        s_send=f32(count, 1, model + LANES),
        s_seq=f32(count, 1, model + LANES),
        s_mine=f32(1, model + LANES),
        s_dp=f32(8, 1, model + LANES),
        s_done=f32(1, model + LANES),
        s_fin=f32(count, 1, model + LANES),
        spread_sems=wire_sems(3),
        hid_sems=wire_sems(4),
        wq_sems=wire_sems(9),
        wo_sems=wire_sems(9),
        gather_sems=wire_sems(9),
        sum_sems=wire_sems(6),
        conv_sems=wire_sems(2),
        grad_sems=wire_sems(2),
        mix_sems=wire_sems(4),
        kv_sems=wire_sems(8),
        red_sems=wire_sems(6),
        core_sems=wire_sems(16),
        w_sems=wire_sems(8),
        o_sems=wire_sems(8),
        hi_sems=wire_sems(6),
        w_fin_send=dma(8),
        w_fin_recv=dma(4, 2),
        o_fin_send=dma(8),
        o_fin_recv=dma(4, 2),
        s_sems=wire_sems(count - 1),
        s_dp_sems=wire_sems(7),
        s_fin_sems=wire_sems(count - 1),
    )
    vmem = pl.BlockSpec(memory_space=pltpu.VMEM)
    names = [*ins, *outs, *scratch]
    return pl.pallas_call(
        functools.partial(whole_kernel, names),
        out_shape=list(outs.values()),
        in_specs=[vmem] * len(ins),
        out_specs=[vmem] * len(outs),
        scratch_shapes=list(scratch.values()),
        compiler_params=pltpu.CompilerParams(
            collective_id=0, has_side_effects=True, vmem_limit_bytes=62 * 2**20
        ),
        name="whole",
    )(*ins.values())


def hand_on_kernel(*refs):
    half = len(refs) // 2
    for src, dst in zip(refs[:half], refs[half:]):
        dst[...] = src[...].reshape(dst.shape)


def hand_on(*arrays):
    vmem = pl.BlockSpec(memory_space=pltpu.VMEM)
    return pl.pallas_call(
        hand_on_kernel,
        out_shape=[jax.ShapeDtypeStruct(a.shape, a.dtype) for a in arrays],
        in_specs=[vmem] * len(arrays),
        out_specs=[vmem] * len(arrays),
        name="hand_on",
    )(*arrays)


def local(frames, w_qkv, w_out, norm_gains, conv_kernel, conv_bias, out_grad):
    block_out, grad_input, grad_qkv, grad_out, kernel_sum, bias_sum, norms_sum = hand_on(
        *whole(
            frames[0], w_qkv, w_out, norm_gains, conv_kernel, conv_bias[None], out_grad[0]
        )
    )
    return (
        block_out[None],
        grad_input[None],
        grad_qkv,
        grad_out,
        norms_sum,
        kernel_sum,
        bias_sum[0],
    )


def solution(mesh):
    in_specs = (
        P("dp", "seq", None),
        P("seq", None),
        P("seq", None),
        P(),
        P(),
        P(),
        P("dp", "seq", None),
    )
    out_specs = (
        P("dp", "seq", None),
        P("dp", "seq", None),
        P("seq", None),
        P("seq", None),
        P(),
        P(),
        P(),
    )
    return jax.shard_map(local, mesh=mesh, in_specs=in_specs, out_specs=out_specs, check_vma=False)
```

```python
import functools

import jax
import jax.numpy as jnp
from jax import lax
from jax.experimental import pallas as pl
from jax.experimental.pallas import tpu as pltpu
from jax.sharding import PartitionSpec as P

EPS = 1e-05
GROUPS = 4
PLANE = 8
HEADS = 3
HD = 64
F32 = jnp.float32
BF16 = jnp.bfloat16


def layer_norm(values, gain):
    center = values - jnp.mean(values, axis=-1, keepdims=True)
    spread = jnp.mean(center * center, axis=-1, keepdims=True)
    inverse = lax.rsqrt(spread + EPS)
    normed = center * inverse
    return (normed * gain, normed, inverse)


def norm_back(grad, normed, inverse, gain):
    scaled = grad * gain
    inner = (
        scaled
        - jnp.mean(scaled, axis=-1, keepdims=True)
        - normed * jnp.mean(scaled * normed, axis=-1, keepdims=True)
    )
    return (inverse * inner, jnp.sum(grad * normed, axis=0))


def dot(a, b, ca, cb):
    return lax.dot_general(a, b, (((ca,), (cb,)), ((), ())), preferred_element_type=F32)


class Place:
    def __init__(self):
        seq = lax.axis_index("seq")
        y, z, x = seq // 8, (seq // 4) % 2, seq % 4
        right, left, far, other = (x + 1) % 4, (x + 3) % 4, (x + 2) % 4, 1 - z
        self.y, self.yp, self.ym, self.yf = y, (y + 1) % 4, (y + 3) % 4, (y + 2) % 4
        self.me = z * 4 + x
        self.xp, self.xm, self.xf = z * 4 + right, z * 4 + left, z * 4 + far
        self.zo = other * 4 + x
        self.zxp, self.zxm, self.zxf = other * 4 + right, other * 4 + left, other * 4 + far

        self.seq, self.dp = seq, lax.axis_index("dp")
        self.core, self.hi = self.dp % 2, self.dp // 2

    def plane(self, p):
        return {"seq": self.y * 8 + p}

    def holder(self, y, dp):
        return {"seq": y * 8 + self.me, "dp": dp}

    def greet(self):
        near = [{"seq": (self.seq + i) % 32} for i in range(1, 32)]
        near += [
            self.holder((self.y + i) % 4, (self.dp + j) % 8) for i in range(4) for j in range(1, 8)
        ]
        for device in near:
            pl.semaphore_signal(pltpu.get_barrier_semaphore(), inc=1, device_id=device)
        return len(near)

    def column(self, y):
        return {"seq": y * 8 + self.me}


class Wire:
    def __init__(self, sems):
        self.sems, self.sent = sems, {}

    def go(self, k, src, dst, device):
        copy = pltpu.make_async_remote_copy(
            src_ref=src,
            dst_ref=dst,
            send_sem=self.sems.at[0, k],
            recv_sem=self.sems.at[1, k],
            device_id=device,
        )
        copy.start()
        self.sent[k] = copy

    def got(self, *ks):
        for k in ks:
            self.sent[k].wait_recv()

    def done(self):
        for copy in self.sent.values():
            copy.wait_send()


def wire_sems(count):
    return pltpu.SemaphoreType.DMA((2, count))


class ColumnGather(Wire):
    def __init__(self, sems, place, buf):
        super().__init__(sems)
        self.at, self.buf = place, buf
        self.half = buf.shape[1] // 2

    def begin(self):
        t, own = self.at, self.buf.at[self.at.y]
        self.go(0, own, own, t.column(t.yp))
        self.go(1, own, own, t.column(t.ym))

    def relay(self):
        t, h = self.at, self.half
        self.got(0)
        first = self.buf.at[t.ym, pl.ds(0, h)]
        self.go(2, first, first, t.column(t.yp))
        self.got(1)
        second = self.buf.at[t.yp, pl.ds(h, h)]
        self.go(3, second, second, t.column(t.ym))

    def finish(self):
        self.got(2, 3)


class ColumnReduce(Wire):
    def __init__(self, sems, place, part, relays, lands):
        super().__init__(sems)
        self.at, self.part, self.relays, self.lands = place, part, relays, lands
        self.half = part.shape[1] // 2

    def far(self):
        t, h = self.at, self.half
        self.go(0, self.part.at[t.yf, pl.ds(0, h)], self.relays.at[0], t.column(t.ym))
        self.go(1, self.part.at[t.yf, pl.ds(h, h)], self.relays.at[1], t.column(t.yp))

    def near(self):
        t, h = self.at, self.half
        low, high = pl.ds(0, h), pl.ds(h, h)
        self.go(2, self.part.at[t.ym, high], self.lands.at[0, high], t.column(t.ym))
        self.go(3, self.part.at[t.yp, low], self.lands.at[1, low], t.column(t.yp))

    def relay(self):
        t, h = self.at, self.half
        low, high = pl.ds(0, h), pl.ds(h, h)
        self.got(0)
        self.part[t.ym, low] = (
            self.part[t.ym, low].astype(F32) + self.relays[0].astype(F32)
        ).astype(BF16)
        self.go(4, self.part.at[t.ym, low], self.lands.at[0, low], t.column(t.ym))
        self.got(1)
        self.part[t.yp, high] = (
            self.part[t.yp, high].astype(F32) + self.relays[1].astype(F32)
        ).astype(BF16)
        self.go(5, self.part.at[t.yp, high], self.lands.at[1, high], t.column(t.yp))

    def finish(self):
        self.got(2, 3, 4, 5)
        return (
            self.part[self.at.y].astype(F32)
            + self.lands[0].astype(F32)
            + self.lands[1].astype(F32)
        )


class PlaneGather(Wire):
    def __init__(self, sems, place, full, half):
        super().__init__(sems)
        self.at, self.full, self.half = place, full, half

    def begin(self):
        t, own = self.at, self.full(self.at.me)
        self.go(0, own, own, t.plane(t.xp))
        self.go(1, own, own, t.plane(t.xm))
        self.go(2, own, own, t.plane(t.zo))

    def relay(self):
        t = self.at
        self.got(0)
        first = self.half(t.xm, 0)
        self.go(3, first, first, t.plane(t.xp))
        self.got(1)
        second = self.half(t.xp, 1)
        self.go(4, second, second, t.plane(t.xm))
        self.got(2)
        other = self.full(t.zo)
        self.go(5, other, other, t.plane(t.xp))
        self.go(6, other, other, t.plane(t.xm))

    def cross(self):
        t = self.at
        for k in (0, 1):
            self.got(3 + k)
            part = self.half(t.xf, k)
            self.go(7 + k, part, part, t.plane(t.zo))

    def finish(self):
        self.got(5, 6, 7, 8)


class PlaneReduce(Wire):
    def __init__(self, sems, place, full, half, land, half_land):
        super().__init__(sems)
        self.at, self.full, self.half = place, full, half
        self.land, self.half_land = land, half_land

    def add(self, ref, *more):
        total = ref[...].astype(F32)
        for other in more:
            total = total + other[...].astype(F32)
        ref[...] = total.astype(BF16)

    def far(self):
        t = self.at
        self.go(0, self.full(t.zxf), self.land(0), t.plane(t.zo))

    def sides(self):
        t = self.at
        self.go(1, self.full(t.zxm), self.land(1), t.plane(t.xm))
        self.go(2, self.full(t.zxp), self.land(2), t.plane(t.xp))

    def opposite(self):
        t = self.at
        self.got(0)
        self.add(self.full(t.xf), self.land(0))
        self.go(3, self.half(t.xf, 0), self.half_land(0), t.plane(t.xm))
        self.go(4, self.half(t.xf, 1), self.half_land(1), t.plane(t.xp))

    def across(self):
        t = self.at
        self.got(1, 2)
        self.add(self.full(t.zo), self.land(1), self.land(2))
        self.go(5, self.full(t.zo), self.land(3), t.plane(t.zo))

    def near(self):
        t = self.at
        self.got(3)
        self.add(self.half(t.xm, 0), self.half_land(0))
        self.go(6, self.full(t.xm), self.land(4), t.plane(t.xm))
        self.got(4)
        self.add(self.half(t.xp, 1), self.half_land(1))
        self.go(7, self.full(t.xp), self.land(5), t.plane(t.xp))

    def finish(self):
        self.got(5, 6, 7)
        total = self.full(self.at.me)[...].astype(F32)
        for k in (3, 4, 5):
            total = total + self.land(k)[...].astype(F32)
        return total


def pick(i, *values):
    out = values[-1]
    for k in range(len(values) - 2, -1, -1):
        out = jnp.where(i == k, values[k], out)
    return out


def local_copies(pairs, sems):
    copies = [
        pltpu.make_async_copy(src, dst, sems.at[i]) for i, (src, dst) in enumerate(pairs)
    ]
    for copy in copies:
        copy.start()
    return copies


QB = 128


def forward_block(kv, c, h, cols, qpad, top, total, acc):
    both = kv[c, :, h * 128 : (h + 1) * 128]
    scores = dot(both, qpad[h, cols, :], 1, 1)
    old = top[h, :, cols]
    new = jnp.maximum(old, jnp.max(scores, axis=0, keepdims=True))
    shrink = jnp.exp(old - new)
    expo = jnp.exp(scores - new)
    top[h, :, cols] = new
    total[h, :, cols] = total[h, :, cols] * shrink + jnp.sum(expo, axis=0, keepdims=True)
    acc[h, :, cols] = acc[h, :, cols] * shrink + dot(both, expo.astype(BF16), 0, 0)


def forward_chunk(kv, c, qpad, top, total, acc):
    for h in range(HEADS):
        for b in range(qpad.shape[1] // QB):
            forward_block(kv, c, h, slice(b * QB, (b + 1) * QB), qpad, top, total, acc)


def prob_chunk(kv, c, qpad, lse, probs):
    for h in range(HEADS):
        scores = dot(kv[c, :, h * 128 : (h + 1) * 128], qpad[h], 1, 1)
        probs[c, h] = jnp.exp(scores - lse[h]).astype(BF16)


def backward_chunk(kv, c, qpad, dopad, probs, delta, dqt, out):
    for h in range(HEADS):
        lanes = slice(h * 128, (h + 1) * 128)
        both, query, grad = kv[c, :, lanes], qpad[h], dopad[h]
        slopes = dot(both, grad, 1, 1)
        prob = probs[c, h]
        score_grads = (prob.astype(F32) * (slopes - delta[h])).astype(BF16)
        out[c, :, lanes] = (
            dot(prob, grad, 1, 0) + dot(score_grads, query, 1, 0)
        ).astype(BF16)
        dqt[h] += dot(both, score_grads, 0, 0)


HALO = 16
LANES = 128


def shifts(wide, length, taps):
    for low in range(8):
        moved = wide if low == 0 else pltpu.roll(wide, wide.shape[0] - low, 0)
        for offset in range(low, taps + 1, 8):
            if offset > 0:
                yield offset, moved[offset - low : offset - low + length]


class Edge(Wire):
    def __init__(self, sems, place, wide):
        super().__init__(sems)
        t, rows = place, wide.shape[0]
        self.first, self.last = t.seq == 0, t.seq == 31
        nothing = jnp.zeros((HALO, wide.shape[1]), BF16)

        @pl.when(self.first)
        def _():
            wide[0:HALO] = nothing

        @pl.when(self.last)
        def _():
            wide[rows - HALO :] = nothing

        self.up = pltpu.make_async_remote_copy(
            src_ref=wide.at[pl.ds(rows - 2 * HALO, HALO)],
            dst_ref=wide.at[pl.ds(0, HALO)],
            send_sem=sems.at[0, 0],
            recv_sem=sems.at[1, 0],
            device_id={"seq": jnp.minimum(t.seq + 1, 31)},
        )
        self.down = pltpu.make_async_remote_copy(
            src_ref=wide.at[pl.ds(HALO, HALO)],
            dst_ref=wide.at[pl.ds(rows - HALO, HALO)],
            send_sem=sems.at[0, 1],
            recv_sem=sems.at[1, 1],
            device_id={"seq": jnp.maximum(t.seq - 1, 0)},
        )

    def begin(self):
        @pl.when(jnp.logical_not(self.last))
        def _():
            self.up.start()

        @pl.when(jnp.logical_not(self.first))
        def _():
            self.down.start()

    def finish(self):
        @pl.when(jnp.logical_not(self.last))
        def _():
            self.up.wait_send()
            self.down.wait_recv()

        @pl.when(jnp.logical_not(self.first))
        def _():
            self.down.wait_send()
            self.up.wait_recv()


def whole_kernel(names, *refs):
    r = dict(zip(names, refs))
    (
        frames,
        w_qkv,
        w_out,
        gains_in,
        conv_kernel,
        conv_bias,
        out_grad,
        block_out,
        grad_input,
        grad_qkv,
        grad_out,
        kernel_sum,
        bias_sum,
        norms_sum,
        w_parts,
        hid,
        wq,
        wo,
        wo32,
        wo16,
        kv,
        qpad,
        lse,
        total,
        acc,
        att,
        hid_turned,
        probs,
        part,
        relays,
        lands,
        mixed_keep,
        normed_keep,
        conv_wide,
        grad_wide,
        conv_back,
        mix,
        dopad,
        delta,
        dqt,
        dkv,
        kv_land,
        kv_half,
        proj,
        part2,
        relays2,
        lands2,
        w_part,
        w_core,
        w_land,
        w_half,
        w_hi,
        w_done,
        w_fin,
        o_part,
        o_core,
        o_land,
        o_half,
        o_hi,
        o_done,
        o_fin,
        s_send,
        s_seq,
        s_mine,
        s_dp,
        s_done,
        s_fin,
        spread_sems,
        hid_sems,
        wq_sems,
        wo_sems,
        gather_sems,
        sum_sems,
        conv_sems,
        grad_sems,
        mix_sems,
        kv_sems,
        red_sems,
        core_sems,
        w_sems,
        o_sems,
        hi_sems,
        w_fin_send,
        w_fin_recv,
        o_fin_send,
        o_fin_recv,
        s_sems,
        s_dp_sems,
        s_fin_sems,
    ) = (r[n] for n in names)
    t = Place()
    greeted = t.greet()
    rows, model = frames.shape
    many = GROUPS * rows
    width = HEADS * HD
    shard = w_qkv.shape[0]
    gain1, gain2 = gains_in[0:1, :], gains_in[1:2, :]

    for g in range(GROUPS):
        columns = [w_qkv[:, g * width : (g + 1) * width]]
        for h in range(HEADS):
            for kind in (1, 2):
                start = (kind * GROUPS + g) * width + h * HD
                columns.append(w_qkv[:, start : start + HD])
        w_parts[g] = jnp.concatenate(columns, axis=1)
    inputs = frames[...].astype(F32)
    shifted, _, _ = layer_norm(inputs, gain1)
    hid[t.y] = shifted.astype(BF16)
    pl.semaphore_wait(pltpu.get_barrier_semaphore(), greeted)
    hid_net = ColumnGather(hid_sems, t, hid)
    hid_net.begin()
    spread = Wire(spread_sems)
    for k, y in enumerate((t.yp, t.ym, t.yf)):
        spread.go(k, w_parts.at[y], wq.at[t.y, t.me], t.column(y))
    wq[t.y, t.me] = w_parts[t.y]
    share = width // PLANE
    wo[t.me] = jnp.concatenate(
        [w_out[...].astype(F32), jnp.zeros((wo.shape[1] - share, model), F32)], axis=0
    ).astype(BF16)

    spread.got(0, 1, 2)
    wq_net = PlaneGather(
        wq_sems, t, lambda p: wq.at[:, p], lambda p, i: wq.at[pl.ds(2 * i, 2), p]
    )
    wo_net = PlaneGather(
        wo_sems, t, lambda p: wo.at[p], lambda p, i: wo.at[p, pl.ds(16 * i, 16)]
    )
    wq_net.begin()
    hid_net.relay()
    wq_net.relay()
    wq_net.cross()
    wo_net.begin()
    hid_net.finish()
    for y in range(GROUPS):
        turned = hid[y].T.reshape(GROUPS, PLANE, shard, rows)
        hid_turned[:, :, :, y * rows : (y + 1) * rows] = turned
    wq_net.finish()

    hidden = hid[...].reshape(many, model)
    weights = wq[...].reshape(model, 3 * width)
    projected = dot(hidden, weights, 1, 0).astype(BF16)
    kv[t.me] = projected[:, width:]
    kv_net = PlaneGather(
        gather_sems,
        t,
        lambda p: kv.at[p],
        lambda p, i: kv.at[p, pl.ds(i * (many // 2), many // 2)],
    )
    kv_net.begin()
    zeros = jnp.zeros((many, HD), BF16)
    for h in range(HEADS):
        qpad[h] = jnp.concatenate(
            [projected[:, h * HD : (h + 1) * HD] * BF16(HD**-0.5), zeros], axis=1
        )
    lse[...] = jnp.full_like(lse, -jnp.inf)
    total[...] = jnp.zeros_like(total)
    acc[...] = jnp.zeros_like(acc)

    def attend(*chunks):
        if len(chunks) == 1:
            forward_chunk(kv, chunks[0], qpad, lse, total, acc)
            return

        def step(i, carry):
            forward_chunk(kv, pick(i, *chunks), qpad, lse, total, acc)
            return carry

        lax.fori_loop(0, len(chunks), step, 0)

    attend(t.me)
    kv_net.relay()
    wo_net.relay()
    attend(t.xm, t.xp, t.zo)
    kv_net.cross()
    wo_net.cross()
    attend(t.xf)
    wo_net.finish()
    for p in range(PLANE):
        wo32[p * share : (p + 1) * share, :] = wo[p, 0:share, :].astype(F32)
    wo16[...] = wo32[...].astype(BF16)
    kv_net.got(5, 6)
    kv_net.got(7, 8)

    def last(y):
        cols = pl.ds(pl.multiple_of(y * rows, rows), rows)

        for c in (t.zxm, t.zxp, t.zxf):
            for h in range(HEADS):
                forward_block(kv, c, h, cols, qpad, lse, total, acc)
        for h in range(HEADS):
            att[h * HD : (h + 1) * HD, cols] = (
                acc[h, HD : 2 * HD, cols] / total[h, :, cols]
            ).astype(BF16)
            lse[h, :, cols] = lse[h, :, cols] + jnp.log(total[h, :, cols])
        part[y] = dot(att[:, cols], wo16[...], 0, 0).astype(BF16)

    sum_net = ColumnReduce(sum_sems, t, part, relays, lands)
    last(t.yf)
    sum_net.far()
    last(t.ym)
    last(t.yp)
    sum_net.near()
    last(t.y)
    sum_net.relay()

    def foresee(*chunks):
        def step(i, carry):
            prob_chunk(kv, pick(i, *chunks), qpad, lse, probs)
            return carry

        lax.fori_loop(0, len(chunks), step, 0)

    foresee(t.zxf, t.zxm)
    mixed = (frames[...].astype(F32) + sum_net.finish()).astype(BF16)

    mixed32 = mixed.astype(F32)
    mixed_keep[...] = mixed32
    shifted, normed, inverse = layer_norm(mixed32, gain2)
    inside = slice(HALO, HALO + rows)
    conv_wide[inside] = shifted.astype(BF16)
    conv_edge = Edge(conv_sems, t, conv_wide)
    conv_edge.begin()
    normed_keep[...] = normed
    foresee(t.zxp)
    conv_edge.finish()
    taps = conv_kernel.shape[0]

    def lanes_of(b):
        return pl.ds(pl.multiple_of(b * LANES, LANES), LANES)

    def convolve(b, carry):
        lanes = lanes_of(b)
        pre = jnp.zeros((rows, LANES), F32) + conv_bias[lanes][None]
        for offset, moved in shifts(conv_wide[:, lanes].astype(F32), rows, taps):
            pre = pre + moved * conv_kernel[offset - 1 : offset, lanes]
        sigma = 1.0 / (1.0 + jnp.exp(-pre))
        block_out[:, lanes] = (mixed_keep[:, lanes] + pre * sigma).astype(BF16)
        grad_wide[inside, lanes] = (
            out_grad[:, lanes].astype(F32) * sigma * (1.0 + pre * (1.0 - sigma))
        ).astype(BF16)
        return carry

    blocks = model // LANES
    lax.fori_loop(0, blocks, convolve, 0)
    grad_edge = Edge(grad_sems, t, grad_wide)
    grad_edge.begin()
    foresee(t.xf)
    grad_edge.finish()

    def convolve_back(b, carry):
        lanes = lanes_of(b)
        grad = jnp.zeros((rows, LANES), F32)
        for offset, moved in shifts(grad_wide[:, lanes].astype(F32), rows, taps):
            grad = grad + moved * conv_kernel[taps - offset : taps - offset + 1, lanes]
        conv_back[:, lanes] = grad
        return carry

    lax.fori_loop(0, blocks, convolve_back, 0)
    norm_grad, gain2_grad = norm_back(conv_back[...], normed_keep[...], inverse, gain2)
    gain2_grad = gain2_grad[None]
    mix[t.y] = (out_grad[...].astype(F32) + norm_grad).astype(BF16)
    mix_net = ColumnGather(mix_sems, t, mix)
    mix_net.begin()

    def kernel_grads(b, carry):
        lanes = lanes_of(b)
        grad = grad_wide[inside, lanes].astype(F32)
        for offset, moved in shifts(conv_wide[:, lanes].astype(F32), rows, taps):
            s_send[offset - 1, :, lanes] = jnp.sum(grad * moved, axis=0, keepdims=True)
        s_send[taps, :, lanes] = jnp.sum(grad, axis=0, keepdims=True)
        return carry

    lax.fori_loop(0, blocks, kernel_grads, 0)
    foresee(t.zo, t.xm, t.xp)
    mix_net.relay()
    foresee(t.me)
    mix_net.finish()

    mixed = mix[...].reshape(many, model)
    grads = dot(mixed, wo16[...], 1, 1).astype(BF16)
    grads_turned = dot(wo16[...], mixed, 1, 1).astype(BF16).astype(F32)
    for h in range(HEADS):
        lanes = slice(h * HD, (h + 1) * HD)
        mine = grads[:, lanes]
        dopad[h] = jnp.concatenate([zeros, mine], axis=1)
        delta[h] = jnp.sum(
            att[lanes, :].astype(F32) * grads_turned[lanes, :], axis=0, keepdims=True
        )
    dqt[...] = jnp.zeros_like(dqt)

    def backward(*chunks):
        def step(i, carry):
            backward_chunk(kv, pick(i, *chunks), qpad, dopad, probs, delta, dqt, dkv)
            return carry

        if len(chunks) == 1:
            step(0, 0)
        else:
            lax.fori_loop(0, len(chunks), step, 0)

    half = many // 2
    net = PlaneReduce(
        kv_sems,
        t,
        lambda p: dkv.at[p],
        lambda p, i: dkv.at[p, pl.ds(i * half, half)],
        lambda k: kv_land.at[k],
        lambda k: kv_half.at[k],
    )
    backward(t.zxf)
    net.far()
    backward(t.zxm, t.zxp)
    net.sides()
    backward(t.xf)
    net.opposite()
    backward(t.zo)
    net.across()
    backward(t.xm, t.xp)
    net.near()
    backward(t.me)
    for h in range(HEADS):
        proj[:, h * HD : (h + 1) * HD] = (dqt[h, 0:HD, :] * HD**-0.5).T.astype(BF16)

    out_terms = dot(att[...], mixed, 1, 0)
    quarter = o_part.shape[2]
    wide = model // 2
    for c in range(2):
        for p in range(PLANE):
            for i in range(quarter):
                piece = o_part.at[c, p, i]
                if i * 8 < share:
                    start = p * share + i * 8
                    piece[...] = out_terms[
                        start : start + 8, c * wide : (c + 1) * wide
                    ].astype(BF16)
                else:
                    piece[...] = jnp.zeros(piece.shape, BF16)
    order = (t.zxf, t.zxm, t.zxp, t.xf, t.zo, t.xm, t.xp, t.me)
    buddy = {"dp": t.hi * 2 + 1 - t.core}
    pair = Wire(core_sems)
    for k, p in enumerate(order):
        pair.go(k, o_part.at[1 - t.core, p], o_core.at[p], buddy)
    proj[:, width:] = net.finish().astype(BF16)

    weights = wq[...].reshape(model, 3 * width)

    def product(y):
        here = proj[pl.ds(pl.multiple_of(y * rows, rows), rows), :]
        part2[y] = dot(here, weights, 1, 1).astype(BF16)

    red = ColumnReduce(red_sems, t, part2, relays2, lands2)
    product(t.yf)
    red.far()
    half_rows = w_part.shape[3]

    def weight_terms(first, last):
        for k in range(first, last):
            p = order[k]
            terms = dot(hid_turned[:, p].reshape(GROUPS * shard, many), proj[...], 1, 0)
            terms = terms.reshape(GROUPS, 2, half_rows, 3 * width).astype(BF16)
            for c in range(2):
                w_part[c, :, p] = terms[:, c]
            pair.go(8 + k, w_part.at[1 - t.core, :, p], w_core.at[:, p], buddy)

    product(t.ym)
    product(t.yp)
    red.near()
    weight_terms(0, 3)
    product(t.y)
    w_mine, o_mine = w_part.at[t.core], o_part.at[t.core]
    o_net = PlaneReduce(
        o_sems,
        t,
        lambda p: o_mine.at[p],
        lambda p, i: o_mine.at[p, pl.ds(2 * i, 2)],
        lambda k: o_land.at[k],
        lambda k: o_half.at[k],
    )
    w_net = PlaneReduce(
        w_sems,
        t,
        lambda p: w_mine.at[:, p],
        lambda p, i: w_mine.at[pl.ds(2 * i, 2), p],
        lambda k: w_land.at[k],
        lambda k: w_half.at[k],
    )

    def join(first, last):
        for k in range(first, last):
            p = order[k]
            pair.got(k, 8 + k)
            o_net.add(o_mine.at[p], o_core.at[p])
            w_net.add(w_mine.at[:, p], w_core.at[:, p])

    red.relay()
    join(0, 1)
    w_net.far()
    o_net.far()
    join(1, 3)
    w_net.sides()
    o_net.sides()
    weight_terms(3, 8)
    join(3, 8)
    w_net.opposite()
    o_net.opposite()
    w_net.across()
    o_net.across()
    w_net.near()
    o_net.near()

    grad_hidden = red.finish()
    _, normed, inverse = layer_norm(frames[...].astype(F32), gain1)
    norm_grad, gain_sum = norm_back(grad_hidden, normed, inverse, gain1)
    grad_input[...] = (mix[t.y].astype(F32) + norm_grad).astype(BF16)
    gains = (gain_sum[None], gain2_grad)
    count = s_send.shape[0]
    for r in range(count):
        if r < 2 * (model // 128):
            row, col = divmod(r, model // 128)
            s_send[r, :, model:] = gains[row][:, col * 128 : (col + 1) * 128]
        else:
            s_send[r, :, model:] = jnp.zeros((1, 128), F32)
    s_net = Wire(s_sems)
    s_seq[t.seq] = s_send[t.seq]
    for k in range(1, count):
        r = (t.seq + k) % count
        s_net.go(k - 1, s_send.at[r], s_seq.at[t.seq], {"seq": r})

    o_total, w_total = o_net.finish(), w_net.finish()
    o_mine[t.me] = o_total.astype(BF16)
    w_mine[:, t.me] = w_total.astype(BF16)
    hi_net = Wire(hi_sems)
    for k in range(1, 4):
        j = (t.hi + k) % 4
        there = {"dp": j * 2 + t.core}
        hi_net.go(k - 1, w_mine.at[j, t.me], w_hi.at[k - 1], there)
        hi_net.go(2 + k, o_mine.at[t.me, j], o_hi.at[k - 1], there)

    s_net.got(*range(count - 1))
    s_mine[...] = jnp.sum(s_seq[...], axis=0)
    s_dp[t.dp] = s_mine[...]
    s_dp_net = Wire(s_dp_sems)
    for k in range(1, 8):
        s_dp_net.go(k - 1, s_mine, s_dp.at[t.dp], {"dp": (t.dp + k) % 8})

    hi_net.got(*range(6))
    w_out_block = w_mine[t.hi, t.me].astype(F32)
    o_out_block = o_mine[t.me, t.hi].astype(F32)
    for k in range(3):
        w_out_block = w_out_block + w_hi[k].astype(F32)
        o_out_block = o_out_block + o_hi[k].astype(F32)
    w_done[...] = w_out_block.astype(BF16)
    o_done[...] = o_out_block.astype(BF16)
    finals = []
    for k in range(1, 8):
        d = (t.dp + k) % 8
        for src, dst, send, recv, y in (
            (w_done, w_fin.at[t.y, t.core], w_fin_send.at[k], w_fin_recv.at[t.y, t.core], t.hi),
            (o_done, o_fin.at[t.hi, t.core], o_fin_send.at[k], o_fin_recv.at[t.hi, t.core], t.y),
        ):
            copy = pltpu.make_async_remote_copy(
                src_ref=src, dst_ref=dst, send_sem=send, recv_sem=recv, device_id=t.holder(y, d)
            )
            copy.start()
            finals.append(copy)
    o_own = pltpu.make_async_copy(
        o_done, o_fin.at[t.hi, t.core], o_fin_recv.at[t.hi, t.core]
    )
    o_own.start()
    w_own = pltpu.make_async_copy(w_done, w_fin.at[t.y, t.core], w_fin_recv.at[t.y, t.core])
    w_away = pltpu.make_async_remote_copy(
        src_ref=w_done,
        dst_ref=w_fin.at[t.y, t.core],
        send_sem=w_fin_send.at[0],
        recv_sem=w_fin_recv.at[t.y, t.core],
        device_id=t.holder(t.hi, t.dp),
    )

    @pl.when(t.hi == t.y)
    def _():
        w_own.start()

    @pl.when(t.hi != t.y)
    def _():
        w_away.start()

    s_dp_net.got(*range(7))
    summed = s_dp[0]
    for d in range(1, 8):
        summed = summed + s_dp[d]
    s_done[...] = summed
    s_fin[t.seq] = summed
    s_fin_net = Wire(s_fin_sems)
    for k in range(1, count):
        s_fin_net.go(k - 1, s_done, s_fin.at[t.seq], {"seq": (t.seq + k) % count})

    for i in range(4):
        for c in range(2):
            pltpu.make_async_copy(w_done, w_fin.at[i, c], w_fin_recv.at[i, c]).wait()
            pltpu.make_async_copy(o_done, o_fin.at[i, c], o_fin_recv.at[i, c]).wait()
    pieces = [w_fin[y].astype(F32).reshape(2 * half_rows, 3 * width) for y in range(GROUPS)]
    columns = [piece[:, :width] for piece in pieces]
    for kind in range(2):
        for piece in pieces:
            for h in range(HEADS):
                start = width + (2 * h + kind) * HD
                columns.append(piece[:, start : start + HD])
    grad_qkv[...] = jnp.concatenate(columns, axis=1).astype(BF16)
    sides = [
        o_fin[0 : share // 8, c].astype(F32).reshape(share, wide) for c in range(2)
    ]
    grad_out[...] = jnp.concatenate(sides, axis=1).astype(BF16)
    s_fin_net.got(*range(count - 1))
    for r in range(count):
        row = s_fin[r]
        if r < taps:
            kernel_sum[r : r + 1, :] = row[:, :model]
        else:
            bias_sum[...] = row[:, :model]
        if r < 2 * (model // 128):
            i, col = divmod(r, model // 128)
            norms_sum[i : i + 1, col * 128 : (col + 1) * 128] = row[:, model:]
    for copy in finals:
        copy.wait_send()

    @pl.when(t.hi != t.y)
    def _():
        w_away.wait_send()

    for wire in (spread, hid_net, wq_net, wo_net, kv_net, sum_net, mix_net, net, pair, o_net, red, w_net, hi_net, s_net, s_dp_net, s_fin_net):
        wire.done()


def bf16(*shape):
    return pltpu.VMEM(shape, BF16)


def f32(*shape):
    return pltpu.VMEM(shape, F32)


def dma(*shape):
    return pltpu.SemaphoreType.DMA(shape)


def whole(frames, w_qkv, w_out, gains, conv_kernel, conv_bias, out_grad):
    rows, model = frames.shape
    shard = w_qkv.shape[0]
    many = GROUPS * rows
    width = HEADS * HD
    half = shard // 2
    padded = 32
    count = conv_kernel.shape[0] + 1
    like = jax.ShapeDtypeStruct
    ins = dict(
        frames=frames,
        w_qkv=w_qkv,
        w_out=w_out,
        gains_in=gains,
        conv_kernel=conv_kernel,
        conv_bias=conv_bias,
        out_grad=out_grad,
    )
    outs = dict(
        block_out=like((rows, model), BF16),
        grad_input=like((rows, model), BF16),
        grad_qkv=like(w_qkv.shape, BF16),
        grad_out=like(w_out.shape, BF16),
        kernel_sum=like((count - 1, model), F32),
        bias_sum=like((1, model), F32),
        norms_sum=like((2, model), F32),
    )
    scratch = dict(
        w_parts=bf16(GROUPS, shard, 3 * width),
        hid=bf16(GROUPS, rows, model),
        wq=bf16(GROUPS, PLANE, shard, 3 * width),
        wo=bf16(PLANE, padded, model),
        wo32=f32(width, model),
        wo16=bf16(width, model),
        kv=bf16(PLANE, many, 2 * width),
        qpad=bf16(HEADS, many, 2 * HD),
        lse=f32(HEADS, 1, many),
        total=f32(HEADS, 1, many),
        acc=f32(HEADS, 2 * HD, many),
        att=bf16(width, many),
        hid_turned=bf16(GROUPS, PLANE, shard, many),
        probs=bf16(PLANE, HEADS, many, many),
        part=bf16(GROUPS, rows, model),
        relays=bf16(2, rows // 2, model),
        lands=bf16(2, rows, model),
        mixed_keep=f32(rows, model),
        normed_keep=f32(rows, model),
        conv_wide=bf16(rows + 2 * HALO, model),
        grad_wide=bf16(rows + 2 * HALO, model),
        conv_back=f32(rows, model),
        mix=bf16(GROUPS, rows, model),
        dopad=bf16(HEADS, many, 2 * HD),
        delta=f32(HEADS, 1, many),
        dqt=f32(HEADS, 2 * HD, many),
        dkv=bf16(PLANE, many, 2 * width),
        kv_land=bf16(6, many, 2 * width),
        kv_half=bf16(2, many // 2, 2 * width),
        proj=bf16(many, 3 * width),
        part2=bf16(GROUPS, rows, model),
        relays2=bf16(2, rows // 2, model),
        lands2=bf16(2, rows, model),
        w_part=bf16(2, GROUPS, PLANE, half, 3 * width),
        w_core=bf16(GROUPS, PLANE, half, 3 * width),
        w_land=bf16(6, GROUPS, half, 3 * width),
        w_half=bf16(2, GROUPS // 2, half, 3 * width),
        w_hi=bf16(3, half, 3 * width),
        w_done=bf16(half, 3 * width),
        w_fin=bf16(GROUPS, 2, half, 3 * width),
        o_part=bf16(2, PLANE, 4, 8, model // 2),
        o_core=bf16(PLANE, 4, 8, model // 2),
        o_land=bf16(6, 4, 8, model // 2),
        o_half=bf16(2, 2, 8, model // 2),
        o_hi=bf16(3, 8, model // 2),
        o_done=bf16(8, model // 2),
        o_fin=bf16(4, 2, 8, model // 2),
        s_send=f32(count, 1, model + LANES),
        s_seq=f32(count, 1, model + LANES),
        s_mine=f32(1, model + LANES),
        s_dp=f32(8, 1, model + LANES),
        s_done=f32(1, model + LANES),
        s_fin=f32(count, 1, model + LANES),
        spread_sems=wire_sems(3),
        hid_sems=wire_sems(4),
        wq_sems=wire_sems(9),
        wo_sems=wire_sems(9),
        gather_sems=wire_sems(9),
        sum_sems=wire_sems(6),
        conv_sems=wire_sems(2),
        grad_sems=wire_sems(2),
        mix_sems=wire_sems(4),
        kv_sems=wire_sems(8),
        red_sems=wire_sems(6),
        core_sems=wire_sems(16),
        w_sems=wire_sems(8),
        o_sems=wire_sems(8),
        hi_sems=wire_sems(6),
        w_fin_send=dma(8),
        w_fin_recv=dma(4, 2),
        o_fin_send=dma(8),
        o_fin_recv=dma(4, 2),
        s_sems=wire_sems(count - 1),
        s_dp_sems=wire_sems(7),
        s_fin_sems=wire_sems(count - 1),
    )
    vmem = pl.BlockSpec(memory_space=pltpu.VMEM)
    names = [*ins, *outs, *scratch]
    return pl.pallas_call(
        functools.partial(whole_kernel, names),
        out_shape=list(outs.values()),
        in_specs=[vmem] * len(ins),
        out_specs=[vmem] * len(outs),
        scratch_shapes=list(scratch.values()),
        compiler_params=pltpu.CompilerParams(
            collective_id=0, has_side_effects=True, vmem_limit_bytes=62 * 2**20
        ),
        name="whole",
    )(*ins.values())


def hand_on_kernel(*refs):
    half = len(refs) // 2
    for src, dst in zip(refs[:half], refs[half:]):
        dst[...] = src[...].reshape(dst.shape)


def hand_on(*arrays):
    vmem = pl.BlockSpec(memory_space=pltpu.VMEM)
    return pl.pallas_call(
        hand_on_kernel,
        out_shape=[
            jax.ShapeDtypeStruct(a.shape[1:] if a.shape[0] == 1 else a.shape, a.dtype) for a in arrays
        ],
        in_specs=[vmem] * len(arrays),
        out_specs=[vmem] * len(arrays),
        name="hand_on",
    )(*arrays)


def local(frames, w_qkv, w_out, norm_gains, conv_kernel, conv_bias, out_grad):
    block_out, grad_input, grad_qkv, grad_out, kernel_sum, bias_sum, norms_sum = hand_on(
        *whole(
            frames[0], w_qkv, w_out, norm_gains, conv_kernel, conv_bias, out_grad[0]
        )
    )
    return (
        block_out[None],
        grad_input[None],
        grad_qkv,
        grad_out,
        norms_sum,
        kernel_sum,
        bias_sum,
    )


def solution(mesh):
    in_specs = (
        P("dp", "seq", None),
        P("seq", None),
        P("seq", None),
        P(),
        P(),
        P(),
        P("dp", "seq", None),
    )
    out_specs = (
        P("dp", "seq", None),
        P("dp", "seq", None),
        P("seq", None),
        P("seq", None),
        P(),
        P(),
        P(),
    )
    return jax.shard_map(local, mesh=mesh, in_specs=in_specs, out_specs=out_specs, check_vma=False)
```

```python
import functools

import jax
import jax.numpy as jnp
from jax import lax
from jax.experimental import pallas as pl
from jax.experimental.pallas import tpu as pltpu
from jax.sharding import PartitionSpec as P

EPS = 1e-05
GROUPS = 4
PLANE = 8
HEADS = 3
HD = 64
F32 = jnp.float32
BF16 = jnp.bfloat16


def layer_norm(values, gain):
    center = values - jnp.mean(values, axis=-1, keepdims=True)
    spread = jnp.mean(center * center, axis=-1, keepdims=True)
    inverse = lax.rsqrt(spread + EPS)
    normed = center * inverse
    return (normed * gain, normed, inverse)


def norm_back(grad, normed, inverse, gain):
    scaled = grad * gain
    inner = (
        scaled
        - jnp.mean(scaled, axis=-1, keepdims=True)
        - normed * jnp.mean(scaled * normed, axis=-1, keepdims=True)
    )
    return (inverse * inner, jnp.sum(grad * normed, axis=0))


def dot(a, b, ca, cb):
    return lax.dot_general(a, b, (((ca,), (cb,)), ((), ())), preferred_element_type=F32)


class Place:
    def __init__(self):
        seq = lax.axis_index("seq")
        y, z, x = seq // 8, (seq // 4) % 2, seq % 4
        right, left, far, other = (x + 1) % 4, (x + 3) % 4, (x + 2) % 4, 1 - z
        self.y, self.yp, self.ym, self.yf = y, (y + 1) % 4, (y + 3) % 4, (y + 2) % 4
        self.me = z * 4 + x
        self.xp, self.xm, self.xf = z * 4 + right, z * 4 + left, z * 4 + far
        self.zo = other * 4 + x
        self.zxp, self.zxm, self.zxf = other * 4 + right, other * 4 + left, other * 4 + far

        self.seq, self.dp = seq, lax.axis_index("dp")
        self.core, self.hi = self.dp % 2, self.dp // 2

    def plane(self, p):
        return {"seq": self.y * 8 + p}

    def holder(self, y, dp):
        return {"seq": y * 8 + self.me, "dp": dp}

    def greet(self):
        near = [{"seq": (self.seq + i) % 32} for i in range(1, 32)]
        near += [
            self.holder((self.y + i) % 4, (self.dp + j) % 8) for i in range(4) for j in range(1, 8)
        ]
        for device in near:
            pl.semaphore_signal(pltpu.get_barrier_semaphore(), inc=1, device_id=device)
        return len(near)

    def column(self, y):
        return {"seq": y * 8 + self.me}


class Wire:
    def __init__(self, sems):
        self.sems, self.sent = sems, {}

    def go(self, k, src, dst, device):
        copy = pltpu.make_async_remote_copy(
            src_ref=src,
            dst_ref=dst,
            send_sem=self.sems.at[0, k],
            recv_sem=self.sems.at[1, k],
            device_id=device,
        )
        copy.start()
        self.sent[k] = copy

    def got(self, *ks):
        for k in ks:
            self.sent[k].wait_recv()

    def done(self):
        for copy in self.sent.values():
            copy.wait_send()


def wire_sems(count):
    return pltpu.SemaphoreType.DMA((2, count))


class ColumnGather(Wire):
    def __init__(self, sems, place, buf):
        super().__init__(sems)
        self.at, self.buf = place, buf
        self.half = buf.shape[1] // 2

    def begin(self):
        t, own = self.at, self.buf.at[self.at.y]
        self.go(0, own, own, t.column(t.yp))
        self.go(1, own, own, t.column(t.ym))

    def relay(self):
        t, h = self.at, self.half
        self.got(0)
        first = self.buf.at[t.ym, pl.ds(0, h)]
        self.go(2, first, first, t.column(t.yp))
        self.got(1)
        second = self.buf.at[t.yp, pl.ds(h, h)]
        self.go(3, second, second, t.column(t.ym))

    def finish(self):
        self.got(2, 3)


class ColumnReduce(Wire):
    def __init__(self, sems, place, part, relays, lands):
        super().__init__(sems)
        self.at, self.part, self.relays, self.lands = place, part, relays, lands
        self.half = part.shape[1] // 2

    def far(self):
        t, h = self.at, self.half
        self.go(0, self.part.at[t.yf, pl.ds(0, h)], self.relays.at[0], t.column(t.ym))
        self.go(1, self.part.at[t.yf, pl.ds(h, h)], self.relays.at[1], t.column(t.yp))

    def near(self):
        t, h = self.at, self.half
        low, high = pl.ds(0, h), pl.ds(h, h)
        self.go(2, self.part.at[t.ym, high], self.lands.at[0, high], t.column(t.ym))
        self.go(3, self.part.at[t.yp, low], self.lands.at[1, low], t.column(t.yp))

    def relay(self):
        t, h = self.at, self.half
        low, high = pl.ds(0, h), pl.ds(h, h)
        self.got(0)
        self.part[t.ym, low] = (
            self.part[t.ym, low].astype(F32) + self.relays[0].astype(F32)
        ).astype(BF16)
        self.go(4, self.part.at[t.ym, low], self.lands.at[0, low], t.column(t.ym))
        self.got(1)
        self.part[t.yp, high] = (
            self.part[t.yp, high].astype(F32) + self.relays[1].astype(F32)
        ).astype(BF16)
        self.go(5, self.part.at[t.yp, high], self.lands.at[1, high], t.column(t.yp))

    def finish(self):
        self.got(2, 3, 4, 5)
        return (
            self.part[self.at.y].astype(F32)
            + self.lands[0].astype(F32)
            + self.lands[1].astype(F32)
        )


class PlaneGather(Wire):
    def __init__(self, sems, place, full, half):
        super().__init__(sems)
        self.at, self.full, self.half = place, full, half

    def begin(self):
        t, own = self.at, self.full(self.at.me)
        self.go(0, own, own, t.plane(t.xp))
        self.go(1, own, own, t.plane(t.xm))
        self.go(2, own, own, t.plane(t.zo))

    def relay(self):
        t = self.at
        self.got(0)
        first = self.half(t.xm, 0)
        self.go(3, first, first, t.plane(t.xp))
        self.got(1)
        second = self.half(t.xp, 1)
        self.go(4, second, second, t.plane(t.xm))
        self.got(2)
        other = self.full(t.zo)
        self.go(5, other, other, t.plane(t.xp))
        self.go(6, other, other, t.plane(t.xm))

    def cross(self):
        t = self.at
        for k in (0, 1):
            self.got(3 + k)
            part = self.half(t.xf, k)
            self.go(7 + k, part, part, t.plane(t.zo))

    def finish(self):
        self.got(5, 6, 7, 8)


class PlaneReduce(Wire):
    def __init__(self, sems, place, full, half, land, land_half, half_land):
        super().__init__(sems)
        self.at, self.full, self.half = place, full, half
        self.land, self.land_half, self.half_land = land, land_half, half_land

    def add(self, ref, *more):
        total = ref[...].astype(F32)
        for other in more:
            total = total + other[...].astype(F32)
        ref[...] = total.astype(BF16)

    def far(self):
        t = self.at
        self.go(0, self.half(t.zxf, 0), self.land_half(0, 0), t.plane(t.zo))
        self.go(8, self.half(t.zxf, 1), self.land_half(0, 1), t.plane(t.zo))

    def left(self):
        self.go(1, self.full(self.at.zxm), self.land(1), self.at.plane(self.at.xm))

    def right(self):
        self.go(2, self.full(self.at.zxp), self.land(2), self.at.plane(self.at.xp))

    def opposite(self, i):
        t = self.at
        self.got((0, 8)[i])
        self.add(self.half(t.xf, i), self.land_half(0, i))
        self.go(3 + i, self.half(t.xf, i), self.half_land(i), t.plane((t.xm, t.xp)[i]))

    def early(self):
        t = self.at
        self.go(6, self.half(t.xm, 1), self.land_half(4, 1), t.plane(t.xm))
        self.go(7, self.half(t.xp, 0), self.land_half(5, 0), t.plane(t.xp))

    def across(self):
        t = self.at
        self.got(1, 2)
        self.add(self.full(t.zo), self.land(1), self.land(2))
        self.go(5, self.full(t.zo), self.land(3), t.plane(t.zo))

    def near(self):
        t = self.at
        self.got(3)
        self.add(self.half(t.xm, 0), self.half_land(0))
        self.go(9, self.half(t.xm, 0), self.land_half(4, 0), t.plane(t.xm))
        self.got(4)
        self.add(self.half(t.xp, 1), self.half_land(1))
        self.go(10, self.half(t.xp, 1), self.land_half(5, 1), t.plane(t.xp))

    def finish(self):
        self.got(5, 6, 7, 9, 10)
        total = self.full(self.at.me)[...].astype(F32)
        for k in (3, 4, 5):
            total = total + self.land(k)[...].astype(F32)
        return total


def pick(i, *values):
    out = values[-1]
    for k in range(len(values) - 2, -1, -1):
        out = jnp.where(i == k, values[k], out)
    return out


def local_copies(pairs, sems):
    copies = [
        pltpu.make_async_copy(src, dst, sems.at[i]) for i, (src, dst) in enumerate(pairs)
    ]
    for copy in copies:
        copy.start()
    return copies


QB = 128


def forward_block(kv, c, h, cols, qpad, top, total, acc):
    both = kv[c, :, h * 128 : (h + 1) * 128]
    scores = dot(both, qpad[h, cols, :], 1, 1)
    old = top[h, :, cols]
    new = jnp.maximum(old, jnp.max(scores, axis=0, keepdims=True))
    shrink = jnp.exp(old - new)
    expo = jnp.exp(scores - new)
    top[h, :, cols] = new
    total[h, :, cols] = total[h, :, cols] * shrink + jnp.sum(expo, axis=0, keepdims=True)
    acc[h, :, cols] = acc[h, :, cols] * shrink + dot(both, expo.astype(BF16), 0, 0)


def forward_chunk(kv, c, qpad, top, total, acc):
    for h in range(HEADS):
        for b in range(qpad.shape[1] // QB):
            forward_block(kv, c, h, slice(b * QB, (b + 1) * QB), qpad, top, total, acc)


def prob_chunk(kv, c, qpad, lse, probs):
    for h in range(HEADS):
        scores = dot(kv[c, :, h * 128 : (h + 1) * 128], qpad[h], 1, 1)
        probs[c, h] = jnp.exp(scores - lse[h]).astype(BF16)


def backward_chunk(kv, c, qpad, dopad, probs, delta, dqt, out):
    for h in range(HEADS):
        lanes = slice(h * 128, (h + 1) * 128)
        both, query, grad = kv[c, :, lanes], qpad[h], dopad[h]
        slopes = dot(both, grad, 1, 1)
        prob = probs[c, h]
        score_grads = (prob.astype(F32) * (slopes - delta[h])).astype(BF16)
        out[c, :, lanes] = (
            dot(prob, grad, 1, 0) + dot(score_grads, query, 1, 0)
        ).astype(BF16)
        dqt[h] += dot(both, score_grads, 0, 0)


HALO = 16
LANES = 128


def shifts(wide, length, taps):
    for low in range(8):
        moved = wide if low == 0 else pltpu.roll(wide, wide.shape[0] - low, 0)
        for offset in range(low, taps + 1, 8):
            if offset > 0:
                yield offset, moved[offset - low : offset - low + length]


class Edge(Wire):
    def __init__(self, sems, place, wide):
        super().__init__(sems)
        t, rows = place, wide.shape[0]
        self.first, self.last = t.seq == 0, t.seq == 31
        nothing = jnp.zeros((HALO, wide.shape[1]), BF16)

        @pl.when(self.first)
        def _():
            wide[0:HALO] = nothing

        @pl.when(self.last)
        def _():
            wide[rows - HALO :] = nothing

        self.up = pltpu.make_async_remote_copy(
            src_ref=wide.at[pl.ds(rows - 2 * HALO, HALO)],
            dst_ref=wide.at[pl.ds(0, HALO)],
            send_sem=sems.at[0, 0],
            recv_sem=sems.at[1, 0],
            device_id={"seq": jnp.minimum(t.seq + 1, 31)},
        )
        self.down = pltpu.make_async_remote_copy(
            src_ref=wide.at[pl.ds(HALO, HALO)],
            dst_ref=wide.at[pl.ds(rows - HALO, HALO)],
            send_sem=sems.at[0, 1],
            recv_sem=sems.at[1, 1],
            device_id={"seq": jnp.maximum(t.seq - 1, 0)},
        )

    def begin(self):
        @pl.when(jnp.logical_not(self.last))
        def _():
            self.up.start()

        @pl.when(jnp.logical_not(self.first))
        def _():
            self.down.start()

    def finish(self):
        @pl.when(jnp.logical_not(self.last))
        def _():
            self.up.wait_send()
            self.down.wait_recv()

        @pl.when(jnp.logical_not(self.first))
        def _():
            self.down.wait_send()
            self.up.wait_recv()


def whole_kernel(names, *refs):
    r = dict(zip(names, refs))
    (
        frames,
        w_qkv,
        w_out,
        gains_in,
        conv_kernel,
        conv_bias,
        out_grad,
        block_out,
        grad_input,
        grad_qkv,
        grad_out,
        kernel_sum,
        bias_sum,
        norms_sum,
        w_parts,
        hid,
        wq,
        wo,
        wo32,
        wo16,
        kv,
        qpad,
        lse,
        total,
        acc,
        att,
        probs,
        part,
        relays,
        lands,
        mixed_keep,
        normed_keep,
        conv_wide,
        grad_wide,
        conv_back,
        mix,
        dopad,
        delta,
        dqt,
        dkv,
        kv_land,
        kv_half,
        proj,
        part2,
        relays2,
        lands2,
        w_part,
        w_core,
        w_land,
        w_half,
        w_hi,
        w_done,
        w_fin,
        o_part,
        o_core,
        o_land,
        o_half,
        o_hi,
        o_done,
        o_fin,
        s_send,
        s_seq,
        s_mine,
        s_dp,
        s_done,
        s_fin,
        spread_sems,
        swap_sems,
        hid_sems,
        wq_sems,
        wo_sems,
        gather_sems,
        sum_sems,
        conv_sems,
        grad_sems,
        mix_sems,
        kv_sems,
        red_sems,
        core_sems,
        w_sems,
        o_sems,
        hi_sems,
        o_hi_sems,
        w_fin_send,
        w_fin_recv,
        o_fin_send,
        o_fin_recv,
        s_sems,
        s_dp_sems,
        s_fin_sems,
    ) = (r[n] for n in names)
    t = Place()
    greeted = t.greet()
    rows, model = frames.shape
    many = GROUPS * rows
    width = HEADS * HD
    shard = w_qkv.shape[0]
    gain1, gain2 = gains_in[0:1, :], gains_in[1:2, :]

    for g in range(GROUPS):
        columns = [w_qkv[:, g * width : (g + 1) * width]]
        for h in range(HEADS):
            for kind in (1, 2):
                start = (kind * GROUPS + g) * width + h * HD
                columns.append(w_qkv[:, start : start + HD])
        w_parts[g] = jnp.concatenate(columns, axis=1)
    inputs = frames[...].astype(F32)
    shifted, _, _ = layer_norm(inputs, gain1)
    hid[t.y] = shifted.astype(BF16)
    pl.semaphore_wait(pltpu.get_barrier_semaphore(), greeted)
    hid_net = ColumnGather(hid_sems, t, hid)
    hid_net.begin()
    holds = t.y // 2 == t.core
    spread_copies = []
    for k in range(1, GROUPS):
        y = (t.y + k) % GROUPS
        copy = pltpu.make_async_remote_copy(
            src_ref=w_parts.at[y],
            dst_ref=wq.at[t.y, t.me],
            send_sem=spread_sems.at[0, k - 1],
            recv_sem=spread_sems.at[1, k - 1],
            device_id=t.column(y),
        )
        spread_copies.append((copy, ((t.y + GROUPS - k) % GROUPS) // 2 == t.core))

    @pl.when(holds)
    def _():
        for copy, _ in spread_copies:
            copy.start()
        wq[t.y, t.me] = w_parts[t.y]

    share = width // PLANE
    wo[t.me] = jnp.concatenate(
        [w_out[...].astype(F32), jnp.zeros((wo.shape[1] - share, model), F32)], axis=0
    ).astype(BF16)

    for copy, comes in spread_copies:
        pl.when(comes)(copy.wait_recv)
    base = 2 * t.core
    wq_net = PlaneGather(
        wq_sems, t, lambda p: wq.at[pl.ds(base, 2), p], lambda p, i: wq.at[base + i, p]
    )
    swap = Wire(swap_sems)
    buddy = {"dp": t.hi * 2 + 1 - t.core}

    def trade(*ps):
        for p in ps:
            half = wq.at[pl.ds(base, 2), p]
            swap.go(len(swap.sent), half, half, buddy)
    wo_net = PlaneGather(
        wo_sems, t, lambda p: wo.at[p], lambda p, i: wo.at[p, pl.ds(16 * i, 16)]
    )
    wq_net.begin()
    trade(t.me)
    wq_net.relay()
    trade(t.xm, t.xp, t.zo)
    hid_net.relay()
    wq_net.cross()
    trade(t.xf)
    wo_net.begin()
    wq_net.finish()
    trade(t.zxm, t.zxp, t.zxf)
    hid_net.finish()
    swap.got(*range(PLANE))

    hidden = hid[...].reshape(many, model)
    weights = wq[...].reshape(model, 3 * width)
    projected = dot(hidden, weights, 1, 0).astype(BF16)
    kv[t.me] = projected[:, width:]
    kv_net = PlaneGather(
        gather_sems,
        t,
        lambda p: kv.at[p],
        lambda p, i: kv.at[p, pl.ds(i * (many // 2), many // 2)],
    )
    kv_net.begin()
    zeros = jnp.zeros((many, HD), BF16)
    for h in range(HEADS):
        qpad[h] = jnp.concatenate(
            [projected[:, h * HD : (h + 1) * HD] * BF16(HD**-0.5), zeros], axis=1
        )
    lse[...] = jnp.full_like(lse, -jnp.inf)
    total[...] = jnp.zeros_like(total)
    acc[...] = jnp.zeros_like(acc)

    def attend(*chunks):
        if len(chunks) == 1:
            forward_chunk(kv, chunks[0], qpad, lse, total, acc)
            return

        def step(i, carry):
            forward_chunk(kv, pick(i, *chunks), qpad, lse, total, acc)
            return carry

        lax.fori_loop(0, len(chunks), step, 0)

    attend(t.me)
    kv_net.relay()
    wo_net.relay()
    attend(t.xm, t.xp, t.zo)
    kv_net.cross()
    wo_net.cross()
    attend(t.xf)
    wo_net.finish()
    for p in range(PLANE):
        wo32[p * share : (p + 1) * share, :] = wo[p, 0:share, :].astype(F32)
    wo16[...] = wo32[...].astype(BF16)
    kv_net.got(5, 6)
    kv_net.got(7, 8)

    def last(y):
        cols = pl.ds(pl.multiple_of(y * rows, rows), rows)

        for c in (t.zxm, t.zxp, t.zxf):
            for h in range(HEADS):
                forward_block(kv, c, h, cols, qpad, lse, total, acc)
        for h in range(HEADS):
            att[h * HD : (h + 1) * HD, cols] = (
                acc[h, HD : 2 * HD, cols] / total[h, :, cols]
            ).astype(BF16)
            lse[h, :, cols] = lse[h, :, cols] + jnp.log(total[h, :, cols])
        part[y] = dot(att[:, cols], wo16[...], 0, 0).astype(BF16)

    sum_net = ColumnReduce(sum_sems, t, part, relays, lands)
    last(t.yf)
    sum_net.far()
    last(t.ym)
    last(t.yp)
    sum_net.near()
    last(t.y)
    sum_net.relay()

    def foresee(*chunks):
        def step(i, carry):
            prob_chunk(kv, pick(i, *chunks), qpad, lse, probs)
            return carry

        lax.fori_loop(0, len(chunks), step, 0)

    foresee(t.zxf, t.zxm)
    mixed = (frames[...].astype(F32) + sum_net.finish()).astype(BF16)

    mixed32 = mixed.astype(F32)
    mixed_keep[...] = mixed32
    shifted, normed, inverse = layer_norm(mixed32, gain2)
    inside = slice(HALO, HALO + rows)
    conv_wide[inside] = shifted.astype(BF16)
    conv_edge = Edge(conv_sems, t, conv_wide)
    conv_edge.begin()
    normed_keep[...] = normed
    foresee(t.zxp)
    conv_edge.finish()
    taps = conv_kernel.shape[0]

    def lanes_of(b):
        return pl.ds(pl.multiple_of(b * LANES, LANES), LANES)

    def convolve(b, carry):
        lanes = lanes_of(b)
        pre = jnp.zeros((rows, LANES), F32) + conv_bias[lanes][None]
        for offset, moved in shifts(conv_wide[:, lanes].astype(F32), rows, taps):
            pre = pre + moved * conv_kernel[offset - 1 : offset, lanes]
        sigma = 1.0 / (1.0 + jnp.exp(-pre))
        block_out[:, lanes] = (mixed_keep[:, lanes] + pre * sigma).astype(BF16)
        grad_wide[inside, lanes] = (
            out_grad[:, lanes].astype(F32) * sigma * (1.0 + pre * (1.0 - sigma))
        ).astype(BF16)
        return carry

    blocks = model // LANES
    lax.fori_loop(0, blocks, convolve, 0)
    grad_edge = Edge(grad_sems, t, grad_wide)
    grad_edge.begin()
    foresee(t.xf)
    grad_edge.finish()

    def convolve_back(b, carry):
        lanes = lanes_of(b)
        grad = jnp.zeros((rows, LANES), F32)
        for offset, moved in shifts(grad_wide[:, lanes].astype(F32), rows, taps):
            grad = grad + moved * conv_kernel[taps - offset : taps - offset + 1, lanes]
        conv_back[:, lanes] = grad
        return carry

    lax.fori_loop(0, blocks, convolve_back, 0)
    norm_grad, gain2_grad = norm_back(conv_back[...], normed_keep[...], inverse, gain2)
    gain2_grad = gain2_grad[None]
    mix[t.y] = (out_grad[...].astype(F32) + norm_grad).astype(BF16)
    mix_net = ColumnGather(mix_sems, t, mix)
    mix_net.begin()

    def kernel_grads(b, carry):
        lanes = lanes_of(b)
        grad = grad_wide[inside, lanes].astype(F32)
        for offset, moved in shifts(conv_wide[:, lanes].astype(F32), rows, taps):
            s_send[offset - 1, :, lanes] = jnp.sum(grad * moved, axis=0, keepdims=True)
        s_send[taps, :, lanes] = jnp.sum(grad, axis=0, keepdims=True)
        return carry

    lax.fori_loop(0, blocks, kernel_grads, 0)
    foresee(t.zo, t.xm, t.xp)
    mix_net.relay()
    foresee(t.me)
    mix_net.finish()

    mixed = mix[...].reshape(many, model)
    grads = dot(mixed, wo16[...], 1, 1).astype(BF16)
    grads_turned = dot(wo16[...], mixed, 1, 1).astype(BF16).astype(F32)
    for h in range(HEADS):
        lanes = slice(h * HD, (h + 1) * HD)
        mine = grads[:, lanes]
        dopad[h] = jnp.concatenate([zeros, mine], axis=1)
        delta[h] = jnp.sum(
            att[lanes, :].astype(F32) * grads_turned[lanes, :], axis=0, keepdims=True
        )
    dqt[...] = jnp.zeros_like(dqt)

    def backward(*chunks):
        def step(i, carry):
            backward_chunk(kv, pick(i, *chunks), qpad, dopad, probs, delta, dqt, dkv)
            return carry

        if len(chunks) == 1:
            step(0, 0)
        else:
            lax.fori_loop(0, len(chunks), step, 0)

    half = many // 2
    net = PlaneReduce(
        kv_sems,
        t,
        lambda p: dkv.at[p],
        lambda p, i: dkv.at[p, pl.ds(i * half, half)],
        lambda k: kv_land.at[k],
        lambda k, i: kv_land.at[k, pl.ds(i * half, half)],
        lambda k: kv_half.at[k],
    )
    out_terms = dot(att[...], mixed, 1, 0)
    quarter = o_part.shape[2]
    wide = model // 2
    for c in range(2):
        for p in range(PLANE):
            for i in range(quarter):
                piece = o_part.at[c, p, i]
                if i * 8 < share:
                    start = p * share + i * 8
                    piece[...] = out_terms[
                        start : start + 8, c * wide : (c + 1) * wide
                    ].astype(BF16)
                else:
                    piece[...] = jnp.zeros(piece.shape, BF16)
    order = (t.zxf, t.zxm, t.zxp, t.xf, t.zo, t.xm, t.xp, t.me)
    pair = Wire(core_sems)
    pair.go(16, o_part.at[1 - t.core], o_core, buddy)
    o_mine = o_part.at[t.core]
    o_net = PlaneReduce(
        o_sems,
        t,
        lambda p: o_mine.at[p],
        lambda p, i: o_mine.at[p, pl.ds(2 * i, 2)],
        lambda k: o_land.at[k],
        lambda k, i: o_land.at[k, pl.ds(2 * i, 2)],
        lambda k: o_half.at[k],
    )
    backward(t.zxf)
    net.far()
    backward(t.zxm)
    net.left()
    backward(t.zxp)
    net.right()
    backward(t.xf)
    net.opposite(0)
    pair.got(16)
    o_net.add(o_mine, o_core)
    o_net.far()
    backward(t.xm)
    net.opposite(1)
    o_net.left()
    o_net.right()
    backward(t.xp)
    net.early()
    o_net.early()
    backward(t.zo)
    net.across()
    net.near()
    o_net.opposite(0)
    o_net.opposite(1)
    o_net.across()
    backward(t.me)
    o_net.near()
    for h in range(HEADS):
        proj[:, h * HD : (h + 1) * HD] = (dqt[h, 0:HD, :] * HD**-0.5).T.astype(BF16)

    proj[:, width:] = net.finish().astype(BF16)

    weights = wq[...].reshape(model, 3 * width)

    def product(y):
        here = proj[pl.ds(pl.multiple_of(y * rows, rows), rows), :]
        part2[y] = dot(here, weights, 1, 1).astype(BF16)

    red = ColumnReduce(red_sems, t, part2, relays2, lands2)
    product(t.yf)
    red.far()
    half_rows = w_part.shape[3]
    hidden = hid[...].reshape(many, model)
    w_terms = dot(hidden, proj[...], 0, 0).reshape(GROUPS, PLANE, 2, half_rows, 3 * width)
    for c in range(2):
        w_part[c] = w_terms[:, :, c].astype(BF16)
    for k, p in enumerate(order):
        pair.go(8 + k, w_part.at[1 - t.core, :, p], w_core.at[:, p], buddy)
    product(t.ym)
    product(t.yp)
    red.near()
    w_mine = w_part.at[t.core]
    w_net = PlaneReduce(
        w_sems,
        t,
        lambda p: w_mine.at[:, p],
        lambda p, i: w_mine.at[pl.ds(2 * i, 2), p],
        lambda k: w_land.at[k],
        lambda k, i: w_land.at[k, pl.ds(2 * i, 2)],
        lambda k: w_half.at[k],
    )

    def join(first, last):
        for k in range(first, last):
            p = order[k]
            pair.got(8 + k)
            w_net.add(w_mine.at[:, p], w_core.at[:, p])

    join(0, 1)
    w_net.far()
    join(1, 2)
    w_net.left()
    join(2, 3)
    w_net.right()
    product(t.y)
    red.relay()
    join(3, 4)
    w_net.opposite(0)
    w_net.opposite(1)
    join(4, 7)
    w_net.early()
    o_mine[t.me] = o_net.finish().astype(BF16)
    o_hi_net = Wire(o_hi_sems)
    for k in range(1, 4):
        j = (t.hi + k) % 4
        o_hi_net.go(k - 1, o_mine.at[t.me, j], o_hi.at[k - 1], {"dp": j * 2 + t.core})
    join(7, 8)
    w_net.across()
    w_net.near()

    grad_hidden = red.finish()
    _, normed, inverse = layer_norm(frames[...].astype(F32), gain1)
    norm_grad, gain_sum = norm_back(grad_hidden, normed, inverse, gain1)
    grad_input[...] = (mix[t.y].astype(F32) + norm_grad).astype(BF16)
    gains = (gain_sum[None], gain2_grad)
    count = s_send.shape[0]
    for r in range(count):
        if r < 2 * (model // 128):
            row, col = divmod(r, model // 128)
            s_send[r, :, model:] = gains[row][:, col * 128 : (col + 1) * 128]
        else:
            s_send[r, :, model:] = jnp.zeros((1, 128), F32)
    s_net = Wire(s_sems)
    s_seq[t.seq] = s_send[t.seq]
    for k in range(1, count):
        r = (t.seq + k) % count
        s_net.go(k - 1, s_send.at[r], s_seq.at[t.seq], {"seq": r})

    o_hi_net.got(0, 1, 2)
    o_out_block = o_mine[t.me, t.hi].astype(F32)
    for k in range(3):
        o_out_block = o_out_block + o_hi[k].astype(F32)
    o_done[...] = o_out_block.astype(BF16)
    finals = []

    def deliver(src, dst, send, recv, y):
        for k in range(1, 8):
            copy = pltpu.make_async_remote_copy(
                src_ref=src,
                dst_ref=dst,
                send_sem=send.at[k],
                recv_sem=recv,
                device_id=t.holder(y, (t.dp + k) % 8),
            )
            copy.start()
            finals.append(copy)

    deliver(o_done, o_fin.at[t.hi, t.core], o_fin_send, o_fin_recv.at[t.hi, t.core], t.y)
    w_mine[:, t.me] = w_net.finish().astype(BF16)
    hi_net = Wire(hi_sems)
    for k in range(1, 4):
        j = (t.hi + k) % 4
        there = {"dp": j * 2 + t.core}
        hi_net.go(k - 1, w_mine.at[j, t.me], w_hi.at[k - 1], there)

    s_net.got(*range(count - 1))
    s_mine[...] = jnp.sum(s_seq[...], axis=0)
    s_dp[t.dp] = s_mine[...]
    s_dp_net = Wire(s_dp_sems)
    for k in range(1, 8):
        s_dp_net.go(k - 1, s_mine, s_dp.at[t.dp], {"dp": (t.dp + k) % 8})

    hi_net.got(*range(3))
    w_out_block = w_mine[t.hi, t.me].astype(F32)
    for k in range(3):
        w_out_block = w_out_block + w_hi[k].astype(F32)
    w_done[...] = w_out_block.astype(BF16)
    deliver(w_done, w_fin.at[t.y, t.core], w_fin_send, w_fin_recv.at[t.y, t.core], t.hi)
    o_own = pltpu.make_async_copy(
        o_done, o_fin.at[t.hi, t.core], o_fin_recv.at[t.hi, t.core]
    )
    o_own.start()
    w_own = pltpu.make_async_copy(w_done, w_fin.at[t.y, t.core], w_fin_recv.at[t.y, t.core])
    w_away = pltpu.make_async_remote_copy(
        src_ref=w_done,
        dst_ref=w_fin.at[t.y, t.core],
        send_sem=w_fin_send.at[0],
        recv_sem=w_fin_recv.at[t.y, t.core],
        device_id=t.holder(t.hi, t.dp),
    )

    @pl.when(t.hi == t.y)
    def _():
        w_own.start()

    @pl.when(t.hi != t.y)
    def _():
        w_away.start()

    s_dp_net.got(*range(7))
    summed = s_dp[0]
    for d in range(1, 8):
        summed = summed + s_dp[d]
    s_done[...] = summed
    s_fin[t.seq] = summed
    s_fin_net = Wire(s_fin_sems)
    for k in range(1, count):
        s_fin_net.go(k - 1, s_done, s_fin.at[t.seq], {"seq": (t.seq + k) % count})

    for i in range(4):
        for c in range(2):
            pltpu.make_async_copy(w_done, w_fin.at[i, c], w_fin_recv.at[i, c]).wait()
            pltpu.make_async_copy(o_done, o_fin.at[i, c], o_fin_recv.at[i, c]).wait()
    pieces = [w_fin[y].astype(F32).reshape(2 * half_rows, 3 * width) for y in range(GROUPS)]
    columns = [piece[:, :width] for piece in pieces]
    for kind in range(2):
        for piece in pieces:
            for h in range(HEADS):
                start = width + (2 * h + kind) * HD
                columns.append(piece[:, start : start + HD])
    grad_qkv[...] = jnp.concatenate(columns, axis=1).astype(BF16)
    sides = [
        o_fin[0 : share // 8, c].astype(F32).reshape(share, wide) for c in range(2)
    ]
    grad_out[...] = jnp.concatenate(sides, axis=1).astype(BF16)
    s_fin_net.got(*range(count - 1))
    for r in range(count):
        row = s_fin[r]
        if r < taps:
            kernel_sum[r : r + 1, :] = row[:, :model]
        else:
            bias_sum[...] = row[:, :model]
        if r < 2 * (model // 128):
            i, col = divmod(r, model // 128)
            norms_sum[i : i + 1, col * 128 : (col + 1) * 128] = row[:, model:]
    for copy in finals:
        copy.wait_send()

    @pl.when(t.hi != t.y)
    def _():
        w_away.wait_send()

    @pl.when(holds)
    def _():
        for copy, _ in spread_copies:
            copy.wait_send()

    for wire in (swap, hid_net, wq_net, wo_net, kv_net, sum_net, mix_net, net, pair, o_net, red, w_net, hi_net, o_hi_net, s_net, s_dp_net, s_fin_net):
        wire.done()


def bf16(*shape):
    return pltpu.VMEM(shape, BF16)


def f32(*shape):
    return pltpu.VMEM(shape, F32)


def dma(*shape):
    return pltpu.SemaphoreType.DMA(shape)


def whole(frames, w_qkv, w_out, gains, conv_kernel, conv_bias, out_grad):
    rows, model = frames.shape
    shard = w_qkv.shape[0]
    many = GROUPS * rows
    width = HEADS * HD
    half = shard // 2
    padded = 32
    count = conv_kernel.shape[0] + 1
    like = jax.ShapeDtypeStruct
    ins = dict(
        frames=frames,
        w_qkv=w_qkv,
        w_out=w_out,
        gains_in=gains,
        conv_kernel=conv_kernel,
        conv_bias=conv_bias,
        out_grad=out_grad,
    )
    outs = dict(
        block_out=like((rows, model), BF16),
        grad_input=like((rows, model), BF16),
        grad_qkv=like(w_qkv.shape, BF16),
        grad_out=like(w_out.shape, BF16),
        kernel_sum=like((count - 1, model), F32),
        bias_sum=like((1, model), F32),
        norms_sum=like((2, model), F32),
    )
    scratch = dict(
        w_parts=bf16(GROUPS, shard, 3 * width),
        hid=bf16(GROUPS, rows, model),
        wq=bf16(GROUPS, PLANE, shard, 3 * width),
        wo=bf16(PLANE, padded, model),
        wo32=f32(width, model),
        wo16=bf16(width, model),
        kv=bf16(PLANE, many, 2 * width),
        qpad=bf16(HEADS, many, 2 * HD),
        lse=f32(HEADS, 1, many),
        total=f32(HEADS, 1, many),
        acc=f32(HEADS, 2 * HD, many),
        att=bf16(width, many),
        probs=bf16(PLANE, HEADS, many, many),
        part=bf16(GROUPS, rows, model),
        relays=bf16(2, rows // 2, model),
        lands=bf16(2, rows, model),
        mixed_keep=f32(rows, model),
        normed_keep=f32(rows, model),
        conv_wide=bf16(rows + 2 * HALO, model),
        grad_wide=bf16(rows + 2 * HALO, model),
        conv_back=f32(rows, model),
        mix=bf16(GROUPS, rows, model),
        dopad=bf16(HEADS, many, 2 * HD),
        delta=f32(HEADS, 1, many),
        dqt=f32(HEADS, 2 * HD, many),
        dkv=bf16(PLANE, many, 2 * width),
        kv_land=bf16(6, many, 2 * width),
        kv_half=bf16(2, many // 2, 2 * width),
        proj=bf16(many, 3 * width),
        part2=bf16(GROUPS, rows, model),
        relays2=bf16(2, rows // 2, model),
        lands2=bf16(2, rows, model),
        w_part=bf16(2, GROUPS, PLANE, half, 3 * width),
        w_core=bf16(GROUPS, PLANE, half, 3 * width),
        w_land=bf16(6, GROUPS, half, 3 * width),
        w_half=bf16(2, GROUPS // 2, half, 3 * width),
        w_hi=bf16(3, half, 3 * width),
        w_done=bf16(half, 3 * width),
        w_fin=bf16(GROUPS, 2, half, 3 * width),
        o_part=bf16(2, PLANE, 4, 8, model // 2),
        o_core=bf16(PLANE, 4, 8, model // 2),
        o_land=bf16(6, 4, 8, model // 2),
        o_half=bf16(2, 2, 8, model // 2),
        o_hi=bf16(3, 8, model // 2),
        o_done=bf16(8, model // 2),
        o_fin=bf16(4, 2, 8, model // 2),
        s_send=f32(count, 1, model + LANES),
        s_seq=f32(count, 1, model + LANES),
        s_mine=f32(1, model + LANES),
        s_dp=f32(8, 1, model + LANES),
        s_done=f32(1, model + LANES),
        s_fin=f32(count, 1, model + LANES),
        spread_sems=wire_sems(3),
        swap_sems=wire_sems(PLANE),
        hid_sems=wire_sems(4),
        wq_sems=wire_sems(9),
        wo_sems=wire_sems(9),
        gather_sems=wire_sems(9),
        sum_sems=wire_sems(6),
        conv_sems=wire_sems(2),
        grad_sems=wire_sems(2),
        mix_sems=wire_sems(4),
        kv_sems=wire_sems(11),
        red_sems=wire_sems(6),
        core_sems=wire_sems(17),
        w_sems=wire_sems(11),
        o_sems=wire_sems(11),
        hi_sems=wire_sems(3),
        o_hi_sems=wire_sems(3),
        w_fin_send=dma(8),
        w_fin_recv=dma(4, 2),
        o_fin_send=dma(8),
        o_fin_recv=dma(4, 2),
        s_sems=wire_sems(count - 1),
        s_dp_sems=wire_sems(7),
        s_fin_sems=wire_sems(count - 1),
    )
    vmem = pl.BlockSpec(memory_space=pltpu.VMEM)
    names = [*ins, *outs, *scratch]
    return pl.pallas_call(
        functools.partial(whole_kernel, names),
        out_shape=list(outs.values()),
        in_specs=[vmem] * len(ins),
        out_specs=[vmem] * len(outs),
        scratch_shapes=list(scratch.values()),
        compiler_params=pltpu.CompilerParams(
            collective_id=0, has_side_effects=True, vmem_limit_bytes=62 * 2**20
        ),
        name="whole",
    )(*ins.values())


def hand_on_kernel(*refs):
    half = len(refs) // 2
    for src, dst in zip(refs[:half], refs[half:]):
        dst[...] = src[...].reshape(dst.shape)


def hand_on(*arrays):
    vmem = pl.BlockSpec(memory_space=pltpu.VMEM)
    return pl.pallas_call(
        hand_on_kernel,
        out_shape=[
            jax.ShapeDtypeStruct(a.shape[1:] if a.shape[0] == 1 else a.shape, a.dtype) for a in arrays
        ],
        in_specs=[vmem] * len(arrays),
        out_specs=[vmem] * len(arrays),
        name="hand_on",
    )(*arrays)


def local(frames, w_qkv, w_out, norm_gains, conv_kernel, conv_bias, out_grad):
    block_out, grad_input, grad_qkv, grad_out, kernel_sum, bias_sum, norms_sum = hand_on(
        *whole(
            frames[0], w_qkv, w_out, norm_gains, conv_kernel, conv_bias, out_grad[0]
        )
    )
    return (
        block_out[None],
        grad_input[None],
        grad_qkv,
        grad_out,
        norms_sum,
        kernel_sum,
        bias_sum,
    )


def solution(mesh):
    in_specs = (
        P("dp", "seq", None),
        P("seq", None),
        P("seq", None),
        P(),
        P(),
        P(),
        P("dp", "seq", None),
    )
    out_specs = (
        P("dp", "seq", None),
        P("dp", "seq", None),
        P("seq", None),
        P("seq", None),
        P(),
        P(),
        P(),
    )
    return jax.shard_map(local, mesh=mesh, in_specs=in_specs, out_specs=out_specs, check_vma=False)
```

```python
import functools

import jax
import jax.numpy as jnp
from jax import lax
from jax.experimental import pallas as pl
from jax.experimental.pallas import tpu as pltpu
from jax.sharding import PartitionSpec as P

EPS = 1e-05
GROUPS = 4
PLANE = 8
HEADS = 3
HD = 64
F32 = jnp.float32
BF16 = jnp.bfloat16


def layer_norm(values, gain):
    center = values - jnp.mean(values, axis=-1, keepdims=True)
    spread = jnp.mean(center * center, axis=-1, keepdims=True)
    inverse = lax.rsqrt(spread + EPS)
    normed = center * inverse
    return (normed * gain, normed, inverse)


def norm_back(grad, normed, inverse, gain):
    scaled = grad * gain
    inner = (
        scaled
        - jnp.mean(scaled, axis=-1, keepdims=True)
        - normed * jnp.mean(scaled * normed, axis=-1, keepdims=True)
    )
    return (inverse * inner, jnp.sum(grad * normed, axis=0))


def dot(a, b, ca, cb):
    return lax.dot_general(a, b, (((ca,), (cb,)), ((), ())), preferred_element_type=F32)


class Place:
    def __init__(self):
        seq = lax.axis_index("seq")
        y, z, x = seq // 8, (seq // 4) % 2, seq % 4
        right, left, far, other = (x + 1) % 4, (x + 3) % 4, (x + 2) % 4, 1 - z
        self.y, self.yp, self.ym, self.yf = y, (y + 1) % 4, (y + 3) % 4, (y + 2) % 4
        self.me = z * 4 + x
        self.xp, self.xm, self.xf = z * 4 + right, z * 4 + left, z * 4 + far
        self.zo = other * 4 + x
        self.zxp, self.zxm, self.zxf = other * 4 + right, other * 4 + left, other * 4 + far

        self.seq, self.dp = seq, lax.axis_index("dp")
        self.core, self.hi = self.dp % 2, self.dp // 2

    def plane(self, p):
        return {"seq": self.y * 8 + p}

    def holder(self, y, dp):
        return {"seq": y * 8 + self.me, "dp": dp}

    def greet(self):
        near = [{"seq": (self.seq + i) % 32} for i in range(1, 32)]
        near += [self.holder(self.y, (self.dp + j) % 8) for j in range(1, 8)]
        near += [
            self.holder((self.y + i) % 4, ((self.hi + j) % 4) * 2 + self.core)
            for i in range(1, 4)
            for j in range(1, 4)
        ]
        for device in near:
            pl.semaphore_signal(pltpu.get_barrier_semaphore(), inc=1, device_id=device)
        return len(near)

    def column(self, y):
        return {"seq": y * 8 + self.me}


class Wire:
    def __init__(self, sems):
        self.sems, self.sent = sems, {}

    def go(self, k, src, dst, device):
        copy = pltpu.make_async_remote_copy(
            src_ref=src,
            dst_ref=dst,
            send_sem=self.sems.at[0, k],
            recv_sem=self.sems.at[1, k],
            device_id=device,
        )
        copy.start()
        self.sent[k] = copy

    def got(self, *ks):
        for k in ks:
            self.sent[k].wait_recv()

    def done(self):
        for copy in self.sent.values():
            copy.wait_send()


def wire_sems(count):
    return pltpu.SemaphoreType.DMA((2, count))


class ColumnGather(Wire):
    def __init__(self, sems, place, buf):
        super().__init__(sems)
        self.at, self.buf = place, buf
        self.half = buf.shape[1] // 2

    def begin(self):
        t, own = self.at, self.buf.at[self.at.y]
        self.go(0, own, own, t.column(t.yp))
        self.go(1, own, own, t.column(t.ym))

    def relay(self):
        t, h = self.at, self.half
        self.got(0)
        first = self.buf.at[t.ym, pl.ds(0, h)]
        self.go(2, first, first, t.column(t.yp))
        self.got(1)
        second = self.buf.at[t.yp, pl.ds(h, h)]
        self.go(3, second, second, t.column(t.ym))

    def finish(self):
        self.got(2, 3)


class ColumnReduce(Wire):
    def __init__(self, sems, place, part, relays, lands):
        super().__init__(sems)
        self.at, self.part, self.relays, self.lands = place, part, relays, lands
        self.half = part.shape[1] // 2

    def far(self):
        t, h = self.at, self.half
        self.go(0, self.part.at[t.yf, pl.ds(0, h)], self.relays.at[0], t.column(t.ym))
        self.go(1, self.part.at[t.yf, pl.ds(h, h)], self.relays.at[1], t.column(t.yp))

    def near(self):
        t, h = self.at, self.half
        low, high = pl.ds(0, h), pl.ds(h, h)
        self.go(2, self.part.at[t.ym, high], self.lands.at[0, high], t.column(t.ym))
        self.go(3, self.part.at[t.yp, low], self.lands.at[1, low], t.column(t.yp))

    def relay(self):
        t, h = self.at, self.half
        low, high = pl.ds(0, h), pl.ds(h, h)
        self.got(0)
        self.part[t.ym, low] = (
            self.part[t.ym, low].astype(F32) + self.relays[0].astype(F32)
        ).astype(BF16)
        self.go(4, self.part.at[t.ym, low], self.lands.at[0, low], t.column(t.ym))
        self.got(1)
        self.part[t.yp, high] = (
            self.part[t.yp, high].astype(F32) + self.relays[1].astype(F32)
        ).astype(BF16)
        self.go(5, self.part.at[t.yp, high], self.lands.at[1, high], t.column(t.yp))

    def finish(self):
        self.got(2, 3, 4, 5)
        return (
            self.part[self.at.y].astype(F32)
            + self.lands[0].astype(F32)
            + self.lands[1].astype(F32)
        )


class PlaneGather(Wire):
    def __init__(self, sems, place, full, half):
        super().__init__(sems)
        self.at, self.full, self.half = place, full, half

    def begin(self):
        t, own = self.at, self.full(self.at.me)
        self.go(0, own, own, t.plane(t.xp))
        self.go(1, own, own, t.plane(t.xm))
        self.go(2, own, own, t.plane(t.zo))

    def relay(self):
        t = self.at
        self.got(0)
        first = self.half(t.xm, 0)
        self.go(3, first, first, t.plane(t.xp))
        self.got(1)
        second = self.half(t.xp, 1)
        self.go(4, second, second, t.plane(t.xm))
        self.got(2)
        other = self.full(t.zo)
        self.go(5, other, other, t.plane(t.xp))
        self.go(6, other, other, t.plane(t.xm))

    def cross(self):
        t = self.at
        for k in (0, 1):
            self.got(3 + k)
            part = self.half(t.xf, k)
            self.go(7 + k, part, part, t.plane(t.zo))

    def finish(self):
        self.got(5, 6, 7, 8)


class PlaneReduce(Wire):
    def __init__(self, sems, place, full, half, land, land_half, half_land):
        super().__init__(sems)
        self.at, self.full, self.half = place, full, half
        self.land, self.land_half, self.half_land = land, land_half, half_land

    def add(self, ref, *more):
        total = ref[...].astype(F32)
        for other in more:
            total = total + other[...].astype(F32)
        ref[...] = total.astype(BF16)

    def far(self):
        t = self.at
        self.go(0, self.half(t.zxf, 0), self.land_half(0, 0), t.plane(t.zo))
        self.go(8, self.half(t.zxf, 1), self.land_half(0, 1), t.plane(t.zo))

    def left(self):
        self.go(1, self.full(self.at.zxm), self.land(1), self.at.plane(self.at.xm))

    def right(self):
        self.go(2, self.full(self.at.zxp), self.land(2), self.at.plane(self.at.xp))

    def opposite(self, i):
        t = self.at
        self.got((0, 8)[i])
        self.add(self.half(t.xf, i), self.land_half(0, i))
        self.go(3 + i, self.half(t.xf, i), self.half_land(i), t.plane((t.xm, t.xp)[i]))

    def early(self):
        t = self.at
        self.go(6, self.half(t.xm, 1), self.land_half(4, 1), t.plane(t.xm))
        self.go(7, self.half(t.xp, 0), self.land_half(5, 0), t.plane(t.xp))

    def across(self):
        t = self.at
        self.got(1, 2)
        self.add(self.full(t.zo), self.land(1), self.land(2))
        self.go(5, self.full(t.zo), self.land(3), t.plane(t.zo))

    def near(self):
        t = self.at
        self.got(3)
        self.add(self.half(t.xm, 0), self.half_land(0))
        self.go(9, self.half(t.xm, 0), self.land_half(4, 0), t.plane(t.xm))
        self.got(4)
        self.add(self.half(t.xp, 1), self.half_land(1))
        self.go(10, self.half(t.xp, 1), self.land_half(5, 1), t.plane(t.xp))

    def finish(self):
        self.got(5, 6, 7, 9, 10)
        total = self.full(self.at.me)[...].astype(F32)
        for k in (3, 4, 5):
            total = total + self.land(k)[...].astype(F32)
        return total


def pick(i, *values):
    out = values[-1]
    for k in range(len(values) - 2, -1, -1):
        out = jnp.where(i == k, values[k], out)
    return out


def local_copies(pairs, sems):
    copies = [
        pltpu.make_async_copy(src, dst, sems.at[i]) for i, (src, dst) in enumerate(pairs)
    ]
    for copy in copies:
        copy.start()
    return copies


QB = 128


def forward_block(kv, c, h, cols, qpad, top, total, acc):
    both = kv[c, :, h * 128 : (h + 1) * 128]
    scores = dot(both, qpad[h, cols, :], 1, 1)
    old = top[h, :, cols]
    new = jnp.maximum(old, jnp.max(scores, axis=0, keepdims=True))
    shrink = jnp.exp(old - new)
    expo = jnp.exp(scores - new)
    top[h, :, cols] = new
    total[h, :, cols] = total[h, :, cols] * shrink + jnp.sum(expo, axis=0, keepdims=True)
    acc[h, :, cols] = acc[h, :, cols] * shrink + dot(both, expo.astype(BF16), 0, 0)


def forward_chunk(kv, c, qpad, top, total, acc):
    for h in range(HEADS):
        for b in range(qpad.shape[1] // QB):
            forward_block(kv, c, h, slice(b * QB, (b + 1) * QB), qpad, top, total, acc)


def prob_chunk(kv, c, qpad, lse, probs):
    for h in range(HEADS):
        scores = dot(kv[c, :, h * 128 : (h + 1) * 128], qpad[h], 1, 1)
        probs[c, h] = jnp.exp(scores - lse[h]).astype(BF16)


def backward_chunk(kv, c, qpad, dopad, probs, delta, dqt, out):
    for h in range(HEADS):
        lanes = slice(h * 128, (h + 1) * 128)
        both, query, grad = kv[c, :, lanes], qpad[h], dopad[h]
        slopes = dot(both, grad, 1, 1)
        prob = probs[c, h]
        score_grads = (prob.astype(F32) * (slopes - delta[h])).astype(BF16)
        out[c, :, lanes] = (
            dot(prob, grad, 1, 0) + dot(score_grads, query, 1, 0)
        ).astype(BF16)
        dqt[h] += dot(both, score_grads, 0, 0)


HALO = 16
LANES = 128


def shifts(wide, length, taps):
    for low in range(8):
        moved = wide if low == 0 else pltpu.roll(wide, wide.shape[0] - low, 0)
        for offset in range(low, taps + 1, 8):
            if offset > 0:
                yield offset, moved[offset - low : offset - low + length]


class Edge(Wire):
    def __init__(self, sems, place, wide):
        super().__init__(sems)
        t, rows = place, wide.shape[0]
        self.first, self.last = t.seq == 0, t.seq == 31
        nothing = jnp.zeros((HALO, wide.shape[1]), BF16)

        @pl.when(self.first)
        def _():
            wide[0:HALO] = nothing

        @pl.when(self.last)
        def _():
            wide[rows - HALO :] = nothing

        self.up = pltpu.make_async_remote_copy(
            src_ref=wide.at[pl.ds(rows - 2 * HALO, HALO)],
            dst_ref=wide.at[pl.ds(0, HALO)],
            send_sem=sems.at[0, 0],
            recv_sem=sems.at[1, 0],
            device_id={"seq": jnp.minimum(t.seq + 1, 31)},
        )
        self.down = pltpu.make_async_remote_copy(
            src_ref=wide.at[pl.ds(HALO, HALO)],
            dst_ref=wide.at[pl.ds(rows - HALO, HALO)],
            send_sem=sems.at[0, 1],
            recv_sem=sems.at[1, 1],
            device_id={"seq": jnp.maximum(t.seq - 1, 0)},
        )

    def begin(self):
        @pl.when(jnp.logical_not(self.last))
        def _():
            self.up.start()

        @pl.when(jnp.logical_not(self.first))
        def _():
            self.down.start()

    def finish(self):
        @pl.when(jnp.logical_not(self.last))
        def _():
            self.up.wait_send()
            self.down.wait_recv()

        @pl.when(jnp.logical_not(self.first))
        def _():
            self.down.wait_send()
            self.up.wait_recv()


def whole_kernel(names, *refs):
    r = dict(zip(names, refs))
    (
        frames,
        w_qkv,
        w_out,
        gains_in,
        conv_kernel,
        conv_bias,
        out_grad,
        block_out,
        grad_input,
        grad_qkv,
        grad_out,
        kernel_sum,
        bias_sum,
        norms_sum,
        w_parts,
        hid,
        wq,
        wo,
        wo32,
        wo16,
        kv,
        qpad,
        lse,
        total,
        acc,
        att,
        probs,
        part,
        relays,
        lands,
        mixed_keep,
        normed_keep,
        first_keep,
        conv_wide,
        grad_wide,
        conv_back,
        mix,
        dopad,
        delta,
        dqt,
        dkv,
        kv_land,
        kv_half,
        proj,
        part2,
        relays2,
        lands2,
        w_part,
        w_core,
        w_land,
        w_half,
        w_hi,
        w_done,
        w_fin,
        o_part,
        o_core,
        o_land,
        o_half,
        o_hi,
        o_done,
        o_fin,
        s_send,
        s_seq,
        s_mine,
        s_dp,
        s_done,
        s_fin,
        spread_sems,
        swap_sems,
        hid_sems,
        wq_sems,
        wo_sems,
        gather_sems,
        sum_sems,
        conv_sems,
        grad_sems,
        mix_sems,
        kv_sems,
        red_sems,
        core_sems,
        w_sems,
        o_sems,
        hi_sems,
        o_hi_sems,
        cross_sems,
        w_fin_send,
        w_fin_recv,
        o_fin_send,
        o_fin_recv,
        s_sems,
        s_dp_sems,
        s_fin_sems,
    ) = (r[n] for n in names)
    t = Place()
    greeted = t.greet()
    rows, model = frames.shape
    many = GROUPS * rows
    width = HEADS * HD
    shard = w_qkv.shape[0]
    gain1, gain2 = gains_in[0:1, :], gains_in[1:2, :]

    for g in range(GROUPS):
        columns = [w_qkv[:, g * width : (g + 1) * width]]
        for h in range(HEADS):
            for kind in (1, 2):
                start = (kind * GROUPS + g) * width + h * HD
                columns.append(w_qkv[:, start : start + HD])
        w_parts[g] = jnp.concatenate(columns, axis=1)
    inputs = frames[...].astype(F32)
    shifted, normed, inverse1 = layer_norm(inputs, gain1)
    first_keep[...] = normed
    hid[t.y] = shifted.astype(BF16)
    pl.semaphore_wait(pltpu.get_barrier_semaphore(), greeted)
    hid_net = ColumnGather(hid_sems, t, hid)
    hid_net.begin()
    holds = t.y // 2 == t.core
    spread_copies = []
    for k in range(1, GROUPS):
        y = (t.y + k) % GROUPS
        copy = pltpu.make_async_remote_copy(
            src_ref=w_parts.at[y],
            dst_ref=wq.at[t.y, t.me],
            send_sem=spread_sems.at[0, k - 1],
            recv_sem=spread_sems.at[1, k - 1],
            device_id=t.column(y),
        )
        spread_copies.append((copy, ((t.y + GROUPS - k) % GROUPS) // 2 == t.core))

    @pl.when(holds)
    def _():
        for copy, _ in spread_copies:
            copy.start()
        wq[t.y, t.me] = w_parts[t.y]

    share = width // PLANE
    wide = model // 2
    for c in range(2):

        @pl.when(t.core == c)
        def _(c=c):
            wo[c, t.me] = w_out[:, c * wide : (c + 1) * wide]


    for copy, comes in spread_copies:
        pl.when(comes)(copy.wait_recv)
    base = 2 * t.core
    wq_net = PlaneGather(
        wq_sems, t, lambda p: wq.at[pl.ds(base, 2), p], lambda p, i: wq.at[base + i, p]
    )
    swap = Wire(swap_sems)
    buddy = {"dp": t.hi * 2 + 1 - t.core}

    def trade(*ps):
        for p in ps:
            half = wq.at[pl.ds(base, 2), p]
            swap.go(len(swap.sent), half, half, buddy)
    wo_net = PlaneGather(
        wo_sems,
        t,
        lambda p: wo.at[t.core, p],
        lambda p, i: wo.at[t.core, p, :, pl.ds(i * (wide // 2), wide // 2)],
    )
    wq_net.begin()
    trade(t.me)
    wq_net.relay()
    trade(t.xm, t.xp, t.zo)
    hid_net.relay()
    wq_net.cross()
    trade(t.xf)
    wo_net.begin()
    wq_net.finish()
    trade(t.zxm, t.zxp, t.zxf)
    hid_net.finish()
    swap.got(*range(PLANE))

    hidden = hid[...].reshape(many, model)
    weights = wq[...].reshape(model, 3 * width)
    projected = dot(hidden, weights, 1, 0).astype(BF16)
    kv[t.me] = projected[:, width:]
    kv_net = PlaneGather(
        gather_sems,
        t,
        lambda p: kv.at[p],
        lambda p, i: kv.at[p, pl.ds(i * (many // 2), many // 2)],
    )
    kv_net.begin()
    zeros = jnp.zeros((many, HD), BF16)
    for h in range(HEADS):
        qpad[h] = jnp.concatenate(
            [projected[:, h * HD : (h + 1) * HD] * BF16(HD**-0.5), zeros], axis=1
        )
    lse[...] = jnp.full_like(lse, -jnp.inf)
    total[...] = jnp.zeros_like(total)
    acc[...] = jnp.zeros_like(acc)

    def attend(*chunks):
        if len(chunks) == 1:
            forward_chunk(kv, chunks[0], qpad, lse, total, acc)
            return

        def step(i, carry):
            forward_chunk(kv, pick(i, *chunks), qpad, lse, total, acc)
            return carry

        lax.fori_loop(0, len(chunks), step, 0)

    attend(t.me)
    kv_net.relay()
    wo_net.relay()
    attend(t.xm, t.xp, t.zo)
    kv_net.cross()
    wo_net.cross()
    attend(t.xf)
    wo_net.finish()
    swap.go(PLANE, wo.at[t.core], wo.at[t.core], buddy)
    swap.got(PLANE)
    for p in range(PLANE):
        for c in range(2):
            wo32[p * share : (p + 1) * share, c * wide : (c + 1) * wide] = wo[c, p].astype(F32)
    wo16[...] = wo32[...].astype(BF16)
    kv_net.got(5, 6)
    kv_net.got(7, 8)

    def last(y):
        cols = pl.ds(pl.multiple_of(y * rows, rows), rows)

        for c in (t.zxm, t.zxp, t.zxf):
            for h in range(HEADS):
                forward_block(kv, c, h, cols, qpad, lse, total, acc)
        for h in range(HEADS):
            att[h * HD : (h + 1) * HD, cols] = (
                acc[h, HD : 2 * HD, cols] / total[h, :, cols]
            ).astype(BF16)
            lse[h, :, cols] = lse[h, :, cols] + jnp.log(total[h, :, cols])
        part[y] = dot(att[:, cols], wo16[...], 0, 0).astype(BF16)

    sum_net = ColumnReduce(sum_sems, t, part, relays, lands)
    last(t.yf)
    sum_net.far()
    last(t.ym)
    last(t.yp)
    sum_net.near()
    last(t.y)
    sum_net.relay()

    def foresee(*chunks):
        def step(i, carry):
            prob_chunk(kv, pick(i, *chunks), qpad, lse, probs)
            return carry

        lax.fori_loop(0, len(chunks), step, 0)

    foresee(t.zxf, t.zxm)
    mixed = (frames[...].astype(F32) + sum_net.finish()).astype(BF16)

    mixed32 = mixed.astype(F32)
    mixed_keep[...] = mixed32
    shifted, normed, inverse = layer_norm(mixed32, gain2)
    inside = slice(HALO, HALO + rows)
    conv_wide[inside] = shifted.astype(BF16)
    conv_edge = Edge(conv_sems, t, conv_wide)
    conv_edge.begin()
    normed_keep[...] = normed
    foresee(t.zxp)
    conv_edge.finish()
    taps = conv_kernel.shape[0]

    def lanes_of(b):
        return pl.ds(pl.multiple_of(b * LANES, LANES), LANES)

    def convolve(b, carry):
        lanes = lanes_of(b)
        pre = jnp.zeros((rows, LANES), F32) + conv_bias[lanes][None]
        for offset, moved in shifts(conv_wide[:, lanes].astype(F32), rows, taps):
            pre = pre + moved * conv_kernel[offset - 1 : offset, lanes]
        sigma = 1.0 / (1.0 + jnp.exp(-pre))
        block_out[:, lanes] = (mixed_keep[:, lanes] + pre * sigma).astype(BF16)
        grad_wide[inside, lanes] = (
            out_grad[:, lanes].astype(F32) * sigma * (1.0 + pre * (1.0 - sigma))
        ).astype(BF16)
        return carry

    blocks = model // LANES
    lax.fori_loop(0, blocks, convolve, 0)
    grad_edge = Edge(grad_sems, t, grad_wide)
    grad_edge.begin()
    foresee(t.xf)
    grad_edge.finish()

    def convolve_back(b, carry):
        lanes = lanes_of(b)
        grad = jnp.zeros((rows, LANES), F32)
        for offset, moved in shifts(grad_wide[:, lanes].astype(F32), rows, taps):
            grad = grad + moved * conv_kernel[taps - offset : taps - offset + 1, lanes]
        conv_back[:, lanes] = grad
        return carry

    lax.fori_loop(0, blocks, convolve_back, 0)
    norm_grad, gain2_grad = norm_back(conv_back[...], normed_keep[...], inverse, gain2)
    gain2_grad = gain2_grad[None]
    mix[t.y] = (out_grad[...].astype(F32) + norm_grad).astype(BF16)
    mix_net = ColumnGather(mix_sems, t, mix)
    mix_net.begin()

    def kernel_grads(b, carry):
        lanes = lanes_of(b)
        grad = grad_wide[inside, lanes].astype(F32)
        for offset, moved in shifts(conv_wide[:, lanes].astype(F32), rows, taps):
            s_send[offset - 1, :, lanes] = jnp.sum(grad * moved, axis=0, keepdims=True)
        s_send[taps, :, lanes] = jnp.sum(grad, axis=0, keepdims=True)
        return carry

    lax.fori_loop(0, blocks, kernel_grads, 0)
    foresee(t.zo, t.xm, t.xp)
    mix_net.relay()
    foresee(t.me)
    mix_net.finish()

    mixed = mix[...].reshape(many, model)
    grads = dot(mixed, wo16[...], 1, 1).astype(BF16)
    grads_turned = dot(wo16[...], mixed, 1, 1).astype(BF16).astype(F32)
    for h in range(HEADS):
        lanes = slice(h * HD, (h + 1) * HD)
        mine = grads[:, lanes]
        dopad[h] = jnp.concatenate([zeros, mine], axis=1)
        delta[h] = jnp.sum(
            att[lanes, :].astype(F32) * grads_turned[lanes, :], axis=0, keepdims=True
        )
    dqt[...] = jnp.zeros_like(dqt)

    def backward(*chunks):
        def step(i, carry):
            backward_chunk(kv, pick(i, *chunks), qpad, dopad, probs, delta, dqt, dkv)
            return carry

        if len(chunks) == 1:
            step(0, 0)
        else:
            lax.fori_loop(0, len(chunks), step, 0)

    half = many // 2
    net = PlaneReduce(
        kv_sems,
        t,
        lambda p: dkv.at[p],
        lambda p, i: dkv.at[p, pl.ds(i * half, half)],
        lambda k: kv_land.at[k],
        lambda k, i: kv_land.at[k, pl.ds(i * half, half)],
        lambda k: kv_half.at[k],
    )
    order = (t.zxf, t.zxm, t.zxp, t.xf, t.zo, t.xm, t.xp, t.me)
    backward(t.zxm)
    net.left()
    backward(t.zxp)
    net.right()
    backward(t.zxf)
    net.far()
    out_terms = dot(att[...], mixed, 1, 0)
    quarter = o_part.shape[2]
    for c in range(2):
        for p in range(PLANE):
            for i in range(quarter):
                piece = o_part.at[c, p, i]
                if i * 8 < share:
                    start = p * share + i * 8
                    piece[...] = out_terms[
                        start : start + 8, c * wide : (c + 1) * wide
                    ].astype(BF16)
                else:
                    piece[...] = jnp.zeros(piece.shape, BF16)
    pair = Wire(core_sems)
    pair.go(16, o_part.at[1 - t.core], o_core, buddy)
    o_mine = o_part.at[t.core]
    o_net = PlaneReduce(
        o_sems,
        t,
        lambda p: o_mine.at[p],
        lambda p, i: o_mine.at[p, pl.ds(2 * i, 2)],
        lambda k: o_land.at[k],
        lambda k, i: o_land.at[k, pl.ds(2 * i, 2)],
        lambda k: o_half.at[k],
    )
    backward(t.xf)
    pair.got(16)
    o_net.add(o_mine, o_core)
    o_net.far()
    o_net.left()
    o_net.right()
    backward(t.xm)
    net.opposite(0)
    backward(t.xp)
    net.early()
    net.opposite(1)
    o_net.early()
    backward(t.zo)
    net.across()
    net.near()
    o_net.opposite(0)
    o_net.opposite(1)
    o_net.across()
    backward(t.me)
    o_net.near()
    for h in range(HEADS):
        proj[:, h * HD : (h + 1) * HD] = (dqt[h, 0:HD, :] * HD**-0.5).T.astype(BF16)

    proj[:, width:] = net.finish().astype(BF16)

    weights = wq[...].reshape(model, 3 * width)

    def product(y):
        here = proj[pl.ds(pl.multiple_of(y * rows, rows), rows), :]
        part2[y] = dot(here, weights, 1, 1).astype(BF16)

    red = ColumnReduce(red_sems, t, part2, relays2, lands2)
    product(t.yf)
    red.far()
    half_rows = w_part.shape[3]
    hidden = hid[...].reshape(many, model)
    w_terms = dot(hidden, proj[...], 0, 0).reshape(GROUPS, PLANE, 2, half_rows, 3 * width)
    for c in range(2):
        w_part[c] = w_terms[:, :, c].astype(BF16)
    for k, p in enumerate(order):
        pair.go(8 + k, w_part.at[1 - t.core, :, p], w_core.at[:, p], buddy)
    product(t.ym)
    product(t.yp)
    red.near()
    w_mine = w_part.at[t.core]
    w_net = PlaneReduce(
        w_sems,
        t,
        lambda p: w_mine.at[:, p],
        lambda p, i: w_mine.at[pl.ds(2 * i, 2), p],
        lambda k: w_land.at[k],
        lambda k, i: w_land.at[k, pl.ds(2 * i, 2)],
        lambda k: w_half.at[k],
    )

    def join(first, last):
        for k in range(first, last):
            p = order[k]
            pair.got(8 + k)
            w_net.add(w_mine.at[:, p], w_core.at[:, p])

    join(0, 1)
    w_net.far()
    join(1, 2)
    w_net.left()
    join(2, 3)
    w_net.right()
    product(t.y)
    red.relay()
    join(3, 4)
    w_net.opposite(0)
    w_net.opposite(1)
    join(4, 7)
    w_net.early()
    o_mine[t.me] = o_net.finish().astype(BF16)
    o_hi_net = Wire(o_hi_sems)
    for k in range(1, 4):
        j = (t.hi + k) % 4
        o_hi_net.go(k - 1, o_mine.at[t.me, j], o_hi.at[k - 1], {"dp": j * 2 + t.core})
    join(7, 8)
    w_net.across()
    w_net.near()

    grad_hidden = red.finish()
    norm_grad, gain_sum = norm_back(grad_hidden, first_keep[...], inverse1, gain1)
    grad_input[...] = (mix[t.y].astype(F32) + norm_grad).astype(BF16)
    gains = (gain_sum[None], gain2_grad)
    count = s_send.shape[0]
    for r in range(count):
        if r < 2 * (model // 128):
            row, col = divmod(r, model // 128)
            s_send[r, :, model:] = gains[row][:, col * 128 : (col + 1) * 128]
        else:
            s_send[r, :, model:] = jnp.zeros((1, 128), F32)
    s_net = Wire(s_sems)
    s_seq[t.seq] = s_send[t.seq]
    for k in range(1, count):
        r = (t.seq + k) % count
        s_net.go(k - 1, s_send.at[r], s_seq.at[t.seq], {"seq": r})

    o_hi_net.got(0, 1, 2)
    o_out_block = o_mine[t.me, t.hi].astype(F32)
    for k in range(3):
        o_out_block = o_out_block + o_hi[k].astype(F32)
    o_done[...] = o_out_block.astype(BF16)
    finals = []

    def deliver(src, dst, send, recv, y):
        for k in range(1, 4):
            copy = pltpu.make_async_remote_copy(
                src_ref=src,
                dst_ref=dst,
                send_sem=send.at[k],
                recv_sem=recv,
                device_id=t.holder(y, ((t.hi + k) % 4) * 2 + t.core),
            )
            copy.start()
            finals.append(copy)

    deliver(o_done, o_fin.at[t.hi, t.core], o_fin_send, o_fin_recv.at[t.hi, t.core], t.y)
    o_own = pltpu.make_async_copy(
        o_done, o_fin.at[t.hi, t.core], o_fin_recv.at[t.hi, t.core]
    )
    o_own.start()
    w_mine[:, t.me] = w_net.finish().astype(BF16)
    hi_net = Wire(hi_sems)
    for k in range(1, 4):
        j = (t.hi + k) % 4
        there = {"dp": j * 2 + t.core}
        hi_net.go(k - 1, w_mine.at[j, t.me], w_hi.at[k - 1], there)

    s_net.got(*range(count - 1))
    s_mine[...] = jnp.sum(s_seq[...], axis=0)
    s_dp[t.dp] = s_mine[...]
    s_dp_net = Wire(s_dp_sems)
    for k in range(1, 8):
        s_dp_net.go(k - 1, s_mine, s_dp.at[t.dp], {"dp": (t.dp + k) % 8})

    hi_net.got(*range(3))
    w_out_block = w_mine[t.hi, t.me].astype(F32)
    for k in range(3):
        w_out_block = w_out_block + w_hi[k].astype(F32)
    w_done[...] = w_out_block.astype(BF16)
    deliver(w_done, w_fin.at[t.y, t.core], w_fin_send, w_fin_recv.at[t.y, t.core], t.hi)
    w_own = pltpu.make_async_copy(w_done, w_fin.at[t.y, t.core], w_fin_recv.at[t.y, t.core])
    w_away = pltpu.make_async_remote_copy(
        src_ref=w_done,
        dst_ref=w_fin.at[t.y, t.core],
        send_sem=w_fin_send.at[0],
        recv_sem=w_fin_recv.at[t.y, t.core],
        device_id=t.holder(t.hi, t.dp),
    )

    @pl.when(t.hi == t.y)
    def _():
        w_own.start()

    @pl.when(t.hi != t.y)
    def _():
        w_away.start()

    s_dp_net.got(*range(7))
    summed = s_dp[0]
    for d in range(1, 8):
        summed = summed + s_dp[d]
    s_done[...] = summed
    s_fin[t.seq] = summed
    s_fin_net = Wire(s_fin_sems)
    for k in range(1, count):
        s_fin_net.go(k - 1, s_done, s_fin.at[t.seq], {"seq": (t.seq + k) % count})

    cross = Wire(cross_sems)
    for i in range(4):
        pltpu.make_async_copy(o_done, o_fin.at[i, t.core], o_fin_recv.at[i, t.core]).wait()
        cross.go(i, o_fin.at[i, t.core], o_fin.at[i, t.core], buddy)
    for i in range(4):
        pltpu.make_async_copy(w_done, w_fin.at[i, t.core], w_fin_recv.at[i, t.core]).wait()
        cross.go(4 + i, w_fin.at[i, t.core], w_fin.at[i, t.core], buddy)
    cross.got(*range(8))
    pieces = [w_fin[y].astype(F32).reshape(2 * half_rows, 3 * width) for y in range(GROUPS)]
    columns = [piece[:, :width] for piece in pieces]
    for kind in range(2):
        for piece in pieces:
            for h in range(HEADS):
                start = width + (2 * h + kind) * HD
                columns.append(piece[:, start : start + HD])
    grad_qkv[...] = jnp.concatenate(columns, axis=1).astype(BF16)
    sides = [
        o_fin[0 : share // 8, c].astype(F32).reshape(share, wide) for c in range(2)
    ]
    grad_out[...] = jnp.concatenate(sides, axis=1).astype(BF16)
    s_fin_net.got(*range(count - 1))
    for r in range(count):
        row = s_fin[r]
        if r < taps:
            kernel_sum[r : r + 1, :] = row[:, :model]
        else:
            bias_sum[...] = row[:, :model]
        if r < 2 * (model // 128):
            i, col = divmod(r, model // 128)
            norms_sum[i : i + 1, col * 128 : (col + 1) * 128] = row[:, model:]
    for copy in finals:
        copy.wait_send()

    @pl.when(t.hi != t.y)
    def _():
        w_away.wait_send()

    @pl.when(holds)
    def _():
        for copy, _ in spread_copies:
            copy.wait_send()

    for wire in (swap, hid_net, wq_net, wo_net, kv_net, sum_net, mix_net, net, pair, o_net, red, w_net, hi_net, o_hi_net, cross, s_net, s_dp_net, s_fin_net):
        wire.done()


def bf16(*shape):
    return pltpu.VMEM(shape, BF16)


def f32(*shape):
    return pltpu.VMEM(shape, F32)


def dma(*shape):
    return pltpu.SemaphoreType.DMA(shape)


def whole(frames, w_qkv, w_out, gains, conv_kernel, conv_bias, out_grad):
    rows, model = frames.shape
    shard = w_qkv.shape[0]
    many = GROUPS * rows
    width = HEADS * HD
    half = shard // 2
    count = conv_kernel.shape[0] + 1
    like = jax.ShapeDtypeStruct
    ins = dict(
        frames=frames,
        w_qkv=w_qkv,
        w_out=w_out,
        gains_in=gains,
        conv_kernel=conv_kernel,
        conv_bias=conv_bias,
        out_grad=out_grad,
    )
    outs = dict(
        block_out=like((rows, model), BF16),
        grad_input=like((rows, model), BF16),
        grad_qkv=like(w_qkv.shape, BF16),
        grad_out=like(w_out.shape, BF16),
        kernel_sum=like((count - 1, model), F32),
        bias_sum=like((1, model), F32),
        norms_sum=like((2, model), F32),
    )
    scratch = dict(
        w_parts=bf16(GROUPS, shard, 3 * width),
        hid=bf16(GROUPS, rows, model),
        wq=bf16(GROUPS, PLANE, shard, 3 * width),
        wo=bf16(2, PLANE, width // PLANE, model // 2),
        wo32=f32(width, model),
        wo16=bf16(width, model),
        kv=bf16(PLANE, many, 2 * width),
        qpad=bf16(HEADS, many, 2 * HD),
        lse=f32(HEADS, 1, many),
        total=f32(HEADS, 1, many),
        acc=f32(HEADS, 2 * HD, many),
        att=bf16(width, many),
        probs=bf16(PLANE, HEADS, many, many),
        part=bf16(GROUPS, rows, model),
        relays=bf16(2, rows // 2, model),
        lands=bf16(2, rows, model),
        mixed_keep=f32(rows, model),
        normed_keep=f32(rows, model),
        first_keep=f32(rows, model),
        conv_wide=bf16(rows + 2 * HALO, model),
        grad_wide=bf16(rows + 2 * HALO, model),
        conv_back=f32(rows, model),
        mix=bf16(GROUPS, rows, model),
        dopad=bf16(HEADS, many, 2 * HD),
        delta=f32(HEADS, 1, many),
        dqt=f32(HEADS, 2 * HD, many),
        dkv=bf16(PLANE, many, 2 * width),
        kv_land=bf16(6, many, 2 * width),
        kv_half=bf16(2, many // 2, 2 * width),
        proj=bf16(many, 3 * width),
        part2=bf16(GROUPS, rows, model),
        relays2=bf16(2, rows // 2, model),
        lands2=bf16(2, rows, model),
        w_part=bf16(2, GROUPS, PLANE, half, 3 * width),
        w_core=bf16(GROUPS, PLANE, half, 3 * width),
        w_land=bf16(6, GROUPS, half, 3 * width),
        w_half=bf16(2, GROUPS // 2, half, 3 * width),
        w_hi=bf16(3, half, 3 * width),
        w_done=bf16(half, 3 * width),
        w_fin=bf16(GROUPS, 2, half, 3 * width),
        o_part=bf16(2, PLANE, 4, 8, model // 2),
        o_core=bf16(PLANE, 4, 8, model // 2),
        o_land=bf16(6, 4, 8, model // 2),
        o_half=bf16(2, 2, 8, model // 2),
        o_hi=bf16(3, 8, model // 2),
        o_done=bf16(8, model // 2),
        o_fin=bf16(4, 2, 8, model // 2),
        s_send=f32(count, 1, model + LANES),
        s_seq=f32(count, 1, model + LANES),
        s_mine=f32(1, model + LANES),
        s_dp=f32(8, 1, model + LANES),
        s_done=f32(1, model + LANES),
        s_fin=f32(count, 1, model + LANES),
        spread_sems=wire_sems(3),
        swap_sems=wire_sems(PLANE + 1),
        hid_sems=wire_sems(4),
        wq_sems=wire_sems(9),
        wo_sems=wire_sems(9),
        gather_sems=wire_sems(9),
        sum_sems=wire_sems(6),
        conv_sems=wire_sems(2),
        grad_sems=wire_sems(2),
        mix_sems=wire_sems(4),
        kv_sems=wire_sems(11),
        red_sems=wire_sems(6),
        core_sems=wire_sems(17),
        w_sems=wire_sems(11),
        o_sems=wire_sems(11),
        hi_sems=wire_sems(3),
        o_hi_sems=wire_sems(3),
        cross_sems=wire_sems(8),
        w_fin_send=dma(8),
        w_fin_recv=dma(4, 2),
        o_fin_send=dma(8),
        o_fin_recv=dma(4, 2),
        s_sems=wire_sems(count - 1),
        s_dp_sems=wire_sems(7),
        s_fin_sems=wire_sems(count - 1),
    )
    vmem = pl.BlockSpec(memory_space=pltpu.VMEM)
    names = [*ins, *outs, *scratch]
    return pl.pallas_call(
        functools.partial(whole_kernel, names),
        out_shape=list(outs.values()),
        in_specs=[vmem] * len(ins),
        out_specs=[vmem] * len(outs),
        scratch_shapes=list(scratch.values()),
        compiler_params=pltpu.CompilerParams(
            collective_id=0, has_side_effects=True, vmem_limit_bytes=62 * 2**20
        ),
        name="whole",
    )(*ins.values())


def hand_on_kernel(*refs):
    half = len(refs) // 2
    for src, dst in zip(refs[:half], refs[half:]):
        dst[...] = src[...].reshape(dst.shape)


def hand_on(*arrays):
    vmem = pl.BlockSpec(memory_space=pltpu.VMEM)
    return pl.pallas_call(
        hand_on_kernel,
        out_shape=[
            jax.ShapeDtypeStruct(a.shape[1:] if a.shape[0] == 1 else a.shape, a.dtype) for a in arrays
        ],
        in_specs=[vmem] * len(arrays),
        out_specs=[vmem] * len(arrays),
        name="hand_on",
    )(*arrays)


def local(frames, w_qkv, w_out, norm_gains, conv_kernel, conv_bias, out_grad):
    block_out, grad_input, grad_qkv, grad_out, kernel_sum, bias_sum, norms_sum = hand_on(
        *whole(
            frames[0], w_qkv, w_out, norm_gains, conv_kernel, conv_bias, out_grad[0]
        )
    )
    return (
        block_out[None],
        grad_input[None],
        grad_qkv,
        grad_out,
        norms_sum,
        kernel_sum,
        bias_sum,
    )


def solution(mesh):
    in_specs = (
        P("dp", "seq", None),
        P("seq", None),
        P("seq", None),
        P(),
        P(),
        P(),
        P("dp", "seq", None),
    )
    out_specs = (
        P("dp", "seq", None),
        P("dp", "seq", None),
        P("seq", None),
        P("seq", None),
        P(),
        P(),
        P(),
    )
    return jax.shard_map(local, mesh=mesh, in_specs=in_specs, out_specs=out_specs, check_vma=False)
```

```python
import functools

import jax
import jax.numpy as jnp
from jax import lax
from jax.experimental import pallas as pl
from jax.experimental.pallas import tpu as pltpu
from jax.sharding import PartitionSpec as P

EPS = 1e-05
GROUPS = 4
PLANE = 8
HEADS = 3
HD = 64
F32 = jnp.float32
BF16 = jnp.bfloat16


def layer_norm(values, gain):
    center = values - jnp.mean(values, axis=-1, keepdims=True)
    spread = jnp.mean(center * center, axis=-1, keepdims=True)
    inverse = lax.rsqrt(spread + EPS)
    normed = center * inverse
    return (normed * gain, normed, inverse)


def norm_back(grad, normed, inverse, gain):
    scaled = grad * gain
    inner = (
        scaled
        - jnp.mean(scaled, axis=-1, keepdims=True)
        - normed * jnp.mean(scaled * normed, axis=-1, keepdims=True)
    )
    return (inverse * inner, jnp.sum(grad * normed, axis=0))


def dot(a, b, ca, cb):
    return lax.dot_general(a, b, (((ca,), (cb,)), ((), ())), preferred_element_type=F32)


class Place:
    def __init__(self):
        seq = lax.axis_index("seq")
        y, z, x = seq // 8, (seq // 4) % 2, seq % 4
        right, left, far, other = (x + 1) % 4, (x + 3) % 4, (x + 2) % 4, 1 - z
        self.y, self.yp, self.ym, self.yf = y, (y + 1) % 4, (y + 3) % 4, (y + 2) % 4
        self.me = z * 4 + x
        self.xp, self.xm, self.xf = z * 4 + right, z * 4 + left, z * 4 + far
        self.zo = other * 4 + x
        self.zxp, self.zxm, self.zxf = other * 4 + right, other * 4 + left, other * 4 + far

        self.seq, self.dp = seq, lax.axis_index("dp")
        self.core, self.hi = self.dp % 2, self.dp // 2

    def plane(self, p):
        return {"seq": self.y * 8 + p}

    def holder(self, y, dp):
        return {"seq": y * 8 + self.me, "dp": dp}

    def greet(self):
        near = [{"seq": (self.seq + i) % 32} for i in range(1, 32)]
        near += [self.holder(self.y, (self.dp + j) % 8) for j in range(1, 8)]
        near += [
            self.holder((self.y + i) % 4, ((self.hi + j) % 4) * 2 + self.core)
            for i in range(1, 4)
            for j in range(1, 4)
        ]
        for device in near:
            pl.semaphore_signal(pltpu.get_barrier_semaphore(), inc=1, device_id=device)
        return len(near)

    def column(self, y):
        return {"seq": y * 8 + self.me}


class Wire:
    def __init__(self, sems):
        self.sems, self.sent = sems, {}

    def go(self, k, src, dst, device):
        copy = pltpu.make_async_remote_copy(
            src_ref=src,
            dst_ref=dst,
            send_sem=self.sems.at[0, k],
            recv_sem=self.sems.at[1, k],
            device_id=device,
        )
        copy.start()
        self.sent[k] = copy

    def got(self, *ks):
        for k in ks:
            self.sent[k].wait_recv()

    def done(self):
        for copy in self.sent.values():
            copy.wait_send()


def wire_sems(count):
    return pltpu.SemaphoreType.DMA((2, count))


class ColumnGather(Wire):
    def __init__(self, sems, place, buf):
        super().__init__(sems)
        self.at, self.buf = place, buf
        self.half = buf.shape[1] // 2

    def begin(self):
        t, own = self.at, self.buf.at[self.at.y]
        self.go(0, own, own, t.column(t.yp))
        self.go(1, own, own, t.column(t.ym))

    def relay(self):
        t, h = self.at, self.half
        self.got(0)
        first = self.buf.at[t.ym, pl.ds(0, h)]
        self.go(2, first, first, t.column(t.yp))
        self.got(1)
        second = self.buf.at[t.yp, pl.ds(h, h)]
        self.go(3, second, second, t.column(t.ym))

    def finish(self):
        self.got(2, 3)


class ColumnReduce(Wire):
    def __init__(self, sems, place, part, relays, lands):
        super().__init__(sems)
        self.at, self.part, self.relays, self.lands = place, part, relays, lands
        self.half = part.shape[1] // 2

    def far(self):
        t, h = self.at, self.half
        self.go(0, self.part.at[t.yf, pl.ds(0, h)], self.relays.at[0], t.column(t.ym))
        self.go(1, self.part.at[t.yf, pl.ds(h, h)], self.relays.at[1], t.column(t.yp))

    def near(self):
        t, h = self.at, self.half
        low, high = pl.ds(0, h), pl.ds(h, h)
        self.go(2, self.part.at[t.ym, high], self.lands.at[0, high], t.column(t.ym))
        self.go(3, self.part.at[t.yp, low], self.lands.at[1, low], t.column(t.yp))

    def relay(self):
        t, h = self.at, self.half
        low, high = pl.ds(0, h), pl.ds(h, h)
        self.got(0)
        self.part[t.ym, low] = (
            self.part[t.ym, low].astype(F32) + self.relays[0].astype(F32)
        ).astype(BF16)
        self.go(4, self.part.at[t.ym, low], self.lands.at[0, low], t.column(t.ym))
        self.got(1)
        self.part[t.yp, high] = (
            self.part[t.yp, high].astype(F32) + self.relays[1].astype(F32)
        ).astype(BF16)
        self.go(5, self.part.at[t.yp, high], self.lands.at[1, high], t.column(t.yp))

    def finish(self):
        self.got(2, 3, 4, 5)
        return (
            self.part[self.at.y].astype(F32)
            + self.lands[0].astype(F32)
            + self.lands[1].astype(F32)
        )


class PlaneGather(Wire):
    def __init__(self, sems, place, full, half):
        super().__init__(sems)
        self.at, self.full, self.half = place, full, half

    def begin(self):
        t, own = self.at, self.full(self.at.me)
        self.go(0, own, own, t.plane(t.xp))
        self.go(1, own, own, t.plane(t.xm))
        self.go(2, own, own, t.plane(t.zo))

    def relay(self):
        t = self.at
        self.got(0)
        first = self.half(t.xm, 0)
        self.go(3, first, first, t.plane(t.xp))
        self.got(1)
        second = self.half(t.xp, 1)
        self.go(4, second, second, t.plane(t.xm))
        self.got(2)
        other = self.full(t.zo)
        self.go(5, other, other, t.plane(t.xp))
        self.go(6, other, other, t.plane(t.xm))

    def cross(self):
        t = self.at
        for k in (0, 1):
            self.got(3 + k)
            part = self.half(t.xf, k)
            self.go(7 + k, part, part, t.plane(t.zo))

    def finish(self):
        self.got(5, 6, 7, 8)


class PlaneReduce(Wire):
    def __init__(self, sems, place, full, half, land, land_half, half_land):
        super().__init__(sems)
        self.at, self.full, self.half = place, full, half
        self.land, self.land_half, self.half_land = land, land_half, half_land

    def add(self, ref, *more):
        total = ref[...].astype(F32)
        for other in more:
            total = total + other[...].astype(F32)
        ref[...] = total.astype(BF16)

    def far(self):
        t = self.at
        self.go(0, self.half(t.zxf, 0), self.land_half(0, 0), t.plane(t.zo))
        self.go(8, self.half(t.zxf, 1), self.land_half(0, 1), t.plane(t.zo))

    def left(self):
        self.go(1, self.full(self.at.zxm), self.land(1), self.at.plane(self.at.xm))

    def right(self):
        self.go(2, self.full(self.at.zxp), self.land(2), self.at.plane(self.at.xp))

    def opposite(self, i):
        t = self.at
        self.got((0, 8)[i])
        self.add(self.half(t.xf, i), self.land_half(0, i))
        self.go(3 + i, self.half(t.xf, i), self.half_land(i), t.plane((t.xm, t.xp)[i]))

    def early(self):
        t = self.at
        self.go(6, self.half(t.xm, 1), self.land_half(4, 1), t.plane(t.xm))
        self.go(7, self.half(t.xp, 0), self.land_half(5, 0), t.plane(t.xp))

    def across(self):
        t = self.at
        self.got(1, 2)
        self.add(self.full(t.zo), self.land(1), self.land(2))
        self.go(5, self.full(t.zo), self.land(3), t.plane(t.zo))

    def near(self):
        t = self.at
        self.got(3)
        self.add(self.half(t.xm, 0), self.half_land(0))
        self.go(9, self.half(t.xm, 0), self.land_half(4, 0), t.plane(t.xm))
        self.got(4)
        self.add(self.half(t.xp, 1), self.half_land(1))
        self.go(10, self.half(t.xp, 1), self.land_half(5, 1), t.plane(t.xp))

    def finish(self):
        self.got(5, 6, 7, 9, 10)
        total = self.full(self.at.me)[...].astype(F32)
        for k in (3, 4, 5):
            total = total + self.land(k)[...].astype(F32)
        return total


def pick(i, *values):
    out = values[-1]
    for k in range(len(values) - 2, -1, -1):
        out = jnp.where(i == k, values[k], out)
    return out


def local_copies(pairs, sems):
    copies = [
        pltpu.make_async_copy(src, dst, sems.at[i]) for i, (src, dst) in enumerate(pairs)
    ]
    for copy in copies:
        copy.start()
    return copies


QB = 128


def forward_block(kv, c, h, cols, qpad, top, total, acc):
    both = kv[c, :, h * 128 : (h + 1) * 128]
    scores = dot(both, qpad[h, cols, :], 1, 1)
    old = top[h, :, cols]
    new = jnp.maximum(old, jnp.max(scores, axis=0, keepdims=True))
    shrink = jnp.exp(old - new)
    expo = jnp.exp(scores - new)
    top[h, :, cols] = new
    total[h, :, cols] = total[h, :, cols] * shrink + jnp.sum(expo, axis=0, keepdims=True)
    acc[h, :, cols] = acc[h, :, cols] * shrink + dot(both, expo.astype(BF16), 0, 0)


def forward_chunk(kv, c, qpad, top, total, acc):
    for h in range(HEADS):
        for b in range(qpad.shape[1] // QB):
            forward_block(kv, c, h, slice(b * QB, (b + 1) * QB), qpad, top, total, acc)


def prob_chunk(kv, c, qpad, lse, probs):
    for h in range(HEADS):
        scores = dot(kv[c, :, h * 128 : (h + 1) * 128], qpad[h], 1, 1)
        probs[c, h] = jnp.exp(scores - lse[h]).astype(BF16)


def backward_chunk(kv, c, qpad, dopad, probs, delta, dqt, out):
    for h in range(HEADS):
        lanes = slice(h * 128, (h + 1) * 128)
        both, query, grad = kv[c, :, lanes], qpad[h], dopad[h]
        slopes = dot(both, grad, 1, 1)
        prob = probs[c, h]
        score_grads = (prob.astype(F32) * (slopes - delta[h])).astype(BF16)
        out[c, :, lanes] = (
            dot(prob, grad, 1, 0) + dot(score_grads, query, 1, 0)
        ).astype(BF16)
        dqt[h] += dot(both, score_grads, 0, 0)


HALO = 16
LANES = 128


def shifts(wide, length, taps):
    for low in range(8):
        moved = wide if low == 0 else pltpu.roll(wide, wide.shape[0] - low, 0)
        for offset in range(low, taps + 1, 8):
            if offset > 0:
                yield offset, moved[offset - low : offset - low + length]


class Edge(Wire):
    def __init__(self, sems, place, wide):
        super().__init__(sems)
        t, rows = place, wide.shape[0]
        self.first, self.last = t.seq == 0, t.seq == 31
        nothing = jnp.zeros((HALO, wide.shape[1]), BF16)

        @pl.when(self.first)
        def _():
            wide[0:HALO] = nothing

        @pl.when(self.last)
        def _():
            wide[rows - HALO :] = nothing

        self.up = pltpu.make_async_remote_copy(
            src_ref=wide.at[pl.ds(rows - 2 * HALO, HALO)],
            dst_ref=wide.at[pl.ds(0, HALO)],
            send_sem=sems.at[0, 0],
            recv_sem=sems.at[1, 0],
            device_id={"seq": jnp.minimum(t.seq + 1, 31)},
        )
        self.down = pltpu.make_async_remote_copy(
            src_ref=wide.at[pl.ds(HALO, HALO)],
            dst_ref=wide.at[pl.ds(rows - HALO, HALO)],
            send_sem=sems.at[0, 1],
            recv_sem=sems.at[1, 1],
            device_id={"seq": jnp.maximum(t.seq - 1, 0)},
        )

    def begin(self):
        @pl.when(jnp.logical_not(self.last))
        def _():
            self.up.start()

        @pl.when(jnp.logical_not(self.first))
        def _():
            self.down.start()

    def finish(self):
        @pl.when(jnp.logical_not(self.last))
        def _():
            self.up.wait_send()
            self.down.wait_recv()

        @pl.when(jnp.logical_not(self.first))
        def _():
            self.down.wait_send()
            self.up.wait_recv()


def whole_kernel(names, *refs):
    r = dict(zip(names, refs))
    (
        frames,
        w_qkv,
        w_out,
        gains_in,
        conv_kernel,
        conv_bias,
        out_grad,
        block_out,
        grad_input,
        grad_qkv,
        grad_out,
        kernel_sum,
        bias_sum,
        norms_sum,
        w_parts,
        hid,
        wq,
        wo,
        wo32,
        wo16,
        kv,
        qpad,
        lse,
        total,
        acc,
        att,
        probs,
        part,
        relays,
        lands,
        mixed_keep,
        normed_keep,
        first_keep,
        conv_wide,
        grad_wide,
        conv_back,
        mix,
        dopad,
        delta,
        dqt,
        dkv,
        kv_land,
        kv_half,
        proj,
        part2,
        relays2,
        lands2,
        w_part,
        w_core,
        w_land,
        w_half,
        w_hi,
        w_done,
        w_fin,
        o_part,
        o_core,
        o_land,
        o_half,
        o_hi,
        o_done,
        o_fin,
        s_send,
        s_seq,
        s_mine,
        s_dp,
        s_done,
        s_fin,
        spread_sems,
        swap_sems,
        hid_sems,
        wq_sems,
        wo_sems,
        gather_sems,
        sum_sems,
        conv_sems,
        grad_sems,
        mix_sems,
        kv_sems,
        red_sems,
        core_sems,
        w_sems,
        o_sems,
        hi_sems,
        o_hi_sems,
        cross_sems,
        w_fin_send,
        w_fin_recv,
        o_fin_send,
        o_fin_recv,
        g_mine,
        g_y,
        g_plane_mine,
        g_plane,
        g_dp_mine,
        g_dp,
        g_sems,
        s_sems,
        s_dp_sems,
        s_fin_sems,
    ) = (r[n] for n in names)
    t = Place()
    greeted = t.greet()
    rows, model = frames.shape
    many = GROUPS * rows
    width = HEADS * HD
    shard = w_qkv.shape[0]
    gain1, gain2 = gains_in[0:1, :], gains_in[1:2, :]

    for g in range(GROUPS):
        columns = [w_qkv[:, g * width : (g + 1) * width]]
        for h in range(HEADS):
            for kind in (1, 2):
                start = (kind * GROUPS + g) * width + h * HD
                columns.append(w_qkv[:, start : start + HD])
        w_parts[g] = jnp.concatenate(columns, axis=1)
    inputs = frames[...].astype(F32)
    shifted, normed, inverse1 = layer_norm(inputs, gain1)
    first_keep[...] = normed
    hid[t.y] = shifted.astype(BF16)
    pl.semaphore_wait(pltpu.get_barrier_semaphore(), greeted)
    hid_net = ColumnGather(hid_sems, t, hid)
    hid_net.begin()
    holds = t.y // 2 == t.core
    spread_copies = []
    for k in range(1, GROUPS):
        y = (t.y + k) % GROUPS
        copy = pltpu.make_async_remote_copy(
            src_ref=w_parts.at[y],
            dst_ref=wq.at[t.y, t.me],
            send_sem=spread_sems.at[0, k - 1],
            recv_sem=spread_sems.at[1, k - 1],
            device_id=t.column(y),
        )
        spread_copies.append((copy, ((t.y + GROUPS - k) % GROUPS) // 2 == t.core))

    @pl.when(holds)
    def _():
        for copy, _ in spread_copies:
            copy.start()
        wq[t.y, t.me] = w_parts[t.y]

    share = width // PLANE
    wide = model // 2
    for c in range(2):

        @pl.when(t.core == c)
        def _(c=c):
            wo[c, t.me] = w_out[:, c * wide : (c + 1) * wide]


    for copy, comes in spread_copies:
        pl.when(comes)(copy.wait_recv)
    base = 2 * t.core
    wq_net = PlaneGather(
        wq_sems, t, lambda p: wq.at[pl.ds(base, 2), p], lambda p, i: wq.at[base + i, p]
    )
    swap = Wire(swap_sems)
    buddy = {"dp": t.hi * 2 + 1 - t.core}

    def trade(*ps):
        for p in ps:
            half = wq.at[pl.ds(base, 2), p]
            swap.go(len(swap.sent), half, half, buddy)
    wo_net = PlaneGather(
        wo_sems,
        t,
        lambda p: wo.at[t.core, p],
        lambda p, i: wo.at[t.core, p, :, pl.ds(i * (wide // 2), wide // 2)],
    )
    wq_net.begin()
    trade(t.me)
    wq_net.relay()
    trade(t.xm, t.xp, t.zo)
    hid_net.relay()
    wq_net.cross()
    trade(t.xf)
    wo_net.begin()
    wq_net.finish()
    trade(t.zxm, t.zxp, t.zxf)
    hid_net.finish()
    swap.got(*range(PLANE))

    hidden = hid[...].reshape(many, model)
    weights = wq[...].reshape(model, 3 * width)
    projected = dot(hidden, weights, 1, 0).astype(BF16)
    kv[t.me] = projected[:, width:]
    kv_net = PlaneGather(
        gather_sems,
        t,
        lambda p: kv.at[p],
        lambda p, i: kv.at[p, pl.ds(i * (many // 2), many // 2)],
    )
    kv_net.begin()
    zeros = jnp.zeros((many, HD), BF16)
    for h in range(HEADS):
        qpad[h] = jnp.concatenate(
            [projected[:, h * HD : (h + 1) * HD] * BF16(HD**-0.5), zeros], axis=1
        )
    lse[...] = jnp.full_like(lse, -jnp.inf)
    total[...] = jnp.zeros_like(total)
    acc[...] = jnp.zeros_like(acc)

    def attend(*chunks):
        if len(chunks) == 1:
            forward_chunk(kv, chunks[0], qpad, lse, total, acc)
            return

        def step(i, carry):
            forward_chunk(kv, pick(i, *chunks), qpad, lse, total, acc)
            return carry

        lax.fori_loop(0, len(chunks), step, 0)

    attend(t.me)
    kv_net.relay()
    wo_net.relay()
    attend(t.xm, t.xp, t.zo)
    kv_net.cross()
    wo_net.cross()
    attend(t.xf)
    wo_net.finish()
    swap.go(PLANE, wo.at[t.core], wo.at[t.core], buddy)
    swap.got(PLANE)
    for p in range(PLANE):
        for c in range(2):
            wo32[p * share : (p + 1) * share, c * wide : (c + 1) * wide] = wo[c, p].astype(F32)
    wo16[...] = wo32[...].astype(BF16)
    kv_net.got(5, 6)
    kv_net.got(7, 8)

    def last(y):
        cols = pl.ds(pl.multiple_of(y * rows, rows), rows)

        for c in (t.zxm, t.zxp, t.zxf):
            for h in range(HEADS):
                forward_block(kv, c, h, cols, qpad, lse, total, acc)
        for h in range(HEADS):
            att[h * HD : (h + 1) * HD, cols] = (
                acc[h, HD : 2 * HD, cols] / total[h, :, cols]
            ).astype(BF16)
            lse[h, :, cols] = lse[h, :, cols] + jnp.log(total[h, :, cols])
        part[y] = dot(att[:, cols], wo16[...], 0, 0).astype(BF16)

    sum_net = ColumnReduce(sum_sems, t, part, relays, lands)
    last(t.yf)
    sum_net.far()
    last(t.ym)
    last(t.yp)
    sum_net.near()
    last(t.y)
    sum_net.relay()

    def foresee(*chunks):
        def step(i, carry):
            prob_chunk(kv, pick(i, *chunks), qpad, lse, probs)
            return carry

        lax.fori_loop(0, len(chunks), step, 0)

    foresee(t.zxf, t.zxm)
    mixed = (frames[...].astype(F32) + sum_net.finish()).astype(BF16)

    mixed32 = mixed.astype(F32)
    mixed_keep[...] = mixed32
    shifted, normed, inverse = layer_norm(mixed32, gain2)
    inside = slice(HALO, HALO + rows)
    conv_wide[inside] = shifted.astype(BF16)
    conv_edge = Edge(conv_sems, t, conv_wide)
    conv_edge.begin()
    normed_keep[...] = normed
    foresee(t.zxp)
    conv_edge.finish()
    taps = conv_kernel.shape[0]

    def lanes_of(b):
        return pl.ds(pl.multiple_of(b * LANES, LANES), LANES)

    def convolve(b, carry):
        lanes = lanes_of(b)
        pre = jnp.zeros((rows, LANES), F32) + conv_bias[lanes][None]
        for offset, moved in shifts(conv_wide[:, lanes].astype(F32), rows, taps):
            pre = pre + moved * conv_kernel[offset - 1 : offset, lanes]
        sigma = 1.0 / (1.0 + jnp.exp(-pre))
        block_out[:, lanes] = (mixed_keep[:, lanes] + pre * sigma).astype(BF16)
        grad_wide[inside, lanes] = (
            out_grad[:, lanes].astype(F32) * sigma * (1.0 + pre * (1.0 - sigma))
        ).astype(BF16)
        return carry

    blocks = model // LANES
    lax.fori_loop(0, blocks, convolve, 0)
    grad_edge = Edge(grad_sems, t, grad_wide)
    grad_edge.begin()
    foresee(t.xf)
    grad_edge.finish()

    def convolve_back(b, carry):
        lanes = lanes_of(b)
        grad = jnp.zeros((rows, LANES), F32)
        for offset, moved in shifts(grad_wide[:, lanes].astype(F32), rows, taps):
            grad = grad + moved * conv_kernel[taps - offset : taps - offset + 1, lanes]
        conv_back[:, lanes] = grad
        return carry

    lax.fori_loop(0, blocks, convolve_back, 0)
    norm_grad, gain2_grad = norm_back(conv_back[...], normed_keep[...], inverse, gain2)
    gain2_grad = gain2_grad[None]
    mix[t.y] = (out_grad[...].astype(F32) + norm_grad).astype(BF16)
    mix_net = ColumnGather(mix_sems, t, mix)
    mix_net.begin()

    def kernel_grads(b, carry):
        lanes = lanes_of(b)
        grad = grad_wide[inside, lanes].astype(F32)
        for offset, moved in shifts(conv_wide[:, lanes].astype(F32), rows, taps):
            s_send[offset - 1, :, lanes] = jnp.sum(grad * moved, axis=0, keepdims=True)
        s_send[taps, :, lanes] = jnp.sum(grad, axis=0, keepdims=True)
        return carry

    lax.fori_loop(0, blocks, kernel_grads, 0)
    foresee(t.zo, t.xm, t.xp)
    mix_net.relay()
    foresee(t.me)
    mix_net.finish()

    mixed = mix[...].reshape(many, model)
    grads = dot(mixed, wo16[...], 1, 1).astype(BF16)
    grads_turned = dot(wo16[...], mixed, 1, 1).astype(BF16).astype(F32)
    for h in range(HEADS):
        lanes = slice(h * HD, (h + 1) * HD)
        mine = grads[:, lanes]
        dopad[h] = jnp.concatenate([zeros, mine], axis=1)
        delta[h] = jnp.sum(
            att[lanes, :].astype(F32) * grads_turned[lanes, :], axis=0, keepdims=True
        )
    dqt[...] = jnp.zeros_like(dqt)

    def backward(*chunks):
        def step(i, carry):
            backward_chunk(kv, pick(i, *chunks), qpad, dopad, probs, delta, dqt, dkv)
            return carry

        if len(chunks) == 1:
            step(0, 0)
        else:
            lax.fori_loop(0, len(chunks), step, 0)

    half = many // 2
    net = PlaneReduce(
        kv_sems,
        t,
        lambda p: dkv.at[p],
        lambda p, i: dkv.at[p, pl.ds(i * half, half)],
        lambda k: kv_land.at[k],
        lambda k, i: kv_land.at[k, pl.ds(i * half, half)],
        lambda k: kv_half.at[k],
    )
    order = (t.zxf, t.zxm, t.zxp, t.xf, t.zo, t.xm, t.xp, t.me)
    backward(t.zxm)
    net.left()
    backward(t.zxp)
    net.right()
    backward(t.zxf)
    net.far()
    out_terms = dot(att[...], mixed, 1, 0)
    quarter = o_part.shape[2]
    for c in range(2):
        for p in range(PLANE):
            for i in range(quarter):
                piece = o_part.at[c, p, i]
                if i * 8 < share:
                    start = p * share + i * 8
                    piece[...] = out_terms[
                        start : start + 8, c * wide : (c + 1) * wide
                    ].astype(BF16)
                else:
                    piece[...] = jnp.zeros(piece.shape, BF16)
    pair = Wire(core_sems)
    pair.go(16, o_part.at[1 - t.core], o_core, buddy)
    o_mine = o_part.at[t.core]
    o_net = PlaneReduce(
        o_sems,
        t,
        lambda p: o_mine.at[p],
        lambda p, i: o_mine.at[p, pl.ds(2 * i, 2)],
        lambda k: o_land.at[k],
        lambda k, i: o_land.at[k, pl.ds(2 * i, 2)],
        lambda k: o_half.at[k],
    )
    count = s_send.shape[0]
    for r in range(count):
        if r < model // LANES:
            s_send[r, :, model:] = gain2_grad[:, r * LANES : (r + 1) * LANES]
        else:
            s_send[r, :, model:] = jnp.zeros((1, LANES), F32)
    s_net = Wire(s_sems)
    s_seq[t.seq] = s_send[t.seq]
    for k in range(1, count):
        r = (t.seq + k) % count
        s_net.go(k - 1, s_send.at[r], s_seq.at[t.seq], {"seq": r})
    backward(t.xf)
    pair.got(16)
    o_net.add(o_mine, o_core)
    o_net.far()
    o_net.left()
    o_net.right()
    backward(t.xm)
    net.opposite(0)
    backward(t.xp)
    net.early()
    net.opposite(1)
    s_net.got(*range(count - 1))
    s_mine[...] = jnp.sum(s_seq[...], axis=0)
    s_dp[t.dp] = s_mine[...]
    s_dp_net = Wire(s_dp_sems)
    for k in range(1, 8):
        s_dp_net.go(k - 1, s_mine, s_dp.at[t.dp], {"dp": (t.dp + k) % 8})

    o_net.early()
    backward(t.zo)
    net.across()
    net.near()
    o_net.opposite(0)
    o_net.opposite(1)
    o_net.across()
    backward(t.me)
    o_net.near()
    s_dp_net.got(*range(7))
    summed = s_dp[0]
    for d in range(1, 8):
        summed = summed + s_dp[d]
    s_done[...] = summed
    s_fin[t.seq] = summed
    s_fin_net = Wire(s_fin_sems)
    for k in range(1, count):
        s_fin_net.go(k - 1, s_done, s_fin.at[t.seq], {"seq": (t.seq + k) % count})

    for h in range(HEADS):
        proj[:, h * HD : (h + 1) * HD] = (dqt[h, 0:HD, :] * HD**-0.5).T.astype(BF16)

    proj[:, width:] = net.finish().astype(BF16)

    weights = wq[...].reshape(model, 3 * width)

    def product(y):
        here = proj[pl.ds(pl.multiple_of(y * rows, rows), rows), :]
        part2[y] = dot(here, weights, 1, 1).astype(BF16)

    red = ColumnReduce(red_sems, t, part2, relays2, lands2)
    product(t.yf)
    red.far()
    half_rows = w_part.shape[3]
    hidden = hid[...].reshape(many, model)
    w_terms = dot(hidden, proj[...], 0, 0).reshape(GROUPS, PLANE, 2, half_rows, 3 * width)
    for c in range(2):
        w_part[c] = w_terms[:, :, c].astype(BF16)
    for k, p in enumerate(order):
        pair.go(8 + k, w_part.at[1 - t.core, :, p], w_core.at[:, p], buddy)
    product(t.ym)
    product(t.yp)
    red.near()
    w_mine = w_part.at[t.core]
    w_net = PlaneReduce(
        w_sems,
        t,
        lambda p: w_mine.at[:, p],
        lambda p, i: w_mine.at[pl.ds(2 * i, 2), p],
        lambda k: w_land.at[k],
        lambda k, i: w_land.at[k, pl.ds(2 * i, 2)],
        lambda k: w_half.at[k],
    )

    def join(first, last):
        for k in range(first, last):
            p = order[k]
            pair.got(8 + k)
            w_net.add(w_mine.at[:, p], w_core.at[:, p])

    join(0, 1)
    w_net.far()
    join(1, 2)
    w_net.left()
    join(2, 3)
    w_net.right()
    product(t.y)
    red.relay()
    join(3, 4)
    w_net.opposite(0)
    w_net.opposite(1)
    join(4, 7)
    w_net.early()
    o_mine[t.me] = o_net.finish().astype(BF16)
    o_hi_net = Wire(o_hi_sems)
    for k in range(1, 4):
        j = (t.hi + k) % 4
        o_hi_net.go(k - 1, o_mine.at[t.me, j], o_hi.at[k - 1], {"dp": j * 2 + t.core})
    join(7, 8)
    w_net.across()
    w_net.near()

    s_fin_net.got(*range(count - 1))
    for r in range(count):
        row = s_fin[r]
        if r < taps:
            kernel_sum[r : r + 1, :] = row[:, :model]
        else:
            bias_sum[...] = row[:, :model]
        if r < model // LANES:
            norms_sum[1:2, r * LANES : (r + 1) * LANES] = row[:, model:]
    grad_hidden = red.finish()
    norm_grad, gain_sum = norm_back(grad_hidden, first_keep[...], inverse1, gain1)
    grad_input[...] = (mix[t.y].astype(F32) + norm_grad).astype(BF16)
    g_mine[...] = gain_sum[None]
    g_y[t.y] = g_mine[...]
    g_net = Wire(g_sems)
    for k, y in enumerate((t.yp, t.ym, t.yf)):
        g_net.go(k, g_mine, g_y.at[t.y], t.column(y))

    o_hi_net.got(0, 1, 2)
    o_out_block = o_mine[t.me, t.hi].astype(F32)
    for k in range(3):
        o_out_block = o_out_block + o_hi[k].astype(F32)
    o_done[...] = o_out_block.astype(BF16)
    finals = []

    def deliver(src, dst, send, recv, y):
        for k in range(1, 4):
            copy = pltpu.make_async_remote_copy(
                src_ref=src,
                dst_ref=dst,
                send_sem=send.at[k],
                recv_sem=recv,
                device_id=t.holder(y, ((t.hi + k) % 4) * 2 + t.core),
            )
            copy.start()
            finals.append(copy)

    deliver(o_done, o_fin.at[t.hi, t.core], o_fin_send, o_fin_recv.at[t.hi, t.core], t.y)
    o_own = pltpu.make_async_copy(
        o_done, o_fin.at[t.hi, t.core], o_fin_recv.at[t.hi, t.core]
    )
    o_own.start()
    w_mine[:, t.me] = w_net.finish().astype(BF16)
    hi_net = Wire(hi_sems)
    for k in range(1, 4):
        j = (t.hi + k) % 4
        there = {"dp": j * 2 + t.core}
        hi_net.go(k - 1, w_mine.at[j, t.me], w_hi.at[k - 1], there)

    g_net.got(0, 1, 2)
    g_plane_mine[...] = ((g_y[0] + g_y[1]) + g_y[2]) + g_y[3]
    g_plane[t.me] = g_plane_mine[...]
    for k in range(1, PLANE):
        g_net.go(2 + k, g_plane_mine, g_plane.at[t.me], t.plane((t.me + k) % PLANE))

    hi_net.got(*range(3))
    w_out_block = w_mine[t.hi, t.me].astype(F32)
    for k in range(3):
        w_out_block = w_out_block + w_hi[k].astype(F32)
    w_done[...] = w_out_block.astype(BF16)
    deliver(w_done, w_fin.at[t.y, t.core], w_fin_send, w_fin_recv.at[t.y, t.core], t.hi)
    w_own = pltpu.make_async_copy(w_done, w_fin.at[t.y, t.core], w_fin_recv.at[t.y, t.core])
    w_away = pltpu.make_async_remote_copy(
        src_ref=w_done,
        dst_ref=w_fin.at[t.y, t.core],
        send_sem=w_fin_send.at[0],
        recv_sem=w_fin_recv.at[t.y, t.core],
        device_id=t.holder(t.hi, t.dp),
    )

    @pl.when(t.hi == t.y)
    def _():
        w_own.start()

    @pl.when(t.hi != t.y)
    def _():
        w_away.start()

    g_net.got(*range(3, 10))
    along = g_plane[0]
    for p in range(1, PLANE):
        along = along + g_plane[p]
    g_dp_mine[...] = along
    g_dp[t.dp] = along
    for k in range(1, 8):
        g_net.go(9 + k, g_dp_mine, g_dp.at[t.dp], {"dp": (t.dp + k) % 8})

    cross = Wire(cross_sems)
    for i in range(4):
        pltpu.make_async_copy(o_done, o_fin.at[i, t.core], o_fin_recv.at[i, t.core]).wait()
        cross.go(i, o_fin.at[i, t.core], o_fin.at[i, t.core], buddy)
    for i in range(4):
        pltpu.make_async_copy(w_done, w_fin.at[i, t.core], w_fin_recv.at[i, t.core]).wait()
        cross.go(4 + i, w_fin.at[i, t.core], w_fin.at[i, t.core], buddy)
    cross.got(*range(8))
    pieces = [w_fin[y].astype(F32).reshape(2 * half_rows, 3 * width) for y in range(GROUPS)]
    columns = [piece[:, :width] for piece in pieces]
    for kind in range(2):
        for piece in pieces:
            for h in range(HEADS):
                start = width + (2 * h + kind) * HD
                columns.append(piece[:, start : start + HD])
    grad_qkv[...] = jnp.concatenate(columns, axis=1).astype(BF16)
    sides = [
        o_fin[0 : share // 8, c].astype(F32).reshape(share, wide) for c in range(2)
    ]
    grad_out[...] = jnp.concatenate(sides, axis=1).astype(BF16)
    g_net.got(*range(10, 17))
    along = g_dp[0]
    for d in range(1, 8):
        along = along + g_dp[d]
    norms_sum[0:1, :] = along
    for copy in finals:
        copy.wait_send()

    @pl.when(t.hi != t.y)
    def _():
        w_away.wait_send()

    @pl.when(holds)
    def _():
        for copy, _ in spread_copies:
            copy.wait_send()

    for wire in (swap, hid_net, wq_net, wo_net, kv_net, sum_net, mix_net, net, pair, o_net, red, w_net, hi_net, o_hi_net, cross, s_net, s_dp_net, s_fin_net, g_net):
        wire.done()


def bf16(*shape):
    return pltpu.VMEM(shape, BF16)


def f32(*shape):
    return pltpu.VMEM(shape, F32)


def dma(*shape):
    return pltpu.SemaphoreType.DMA(shape)


def whole(frames, w_qkv, w_out, gains, conv_kernel, conv_bias, out_grad):
    rows, model = frames.shape
    shard = w_qkv.shape[0]
    many = GROUPS * rows
    width = HEADS * HD
    half = shard // 2
    count = conv_kernel.shape[0] + 1
    like = jax.ShapeDtypeStruct
    ins = dict(
        frames=frames,
        w_qkv=w_qkv,
        w_out=w_out,
        gains_in=gains,
        conv_kernel=conv_kernel,
        conv_bias=conv_bias,
        out_grad=out_grad,
    )
    outs = dict(
        block_out=like((rows, model), BF16),
        grad_input=like((rows, model), BF16),
        grad_qkv=like(w_qkv.shape, BF16),
        grad_out=like(w_out.shape, BF16),
        kernel_sum=like((count - 1, model), F32),
        bias_sum=like((1, model), F32),
        norms_sum=like((2, model), F32),
    )
    scratch = dict(
        w_parts=bf16(GROUPS, shard, 3 * width),
        hid=bf16(GROUPS, rows, model),
        wq=bf16(GROUPS, PLANE, shard, 3 * width),
        wo=bf16(2, PLANE, width // PLANE, model // 2),
        wo32=f32(width, model),
        wo16=bf16(width, model),
        kv=bf16(PLANE, many, 2 * width),
        qpad=bf16(HEADS, many, 2 * HD),
        lse=f32(HEADS, 1, many),
        total=f32(HEADS, 1, many),
        acc=f32(HEADS, 2 * HD, many),
        att=bf16(width, many),
        probs=bf16(PLANE, HEADS, many, many),
        part=bf16(GROUPS, rows, model),
        relays=bf16(2, rows // 2, model),
        lands=bf16(2, rows, model),
        mixed_keep=f32(rows, model),
        normed_keep=f32(rows, model),
        first_keep=f32(rows, model),
        conv_wide=bf16(rows + 2 * HALO, model),
        grad_wide=bf16(rows + 2 * HALO, model),
        conv_back=f32(rows, model),
        mix=bf16(GROUPS, rows, model),
        dopad=bf16(HEADS, many, 2 * HD),
        delta=f32(HEADS, 1, many),
        dqt=f32(HEADS, 2 * HD, many),
        dkv=bf16(PLANE, many, 2 * width),
        kv_land=bf16(6, many, 2 * width),
        kv_half=bf16(2, many // 2, 2 * width),
        proj=bf16(many, 3 * width),
        part2=bf16(GROUPS, rows, model),
        relays2=bf16(2, rows // 2, model),
        lands2=bf16(2, rows, model),
        w_part=bf16(2, GROUPS, PLANE, half, 3 * width),
        w_core=bf16(GROUPS, PLANE, half, 3 * width),
        w_land=bf16(6, GROUPS, half, 3 * width),
        w_half=bf16(2, GROUPS // 2, half, 3 * width),
        w_hi=bf16(3, half, 3 * width),
        w_done=bf16(half, 3 * width),
        w_fin=bf16(GROUPS, 2, half, 3 * width),
        o_part=bf16(2, PLANE, 4, 8, model // 2),
        o_core=bf16(PLANE, 4, 8, model // 2),
        o_land=bf16(6, 4, 8, model // 2),
        o_half=bf16(2, 2, 8, model // 2),
        o_hi=bf16(3, 8, model // 2),
        o_done=bf16(8, model // 2),
        o_fin=bf16(4, 2, 8, model // 2),
        s_send=f32(count, 1, model + LANES),
        s_seq=f32(count, 1, model + LANES),
        s_mine=f32(1, model + LANES),
        s_dp=f32(8, 1, model + LANES),
        s_done=f32(1, model + LANES),
        s_fin=f32(count, 1, model + LANES),
        spread_sems=wire_sems(3),
        swap_sems=wire_sems(PLANE + 1),
        hid_sems=wire_sems(4),
        wq_sems=wire_sems(9),
        wo_sems=wire_sems(9),
        gather_sems=wire_sems(9),
        sum_sems=wire_sems(6),
        conv_sems=wire_sems(2),
        grad_sems=wire_sems(2),
        mix_sems=wire_sems(4),
        kv_sems=wire_sems(11),
        red_sems=wire_sems(6),
        core_sems=wire_sems(17),
        w_sems=wire_sems(11),
        o_sems=wire_sems(11),
        hi_sems=wire_sems(3),
        o_hi_sems=wire_sems(3),
        cross_sems=wire_sems(8),
        w_fin_send=dma(8),
        w_fin_recv=dma(4, 2),
        o_fin_send=dma(8),
        o_fin_recv=dma(4, 2),
        g_mine=f32(1, model),
        g_y=f32(GROUPS, 1, model),
        g_plane_mine=f32(1, model),
        g_plane=f32(PLANE, 1, model),
        g_dp_mine=f32(1, model),
        g_dp=f32(8, 1, model),
        g_sems=wire_sems(17),
        s_sems=wire_sems(count - 1),
        s_dp_sems=wire_sems(7),
        s_fin_sems=wire_sems(count - 1),
    )
    vmem = pl.BlockSpec(memory_space=pltpu.VMEM)
    names = [*ins, *outs, *scratch]
    return pl.pallas_call(
        functools.partial(whole_kernel, names),
        out_shape=list(outs.values()),
        in_specs=[vmem] * len(ins),
        out_specs=[vmem] * len(outs),
        scratch_shapes=list(scratch.values()),
        compiler_params=pltpu.CompilerParams(
            collective_id=0, has_side_effects=True, vmem_limit_bytes=62 * 2**20
        ),
        name="whole",
    )(*ins.values())


def hand_on_kernel(*refs):
    half = len(refs) // 2
    for src, dst in zip(refs[:half], refs[half:]):
        dst[...] = src[...].reshape(dst.shape)


def hand_on(*arrays):
    vmem = pl.BlockSpec(memory_space=pltpu.VMEM)
    return pl.pallas_call(
        hand_on_kernel,
        out_shape=[
            jax.ShapeDtypeStruct(a.shape[1:] if a.shape[0] == 1 else a.shape, a.dtype) for a in arrays
        ],
        in_specs=[vmem] * len(arrays),
        out_specs=[vmem] * len(arrays),
        name="hand_on",
    )(*arrays)


def local(frames, w_qkv, w_out, norm_gains, conv_kernel, conv_bias, out_grad):
    block_out, grad_input, grad_qkv, grad_out, kernel_sum, bias_sum, norms_sum = hand_on(
        *whole(
            frames[0], w_qkv, w_out, norm_gains, conv_kernel, conv_bias, out_grad[0]
        )
    )
    return (
        block_out[None],
        grad_input[None],
        grad_qkv,
        grad_out,
        norms_sum,
        kernel_sum,
        bias_sum,
    )


def solution(mesh):
    in_specs = (
        P("dp", "seq", None),
        P("seq", None),
        P("seq", None),
        P(),
        P(),
        P(),
        P("dp", "seq", None),
    )
    out_specs = (
        P("dp", "seq", None),
        P("dp", "seq", None),
        P("seq", None),
        P("seq", None),
        P(),
        P(),
        P(),
    )
    return jax.shard_map(local, mesh=mesh, in_specs=in_specs, out_specs=out_specs, check_vma=False)
```

```python
import functools

import jax
import jax.numpy as jnp
from jax import lax
from jax.experimental import pallas as pl
from jax.experimental.pallas import tpu as pltpu
from jax.sharding import PartitionSpec as P

EPS = 1e-05
GROUPS = 4
PLANE = 8
HEADS = 3
HD = 64
F32 = jnp.float32
BF16 = jnp.bfloat16


def layer_norm(values, gain):
    center = values - jnp.mean(values, axis=-1, keepdims=True)
    spread = jnp.mean(center * center, axis=-1, keepdims=True)
    inverse = lax.rsqrt(spread + EPS)
    normed = center * inverse
    return (normed * gain, normed, inverse)


def norm_back(grad, normed, inverse, gain):
    scaled = grad * gain
    inner = (
        scaled
        - jnp.mean(scaled, axis=-1, keepdims=True)
        - normed * jnp.mean(scaled * normed, axis=-1, keepdims=True)
    )
    return (inverse * inner, jnp.sum(grad * normed, axis=0))


def dot(a, b, ca, cb):
    return lax.dot_general(a, b, (((ca,), (cb,)), ((), ())), preferred_element_type=F32)


class Place:
    def __init__(self):
        seq = lax.axis_index("seq")
        y, z, x = seq // 8, (seq // 4) % 2, seq % 4
        right, left, far, other = (x + 1) % 4, (x + 3) % 4, (x + 2) % 4, 1 - z
        self.y, self.yp, self.ym, self.yf = y, (y + 1) % 4, (y + 3) % 4, (y + 2) % 4
        self.me = z * 4 + x
        self.xp, self.xm, self.xf = z * 4 + right, z * 4 + left, z * 4 + far
        self.zo = other * 4 + x
        self.zxp, self.zxm, self.zxf = other * 4 + right, other * 4 + left, other * 4 + far

        self.seq, self.dp = seq, lax.axis_index("dp")
        self.core, self.hi = self.dp % 2, self.dp // 2

    def plane(self, p):
        return {"seq": self.y * 8 + p}

    def holder(self, y, dp):
        return {"seq": y * 8 + self.me, "dp": dp}

    def greet(self):
        near = [{"seq": (self.seq + i) % 32} for i in range(1, 32)]
        near += [self.holder(self.y, (self.dp + j) % 8) for j in range(1, 8)]
        near += [
            self.holder((self.y + i) % 4, ((self.hi + j) % 4) * 2 + self.core)
            for i in range(1, 4)
            for j in range(1, 4)
        ]
        for device in near:
            pl.semaphore_signal(pltpu.get_barrier_semaphore(), inc=1, device_id=device)
        return len(near)

    def column(self, y):
        return {"seq": y * 8 + self.me}


class Wire:
    def __init__(self, sems):
        self.sems, self.sent = sems, {}

    def go(self, k, src, dst, device):
        copy = pltpu.make_async_remote_copy(
            src_ref=src,
            dst_ref=dst,
            send_sem=self.sems.at[0, k],
            recv_sem=self.sems.at[1, k],
            device_id=device,
        )
        copy.start()
        self.sent[k] = copy

    def got(self, *ks):
        for k in ks:
            self.sent[k].wait_recv()

    def done(self):
        for copy in self.sent.values():
            copy.wait_send()


def wire_sems(count):
    return pltpu.SemaphoreType.DMA((2, count))


class ColumnGather(Wire):
    def __init__(self, sems, place, buf):
        super().__init__(sems)
        self.at, self.buf = place, buf
        self.half = buf.shape[1] // 2

    def begin(self):
        t, own = self.at, self.buf.at[self.at.y]
        self.go(0, own, own, t.column(t.yp))
        self.go(1, own, own, t.column(t.ym))

    def relay(self):
        t, h = self.at, self.half
        self.got(0)
        first = self.buf.at[t.ym, pl.ds(0, h)]
        self.go(2, first, first, t.column(t.yp))
        self.got(1)
        second = self.buf.at[t.yp, pl.ds(h, h)]
        self.go(3, second, second, t.column(t.ym))

    def finish(self):
        self.got(2, 3)


class ColumnReduce(Wire):
    def __init__(self, sems, place, part, relays, lands):
        super().__init__(sems)
        self.at, self.part, self.relays, self.lands = place, part, relays, lands
        self.half = part.shape[1] // 2

    def far(self):
        t, h = self.at, self.half
        self.go(0, self.part.at[t.yf, pl.ds(0, h)], self.relays.at[0], t.column(t.ym))
        self.go(1, self.part.at[t.yf, pl.ds(h, h)], self.relays.at[1], t.column(t.yp))

    def near(self):
        t, h = self.at, self.half
        low, high = pl.ds(0, h), pl.ds(h, h)
        self.go(2, self.part.at[t.ym, high], self.lands.at[0, high], t.column(t.ym))
        self.go(3, self.part.at[t.yp, low], self.lands.at[1, low], t.column(t.yp))

    def relay(self):
        t, h = self.at, self.half
        low, high = pl.ds(0, h), pl.ds(h, h)
        self.got(0)
        self.part[t.ym, low] = (
            self.part[t.ym, low].astype(F32) + self.relays[0].astype(F32)
        ).astype(BF16)
        self.go(4, self.part.at[t.ym, low], self.lands.at[0, low], t.column(t.ym))
        self.got(1)
        self.part[t.yp, high] = (
            self.part[t.yp, high].astype(F32) + self.relays[1].astype(F32)
        ).astype(BF16)
        self.go(5, self.part.at[t.yp, high], self.lands.at[1, high], t.column(t.yp))

    def finish(self):
        self.got(2, 3, 4, 5)
        return (
            self.part[self.at.y].astype(F32)
            + self.lands[0].astype(F32)
            + self.lands[1].astype(F32)
        )


class PlaneGather(Wire):
    def __init__(self, sems, place, full, half):
        super().__init__(sems)
        self.at, self.full, self.half = place, full, half

    def begin(self):
        t, own = self.at, self.full(self.at.me)
        self.go(0, own, own, t.plane(t.xp))
        self.go(1, own, own, t.plane(t.xm))
        self.go(2, own, own, t.plane(t.zo))

    def relay(self):
        t = self.at
        self.got(0)
        first = self.half(t.xm, 0)
        self.go(3, first, first, t.plane(t.xp))
        self.got(1)
        second = self.half(t.xp, 1)
        self.go(4, second, second, t.plane(t.xm))
        self.got(2)
        other = self.full(t.zo)
        self.go(5, other, other, t.plane(t.xp))
        self.go(6, other, other, t.plane(t.xm))

    def cross(self):
        t = self.at
        for k in (0, 1):
            self.got(3 + k)
            part = self.half(t.xf, k)
            self.go(7 + k, part, part, t.plane(t.zo))

    def finish(self):
        self.got(5, 6, 7, 8)


class PlaneReduce(Wire):
    def __init__(self, sems, place, full, half, land, land_half, half_land):
        super().__init__(sems)
        self.at, self.full, self.half = place, full, half
        self.land, self.land_half, self.half_land = land, land_half, half_land

    def add(self, ref, *more):
        total = ref[...].astype(F32)
        for other in more:
            total = total + other[...].astype(F32)
        ref[...] = total.astype(BF16)

    def far(self):
        t = self.at
        self.go(0, self.half(t.zxf, 0), self.land_half(0, 0), t.plane(t.zo))
        self.go(8, self.half(t.zxf, 1), self.land_half(0, 1), t.plane(t.zo))

    def left(self):
        self.go(1, self.full(self.at.zxm), self.land(1), self.at.plane(self.at.xm))

    def right(self):
        self.go(2, self.full(self.at.zxp), self.land(2), self.at.plane(self.at.xp))

    def opposite(self, i):
        t = self.at
        self.got((0, 8)[i])
        self.add(self.half(t.xf, i), self.land_half(0, i))
        self.go(3 + i, self.half(t.xf, i), self.half_land(i), t.plane((t.xm, t.xp)[i]))

    def early(self):
        t = self.at
        self.go(6, self.half(t.xm, 1), self.land_half(4, 1), t.plane(t.xm))
        self.go(7, self.half(t.xp, 0), self.land_half(5, 0), t.plane(t.xp))

    def across(self):
        t = self.at
        self.got(1, 2)
        self.add(self.full(t.zo), self.land(1), self.land(2))
        self.go(5, self.full(t.zo), self.land(3), t.plane(t.zo))

    def near(self):
        t = self.at
        self.got(3)
        self.add(self.half(t.xm, 0), self.half_land(0))
        self.go(9, self.half(t.xm, 0), self.land_half(4, 0), t.plane(t.xm))
        self.got(4)
        self.add(self.half(t.xp, 1), self.half_land(1))
        self.go(10, self.half(t.xp, 1), self.land_half(5, 1), t.plane(t.xp))

    def finish(self):
        self.got(5, 6, 7, 9, 10)
        total = self.full(self.at.me)[...].astype(F32)
        for k in (3, 4, 5):
            total = total + self.land(k)[...].astype(F32)
        return total


def pick(i, *values):
    out = values[-1]
    for k in range(len(values) - 2, -1, -1):
        out = jnp.where(i == k, values[k], out)
    return out


def local_copies(pairs, sems):
    copies = [
        pltpu.make_async_copy(src, dst, sems.at[i]) for i, (src, dst) in enumerate(pairs)
    ]
    for copy in copies:
        copy.start()
    return copies


QB = 128


def forward_block(kv, c, h, cols, qpad, top, total, acc):
    both = kv[c, :, h * 128 : (h + 1) * 128]
    scores = dot(both, qpad[h, cols, :], 1, 1)
    old = top[h, :, cols]
    new = jnp.maximum(old, jnp.max(scores, axis=0, keepdims=True))
    shrink = jnp.exp(old - new)
    expo = jnp.exp(scores - new)
    top[h, :, cols] = new
    total[h, :, cols] = total[h, :, cols] * shrink + jnp.sum(expo, axis=0, keepdims=True)
    acc[h, :, cols] = acc[h, :, cols] * shrink + dot(both, expo.astype(BF16), 0, 0)


def forward_chunk(kv, c, qpad, top, total, acc):
    for h in range(HEADS):
        for b in range(qpad.shape[1] // QB):
            forward_block(kv, c, h, slice(b * QB, (b + 1) * QB), qpad, top, total, acc)


def prob_chunk(kv, c, qpad, lse, probs):
    for h in range(HEADS):
        scores = dot(kv[c, :, h * 128 : (h + 1) * 128], qpad[h], 1, 1)
        probs[c, h] = jnp.exp(scores - lse[h]).astype(BF16)


def backward_chunk(kv, c, qpad, dopad, probs, delta, dqt, out):
    for h in range(HEADS):
        lanes = slice(h * 128, (h + 1) * 128)
        both, query, grad = kv[c, :, lanes], qpad[h], dopad[h]
        slopes = dot(both, grad, 1, 1)
        prob = probs[c, h]
        score_grads = (prob.astype(F32) * (slopes - delta[h])).astype(BF16)
        out[c, :, lanes] = (
            dot(prob, grad, 1, 0) + dot(score_grads, query, 1, 0)
        ).astype(BF16)
        dqt[h] += dot(both, score_grads, 0, 0)


HALO = 16
LANES = 128


def shifts(wide, length, taps):
    for low in range(8):
        moved = wide if low == 0 else pltpu.roll(wide, wide.shape[0] - low, 0)
        for offset in range(low, taps + 1, 8):
            if offset > 0:
                yield offset, moved[offset - low : offset - low + length]


class Edge(Wire):
    def __init__(self, sems, place, wide):
        super().__init__(sems)
        t, rows = place, wide.shape[0]
        self.first, self.last = t.seq == 0, t.seq == 31
        nothing = jnp.zeros((HALO, wide.shape[1]), BF16)

        @pl.when(self.first)
        def _():
            wide[0:HALO] = nothing

        @pl.when(self.last)
        def _():
            wide[rows - HALO :] = nothing

        self.up = pltpu.make_async_remote_copy(
            src_ref=wide.at[pl.ds(rows - 2 * HALO, HALO)],
            dst_ref=wide.at[pl.ds(0, HALO)],
            send_sem=sems.at[0, 0],
            recv_sem=sems.at[1, 0],
            device_id={"seq": jnp.minimum(t.seq + 1, 31)},
        )
        self.down = pltpu.make_async_remote_copy(
            src_ref=wide.at[pl.ds(HALO, HALO)],
            dst_ref=wide.at[pl.ds(rows - HALO, HALO)],
            send_sem=sems.at[0, 1],
            recv_sem=sems.at[1, 1],
            device_id={"seq": jnp.maximum(t.seq - 1, 0)},
        )

    def begin(self):
        @pl.when(jnp.logical_not(self.last))
        def _():
            self.up.start()

        @pl.when(jnp.logical_not(self.first))
        def _():
            self.down.start()

    def finish(self):
        @pl.when(jnp.logical_not(self.last))
        def _():
            self.up.wait_send()
            self.down.wait_recv()

        @pl.when(jnp.logical_not(self.first))
        def _():
            self.down.wait_send()
            self.up.wait_recv()


def whole_kernel(names, *refs):
    r = dict(zip(names, refs))
    (
        frames,
        w_qkv,
        w_out,
        gains_in,
        conv_kernel,
        conv_bias,
        out_grad,
        block_out,
        grad_input,
        grad_qkv,
        grad_out,
        kernel_sum,
        bias_sum,
        norms_sum,
        w_parts,
        hid,
        wq,
        wo,
        wo32,
        wo16,
        kv,
        qpad,
        lse,
        total,
        acc,
        att,
        probs,
        part,
        relays,
        lands,
        mixed_keep,
        normed_keep,
        first_keep,
        conv_wide,
        grad_wide,
        conv_back,
        mix,
        dopad,
        delta,
        dqt,
        dkv,
        kv_land,
        kv_half,
        proj,
        part2,
        relays2,
        lands2,
        w_part,
        w_core,
        w_land,
        w_half,
        w_hi,
        w_done,
        w_fin,
        o_part,
        o_core,
        o_land,
        o_half,
        o_hi,
        o_done,
        o_fin,
        s_send,
        s_seq,
        s_mine,
        s_dp,
        s_done,
        s_fin,
        spread_sems,
        swap_sems,
        hid_sems,
        wq_sems,
        wo_sems,
        gather_sems,
        sum_sems,
        conv_sems,
        grad_sems,
        mix_sems,
        kv_sems,
        red_sems,
        core_sems,
        w_sems,
        o_sems,
        hi_sems,
        o_hi_sems,
        cross_sems,
        w_fin_send,
        w_fin_recv,
        o_fin_send,
        o_fin_recv,
        g_mine,
        g_y,
        g_plane_mine,
        g_plane,
        g_dp_mine,
        g_dp,
        g_sems,
        s_sems,
        s_dp_sems,
        s_fin_sems,
    ) = (r[n] for n in names)
    t = Place()
    greeted = t.greet()
    rows, model = frames.shape
    many = GROUPS * rows
    width = HEADS * HD
    shard = w_qkv.shape[0]
    gain1, gain2 = gains_in[0:1, :], gains_in[1:2, :]

    for g in range(GROUPS):
        columns = [w_qkv[:, g * width : (g + 1) * width]]
        for h in range(HEADS):
            for kind in (1, 2):
                start = (kind * GROUPS + g) * width + h * HD
                columns.append(w_qkv[:, start : start + HD])
        w_parts[g] = jnp.concatenate(columns, axis=1)
    inputs = frames[...].astype(F32)
    shifted, normed, inverse1 = layer_norm(inputs, gain1)
    first_keep[...] = normed
    hid[t.y] = shifted.astype(BF16)
    pl.semaphore_wait(pltpu.get_barrier_semaphore(), greeted)
    hid_net = ColumnGather(hid_sems, t, hid)
    hid_net.begin()
    holds = t.y // 2 == t.core
    spread_copies = []
    for k in range(1, GROUPS):
        y = (t.y + k) % GROUPS
        copy = pltpu.make_async_remote_copy(
            src_ref=w_parts.at[y],
            dst_ref=wq.at[t.y, t.me],
            send_sem=spread_sems.at[0, k - 1],
            recv_sem=spread_sems.at[1, k - 1],
            device_id=t.column(y),
        )
        spread_copies.append((copy, ((t.y + GROUPS - k) % GROUPS) // 2 == t.core))

    @pl.when(holds)
    def _():
        for copy, _ in spread_copies:
            copy.start()
        wq[t.y, t.me] = w_parts[t.y]

    share = width // PLANE
    wide = model // 2
    for c in range(2):

        @pl.when(t.core == c)
        def _(c=c):
            wo[c, t.me] = w_out[:, c * wide : (c + 1) * wide]


    for copy, comes in spread_copies:
        pl.when(comes)(copy.wait_recv)
    base = 2 * t.core
    wq_net = PlaneGather(
        wq_sems, t, lambda p: wq.at[pl.ds(base, 2), p], lambda p, i: wq.at[base + i, p]
    )
    swap = Wire(swap_sems)
    buddy = {"dp": t.hi * 2 + 1 - t.core}

    def trade(*ps):
        for p in ps:
            half = wq.at[pl.ds(base, 2), p]
            swap.go(len(swap.sent), half, half, buddy)
    wo_net = PlaneGather(
        wo_sems,
        t,
        lambda p: wo.at[t.core, p],
        lambda p, i: wo.at[t.core, p, :, pl.ds(i * (wide // 2), wide // 2)],
    )
    wq_net.begin()
    trade(t.me)
    wq_net.relay()
    trade(t.xm, t.xp, t.zo)
    hid_net.relay()
    wq_net.cross()
    trade(t.xf)
    wo_net.begin()
    wq_net.finish()
    trade(t.zxm, t.zxp, t.zxf)
    hid_net.finish()
    swap.got(*range(PLANE))

    hidden = hid[...].reshape(many, model)
    weights = wq[...].reshape(model, 3 * width)
    projected = dot(hidden, weights, 1, 0).astype(BF16)
    kv[t.me] = projected[:, width:]
    kv_net = PlaneGather(
        gather_sems,
        t,
        lambda p: kv.at[p],
        lambda p, i: kv.at[p, pl.ds(i * (many // 2), many // 2)],
    )
    kv_net.begin()
    zeros = jnp.zeros((many, HD), BF16)
    for h in range(HEADS):
        qpad[h] = jnp.concatenate(
            [projected[:, h * HD : (h + 1) * HD] * BF16(HD**-0.5), zeros], axis=1
        )
    lse[...] = jnp.full_like(lse, -jnp.inf)
    total[...] = jnp.zeros_like(total)
    acc[...] = jnp.zeros_like(acc)

    def attend(*chunks):
        if len(chunks) == 1:
            forward_chunk(kv, chunks[0], qpad, lse, total, acc)
            return

        def step(i, carry):
            forward_chunk(kv, pick(i, *chunks), qpad, lse, total, acc)
            return carry

        lax.fori_loop(0, len(chunks), step, 0)

    attend(t.me)
    kv_net.relay()
    wo_net.relay()
    attend(t.xm, t.xp, t.zo)
    kv_net.cross()
    wo_net.cross()
    attend(t.xf)
    wo_net.finish()
    swap.go(PLANE, wo.at[t.core], wo.at[t.core], buddy)
    swap.got(PLANE)
    for p in range(PLANE):
        for c in range(2):
            wo32[p * share : (p + 1) * share, c * wide : (c + 1) * wide] = wo[c, p].astype(F32)
    wo16[...] = wo32[...].astype(BF16)
    kv_net.got(5, 6)
    kv_net.got(7, 8)

    def last(y):
        cols = pl.ds(pl.multiple_of(y * rows, rows), rows)

        for c in (t.zxm, t.zxp, t.zxf):
            for h in range(HEADS):
                forward_block(kv, c, h, cols, qpad, lse, total, acc)
        for h in range(HEADS):
            att[h * HD : (h + 1) * HD, cols] = (
                acc[h, HD : 2 * HD, cols] / total[h, :, cols]
            ).astype(BF16)
            lse[h, :, cols] = lse[h, :, cols] + jnp.log(total[h, :, cols])
        part[y] = dot(att[:, cols], wo16[...], 0, 0).astype(BF16)

    sum_net = ColumnReduce(sum_sems, t, part, relays, lands)
    last(t.yf)
    sum_net.far()
    last(t.ym)
    last(t.yp)
    sum_net.near()
    last(t.y)
    sum_net.relay()

    def foresee(*chunks):
        def step(i, carry):
            prob_chunk(kv, pick(i, *chunks), qpad, lse, probs)
            return carry

        lax.fori_loop(0, len(chunks), step, 0)

    mixed = (frames[...].astype(F32) + sum_net.finish()).astype(BF16)

    mixed32 = mixed.astype(F32)
    mixed_keep[...] = mixed32
    shifted, normed, inverse = layer_norm(mixed32, gain2)
    inside = slice(HALO, HALO + rows)
    conv_wide[inside] = shifted.astype(BF16)
    conv_edge = Edge(conv_sems, t, conv_wide)
    conv_edge.begin()
    normed_keep[...] = normed
    foresee(t.zxp)
    conv_edge.finish()
    taps = conv_kernel.shape[0]

    def lanes_of(b):
        return pl.ds(pl.multiple_of(b * LANES, LANES), LANES)

    def convolve(b, carry):
        lanes = lanes_of(b)
        pre = jnp.zeros((rows, LANES), F32) + conv_bias[lanes][None]
        for offset, moved in shifts(conv_wide[:, lanes].astype(F32), rows, taps):
            pre = pre + moved * conv_kernel[offset - 1 : offset, lanes]
        sigma = 1.0 / (1.0 + jnp.exp(-pre))
        block_out[:, lanes] = (mixed_keep[:, lanes] + pre * sigma).astype(BF16)
        grad_wide[inside, lanes] = (
            out_grad[:, lanes].astype(F32) * sigma * (1.0 + pre * (1.0 - sigma))
        ).astype(BF16)
        return carry

    blocks = model // LANES
    lax.fori_loop(0, blocks, convolve, 0)
    grad_edge = Edge(grad_sems, t, grad_wide)
    grad_edge.begin()
    foresee(t.xf)
    grad_edge.finish()

    def convolve_back(b, carry):
        lanes = lanes_of(b)
        grad = jnp.zeros((rows, LANES), F32)
        for offset, moved in shifts(grad_wide[:, lanes].astype(F32), rows, taps):
            grad = grad + moved * conv_kernel[taps - offset : taps - offset + 1, lanes]
        conv_back[:, lanes] = grad
        return carry

    lax.fori_loop(0, blocks, convolve_back, 0)
    norm_grad, gain2_grad = norm_back(conv_back[...], normed_keep[...], inverse, gain2)
    gain2_grad = gain2_grad[None]
    mix[t.y] = (out_grad[...].astype(F32) + norm_grad).astype(BF16)
    mix_net = ColumnGather(mix_sems, t, mix)
    mix_net.begin()

    def kernel_grads(b, carry):
        lanes = lanes_of(b)
        grad = grad_wide[inside, lanes].astype(F32)
        for offset, moved in shifts(conv_wide[:, lanes].astype(F32), rows, taps):
            s_send[offset - 1, :, lanes] = jnp.sum(grad * moved, axis=0, keepdims=True)
        s_send[taps, :, lanes] = jnp.sum(grad, axis=0, keepdims=True)
        return carry

    lax.fori_loop(0, blocks, kernel_grads, 0)
    foresee(t.zo, t.xm, t.xp)
    mix_net.relay()
    foresee(t.zxf, t.zxm, t.me)
    mix_net.finish()

    mixed = mix[...].reshape(many, model)
    grads = dot(mixed, wo16[...], 1, 1).astype(BF16)
    grads_turned = dot(wo16[...], mixed, 1, 1).astype(BF16).astype(F32)
    for h in range(HEADS):
        lanes = slice(h * HD, (h + 1) * HD)
        mine = grads[:, lanes]
        dopad[h] = jnp.concatenate([zeros, mine], axis=1)
        delta[h] = jnp.sum(
            att[lanes, :].astype(F32) * grads_turned[lanes, :], axis=0, keepdims=True
        )
    dqt[...] = jnp.zeros_like(dqt)

    def backward(*chunks):
        def step(i, carry):
            backward_chunk(kv, pick(i, *chunks), qpad, dopad, probs, delta, dqt, dkv)
            return carry

        if len(chunks) == 1:
            step(0, 0)
        else:
            lax.fori_loop(0, len(chunks), step, 0)

    half = many // 2
    net = PlaneReduce(
        kv_sems,
        t,
        lambda p: dkv.at[p],
        lambda p, i: dkv.at[p, pl.ds(i * half, half)],
        lambda k: kv_land.at[k],
        lambda k, i: kv_land.at[k, pl.ds(i * half, half)],
        lambda k: kv_half.at[k],
    )
    order = (t.zxf, t.zxm, t.zxp, t.xf, t.zo, t.xm, t.xp, t.me)
    backward(t.zxm)
    net.left()
    backward(t.zxp)
    net.right()
    backward(t.zxf)
    net.far()
    out_terms = dot(att[...], mixed, 1, 0)
    quarter = o_part.shape[2]
    for c in range(2):
        for p in range(PLANE):
            for i in range(quarter):
                piece = o_part.at[c, p, i]
                if i * 8 < share:
                    start = p * share + i * 8
                    piece[...] = out_terms[
                        start : start + 8, c * wide : (c + 1) * wide
                    ].astype(BF16)
                else:
                    piece[...] = jnp.zeros(piece.shape, BF16)
    pair = Wire(core_sems)
    pair.go(16, o_part.at[1 - t.core], o_core, buddy)
    o_mine = o_part.at[t.core]
    o_net = PlaneReduce(
        o_sems,
        t,
        lambda p: o_mine.at[p],
        lambda p, i: o_mine.at[p, pl.ds(2 * i, 2)],
        lambda k: o_land.at[k],
        lambda k, i: o_land.at[k, pl.ds(2 * i, 2)],
        lambda k: o_half.at[k],
    )
    count = s_send.shape[0]
    for r in range(count):
        if r < model // LANES:
            s_send[r, :, model:] = gain2_grad[:, r * LANES : (r + 1) * LANES]
        else:
            s_send[r, :, model:] = jnp.zeros((1, LANES), F32)
    s_net = Wire(s_sems)
    s_seq[t.seq] = s_send[t.seq]
    for k in range(1, count):
        r = (t.seq + k) % count
        s_net.go(k - 1, s_send.at[r], s_seq.at[t.seq], {"seq": r})
    backward(t.xf)
    pair.got(16)
    o_net.add(o_mine, o_core)
    o_net.far()
    o_net.left()
    o_net.right()
    backward(t.xm)
    net.opposite(0)
    backward(t.xp)
    net.early()
    net.opposite(1)
    s_net.got(*range(count - 1))
    s_mine[...] = jnp.sum(s_seq[...], axis=0)
    s_dp[t.dp] = s_mine[...]
    s_dp_net = Wire(s_dp_sems)
    for k in range(1, 8):
        s_dp_net.go(k - 1, s_mine, s_dp.at[t.dp], {"dp": (t.dp + k) % 8})

    o_net.early()
    backward(t.zo)
    net.across()
    net.near()
    o_net.opposite(0)
    o_net.opposite(1)
    o_net.across()
    backward(t.me)
    o_net.near()
    s_dp_net.got(*range(7))
    summed = s_dp[0]
    for d in range(1, 8):
        summed = summed + s_dp[d]
    s_done[...] = summed
    s_fin[t.seq] = summed
    s_fin_net = Wire(s_fin_sems)
    for k in range(1, count):
        s_fin_net.go(k - 1, s_done, s_fin.at[t.seq], {"seq": (t.seq + k) % count})

    for h in range(HEADS):
        proj[:, h * HD : (h + 1) * HD] = (dqt[h, 0:HD, :] * HD**-0.5).T.astype(BF16)

    proj[:, width:] = net.finish().astype(BF16)

    weights = wq[...].reshape(model, 3 * width)

    def product(y):
        here = proj[pl.ds(pl.multiple_of(y * rows, rows), rows), :]
        part2[y] = dot(here, weights, 1, 1).astype(BF16)

    red = ColumnReduce(red_sems, t, part2, relays2, lands2)
    product(t.yf)
    red.far()
    half_rows = w_part.shape[3]
    hidden = hid[...].reshape(many, model)
    w_terms = dot(hidden, proj[...], 0, 0).reshape(GROUPS, PLANE, 2, half_rows, 3 * width)
    for c in range(2):
        w_part[c] = w_terms[:, :, c].astype(BF16)
    for k, p in enumerate(order):
        pair.go(8 + k, w_part.at[1 - t.core, :, p], w_core.at[:, p], buddy)
    product(t.ym)
    product(t.yp)
    red.near()
    w_mine = w_part.at[t.core]
    w_net = PlaneReduce(
        w_sems,
        t,
        lambda p: w_mine.at[:, p],
        lambda p, i: w_mine.at[pl.ds(2 * i, 2), p],
        lambda k: w_land.at[k],
        lambda k, i: w_land.at[k, pl.ds(2 * i, 2)],
        lambda k: w_half.at[k],
    )

    def join(first, last):
        for k in range(first, last):
            p = order[k]
            pair.got(8 + k)
            w_net.add(w_mine.at[:, p], w_core.at[:, p])

    join(0, 1)
    w_net.far()
    join(1, 2)
    w_net.left()
    join(2, 3)
    w_net.right()
    product(t.y)
    red.relay()
    join(3, 4)
    w_net.opposite(0)
    w_net.opposite(1)
    join(4, 7)
    w_net.early()
    o_mine[t.me] = o_net.finish().astype(BF16)
    o_hi_net = Wire(o_hi_sems)
    for k in range(1, 4):
        j = (t.hi + k) % 4
        o_hi_net.go(k - 1, o_mine.at[t.me, j], o_hi.at[k - 1], {"dp": j * 2 + t.core})
    join(7, 8)
    w_net.across()
    w_net.near()

    s_fin_net.got(*range(count - 1))
    for r in range(count):
        row = s_fin[r]
        if r < taps:
            kernel_sum[r : r + 1, :] = row[:, :model]
        else:
            bias_sum[...] = row[:, :model]
        if r < model // LANES:
            norms_sum[1:2, r * LANES : (r + 1) * LANES] = row[:, model:]
    grad_hidden = red.finish()
    norm_grad, gain_sum = norm_back(grad_hidden, first_keep[...], inverse1, gain1)
    grad_input[...] = (mix[t.y].astype(F32) + norm_grad).astype(BF16)
    g_mine[...] = gain_sum[None]
    g_y[t.y] = g_mine[...]
    g_net = Wire(g_sems)
    for k, y in enumerate((t.yp, t.ym, t.yf)):
        g_net.go(k, g_mine, g_y.at[t.y], t.column(y))

    o_hi_net.got(0, 1, 2)
    o_out_block = o_mine[t.me, t.hi].astype(F32)
    for k in range(3):
        o_out_block = o_out_block + o_hi[k].astype(F32)
    o_done[...] = o_out_block.astype(BF16)
    finals = []

    def deliver(src, dst, send, recv, y):
        for k in range(1, 4):
            copy = pltpu.make_async_remote_copy(
                src_ref=src,
                dst_ref=dst,
                send_sem=send.at[k],
                recv_sem=recv,
                device_id=t.holder(y, ((t.hi + k) % 4) * 2 + t.core),
            )
            copy.start()
            finals.append(copy)

    deliver(o_done, o_fin.at[t.hi, t.core], o_fin_send, o_fin_recv.at[t.hi, t.core], t.y)
    o_own = pltpu.make_async_copy(
        o_done, o_fin.at[t.hi, t.core], o_fin_recv.at[t.hi, t.core]
    )
    o_own.start()
    w_mine[:, t.me] = w_net.finish().astype(BF16)
    hi_net = Wire(hi_sems)
    for k in range(1, 4):
        j = (t.hi + k) % 4
        there = {"dp": j * 2 + t.core}
        hi_net.go(k - 1, w_mine.at[j, t.me], w_hi.at[k - 1], there)

    g_net.got(0, 1, 2)
    g_plane_mine[...] = ((g_y[0] + g_y[1]) + g_y[2]) + g_y[3]
    g_plane[t.me] = g_plane_mine[...]
    for k in range(1, PLANE):
        g_net.go(2 + k, g_plane_mine, g_plane.at[t.me], t.plane((t.me + k) % PLANE))

    hi_net.got(*range(3))
    w_out_block = w_mine[t.hi, t.me].astype(F32)
    for k in range(3):
        w_out_block = w_out_block + w_hi[k].astype(F32)
    w_done[...] = w_out_block.astype(BF16)
    deliver(w_done, w_fin.at[t.y, t.core], w_fin_send, w_fin_recv.at[t.y, t.core], t.hi)
    w_own = pltpu.make_async_copy(w_done, w_fin.at[t.y, t.core], w_fin_recv.at[t.y, t.core])
    w_away = pltpu.make_async_remote_copy(
        src_ref=w_done,
        dst_ref=w_fin.at[t.y, t.core],
        send_sem=w_fin_send.at[0],
        recv_sem=w_fin_recv.at[t.y, t.core],
        device_id=t.holder(t.hi, t.dp),
    )

    @pl.when(t.hi == t.y)
    def _():
        w_own.start()

    @pl.when(t.hi != t.y)
    def _():
        w_away.start()

    g_net.got(*range(3, 10))
    along = g_plane[0]
    for p in range(1, PLANE):
        along = along + g_plane[p]
    g_dp_mine[...] = along
    g_dp[t.dp] = along
    for k in range(1, 8):
        g_net.go(9 + k, g_dp_mine, g_dp.at[t.dp], {"dp": (t.dp + k) % 8})

    cross = Wire(cross_sems)
    for i in range(4):
        pltpu.make_async_copy(o_done, o_fin.at[i, t.core], o_fin_recv.at[i, t.core]).wait()
        cross.go(i, o_fin.at[i, t.core], o_fin.at[i, t.core], buddy)
    for i in range(4):
        pltpu.make_async_copy(w_done, w_fin.at[i, t.core], w_fin_recv.at[i, t.core]).wait()
        cross.go(4 + i, w_fin.at[i, t.core], w_fin.at[i, t.core], buddy)
    cross.got(*range(8))
    pieces = [w_fin[y].astype(F32).reshape(2 * half_rows, 3 * width) for y in range(GROUPS)]
    columns = [piece[:, :width] for piece in pieces]
    for kind in range(2):
        for piece in pieces:
            for h in range(HEADS):
                start = width + (2 * h + kind) * HD
                columns.append(piece[:, start : start + HD])
    grad_qkv[...] = jnp.concatenate(columns, axis=1).astype(BF16)
    sides = [
        o_fin[0 : share // 8, c].astype(F32).reshape(share, wide) for c in range(2)
    ]
    grad_out[...] = jnp.concatenate(sides, axis=1).astype(BF16)
    g_net.got(*range(10, 17))
    along = g_dp[0]
    for d in range(1, 8):
        along = along + g_dp[d]
    norms_sum[0:1, :] = along
    for copy in finals:
        copy.wait_send()

    @pl.when(t.hi != t.y)
    def _():
        w_away.wait_send()

    @pl.when(holds)
    def _():
        for copy, _ in spread_copies:
            copy.wait_send()

    for wire in (swap, hid_net, wq_net, wo_net, kv_net, sum_net, mix_net, net, pair, o_net, red, w_net, hi_net, o_hi_net, cross, s_net, s_dp_net, s_fin_net, g_net):
        wire.done()


def bf16(*shape):
    return pltpu.VMEM(shape, BF16)


def f32(*shape):
    return pltpu.VMEM(shape, F32)


def dma(*shape):
    return pltpu.SemaphoreType.DMA(shape)


def whole(frames, w_qkv, w_out, gains, conv_kernel, conv_bias, out_grad):
    rows, model = frames.shape
    shard = w_qkv.shape[0]
    many = GROUPS * rows
    width = HEADS * HD
    half = shard // 2
    count = conv_kernel.shape[0] + 1
    like = jax.ShapeDtypeStruct
    ins = dict(
        frames=frames,
        w_qkv=w_qkv,
        w_out=w_out,
        gains_in=gains,
        conv_kernel=conv_kernel,
        conv_bias=conv_bias,
        out_grad=out_grad,
    )
    outs = dict(
        block_out=like((rows, model), BF16),
        grad_input=like((rows, model), BF16),
        grad_qkv=like(w_qkv.shape, BF16),
        grad_out=like(w_out.shape, BF16),
        kernel_sum=like((count - 1, model), F32),
        bias_sum=like((1, model), F32),
        norms_sum=like((2, model), F32),
    )
    scratch = dict(
        w_parts=bf16(GROUPS, shard, 3 * width),
        hid=bf16(GROUPS, rows, model),
        wq=bf16(GROUPS, PLANE, shard, 3 * width),
        wo=bf16(2, PLANE, width // PLANE, model // 2),
        wo32=f32(width, model),
        wo16=bf16(width, model),
        kv=bf16(PLANE, many, 2 * width),
        qpad=bf16(HEADS, many, 2 * HD),
        lse=f32(HEADS, 1, many),
        total=f32(HEADS, 1, many),
        acc=f32(HEADS, 2 * HD, many),
        att=bf16(width, many),
        probs=bf16(PLANE, HEADS, many, many),
        part=bf16(GROUPS, rows, model),
        relays=bf16(2, rows // 2, model),
        lands=bf16(2, rows, model),
        mixed_keep=f32(rows, model),
        normed_keep=f32(rows, model),
        first_keep=f32(rows, model),
        conv_wide=bf16(rows + 2 * HALO, model),
        grad_wide=bf16(rows + 2 * HALO, model),
        conv_back=f32(rows, model),
        mix=bf16(GROUPS, rows, model),
        dopad=bf16(HEADS, many, 2 * HD),
        delta=f32(HEADS, 1, many),
        dqt=f32(HEADS, 2 * HD, many),
        dkv=bf16(PLANE, many, 2 * width),
        kv_land=bf16(6, many, 2 * width),
        kv_half=bf16(2, many // 2, 2 * width),
        proj=bf16(many, 3 * width),
        part2=bf16(GROUPS, rows, model),
        relays2=bf16(2, rows // 2, model),
        lands2=bf16(2, rows, model),
        w_part=bf16(2, GROUPS, PLANE, half, 3 * width),
        w_core=bf16(GROUPS, PLANE, half, 3 * width),
        w_land=bf16(6, GROUPS, half, 3 * width),
        w_half=bf16(2, GROUPS // 2, half, 3 * width),
        w_hi=bf16(3, half, 3 * width),
        w_done=bf16(half, 3 * width),
        w_fin=bf16(GROUPS, 2, half, 3 * width),
        o_part=bf16(2, PLANE, 4, 8, model // 2),
        o_core=bf16(PLANE, 4, 8, model // 2),
        o_land=bf16(6, 4, 8, model // 2),
        o_half=bf16(2, 2, 8, model // 2),
        o_hi=bf16(3, 8, model // 2),
        o_done=bf16(8, model // 2),
        o_fin=bf16(4, 2, 8, model // 2),
        s_send=f32(count, 1, model + LANES),
        s_seq=f32(count, 1, model + LANES),
        s_mine=f32(1, model + LANES),
        s_dp=f32(8, 1, model + LANES),
        s_done=f32(1, model + LANES),
        s_fin=f32(count, 1, model + LANES),
        spread_sems=wire_sems(3),
        swap_sems=wire_sems(PLANE + 1),
        hid_sems=wire_sems(4),
        wq_sems=wire_sems(9),
        wo_sems=wire_sems(9),
        gather_sems=wire_sems(9),
        sum_sems=wire_sems(6),
        conv_sems=wire_sems(2),
        grad_sems=wire_sems(2),
        mix_sems=wire_sems(4),
        kv_sems=wire_sems(11),
        red_sems=wire_sems(6),
        core_sems=wire_sems(17),
        w_sems=wire_sems(11),
        o_sems=wire_sems(11),
        hi_sems=wire_sems(3),
        o_hi_sems=wire_sems(3),
        cross_sems=wire_sems(8),
        w_fin_send=dma(8),
        w_fin_recv=dma(4, 2),
        o_fin_send=dma(8),
        o_fin_recv=dma(4, 2),
        g_mine=f32(1, model),
        g_y=f32(GROUPS, 1, model),
        g_plane_mine=f32(1, model),
        g_plane=f32(PLANE, 1, model),
        g_dp_mine=f32(1, model),
        g_dp=f32(8, 1, model),
        g_sems=wire_sems(17),
        s_sems=wire_sems(count - 1),
        s_dp_sems=wire_sems(7),
        s_fin_sems=wire_sems(count - 1),
    )
    vmem = pl.BlockSpec(memory_space=pltpu.VMEM)
    names = [*ins, *outs, *scratch]
    return pl.pallas_call(
        functools.partial(whole_kernel, names),
        out_shape=list(outs.values()),
        in_specs=[vmem] * len(ins),
        out_specs=[vmem] * len(outs),
        scratch_shapes=list(scratch.values()),
        compiler_params=pltpu.CompilerParams(
            collective_id=0, has_side_effects=True, vmem_limit_bytes=62 * 2**20
        ),
        name="whole",
    )(*ins.values())


def hand_on_kernel(*refs):
    half = len(refs) // 2
    for src, dst in zip(refs[:half], refs[half:]):
        dst[...] = src[...].reshape(dst.shape)


def hand_on(*arrays):
    vmem = pl.BlockSpec(memory_space=pltpu.VMEM)
    return pl.pallas_call(
        hand_on_kernel,
        out_shape=[
            jax.ShapeDtypeStruct(a.shape[1:] if a.shape[0] == 1 else a.shape, a.dtype) for a in arrays
        ],
        in_specs=[vmem] * len(arrays),
        out_specs=[vmem] * len(arrays),
        name="hand_on",
    )(*arrays)


def local(frames, w_qkv, w_out, norm_gains, conv_kernel, conv_bias, out_grad):
    block_out, grad_input, grad_qkv, grad_out, kernel_sum, bias_sum, norms_sum = hand_on(
        *whole(
            frames[0], w_qkv, w_out, norm_gains, conv_kernel, conv_bias, out_grad[0]
        )
    )
    return (
        block_out[None],
        grad_input[None],
        grad_qkv,
        grad_out,
        norms_sum,
        kernel_sum,
        bias_sum,
    )


def solution(mesh):
    in_specs = (
        P("dp", "seq", None),
        P("seq", None),
        P("seq", None),
        P(),
        P(),
        P(),
        P("dp", "seq", None),
    )
    out_specs = (
        P("dp", "seq", None),
        P("dp", "seq", None),
        P("seq", None),
        P("seq", None),
        P(),
        P(),
        P(),
    )
    return jax.shard_map(local, mesh=mesh, in_specs=in_specs, out_specs=out_specs, check_vma=False)
```
